32 devices in a mesh: atom: 4 (over x, core), ka: 8 (over z, y).
Axes of the slice: x: 2, y: 2, z: 4, core: 2. Of those that a mesh axis runs over, the one named last changes fastest.
Arguments:
- positions: float32 [3, 65536], P(None, 'atom'), may hold values from 0 to 1
- features: bfloat16 [64, 65536], P(None, 'atom'), may hold values from -6 to 6
- species: int32 [65536], P('atom'), may hold values from 0 to 7
- miller: int32 [3, 4096], P(None, 'ka'), may hold values from -8 to 8
- species_table: float32 [64, 8], replicated, may hold values from -6 to 6
- filter_weight: float32 [64, 16], replicated, may hold values from -6 to 6
- norm_gain: float32 [64], replicated, may hold values from 0.25 to 1.75
- up_weight: bfloat16 [256, 64], replicated, may hold values from -0.75 to 0.75
- down_weight: bfloat16 [64, 256], replicated, may hold values from -0.375 to 0.375
Outputs:
- updated: bfloat16 [64, 65536], P(None, ('atom', 'ka'))
The draws below stay inside these ranges and needn't reach their ends.
All inputs are finite; a program needn't handle non-finite values.
Results may differ from the reference program's by a relative error of at most 0.006.
Values may be sent and summed in bfloat16 or wider, within the bound.
No kernel may reach another device: no remote copies, remote signals or barrier semaphores. Data moves between devices by JAX's collectives and lax.ppermute only.
A program may use at most 64 MiB of HBM per device.

```python
import math
import jax
import jax.numpy as jnp
from jax import lax

C = 64
K = 4096
NRBF = 16
HID = 256
NSPEC = 8
NATOMS = 65536


def plant(result, key, least, high):
    index_at = [jax.random.randint(jax.random.fold_in(key, axis), (), 0, length) for axis, length in enumerate(result.shape)]
    main_axis = result.shape.index(max(result.shape))
    beside = index_at[:main_axis] + [(index_at[main_axis] + 1) % result.shape[main_axis]] + index_at[main_axis + 1:]
    return result.at[tuple(index_at)].set(least).at[tuple(beside)].set(high)


def steps_of(stream_key, shape, pieces, least, high):
    loudness, own = 1.0, jax.random.fold_in(stream_key, 6)
    for position, blocks in pieces:
        draws = jnp.exp(jax.random.uniform(jax.random.fold_in(own, position), (blocks,), jnp.float32, least / len(pieces), high / len(pieces)))
        loudness = loudness * jnp.repeat(draws, shape[position] // blocks).reshape([-1 if axis == position else 1 for axis in range(len(shape))])
    return loudness


def scatter_about(key, shape, deviation, reach, shards=(), kind=jnp.bfloat16):
    entries = deviation * jax.random.normal(key, shape, jnp.float32)
    if shards:
        entries = entries * steps_of(key, shape, shards, -0.22, 0.18)
    return jnp.clip(entries, -reach, reach).astype(kind)


def setup_inputs(seed: int = 0) -> dict:
    splits = jax.random.split(jax.random.key(seed), 10)
    positions = jnp.clip(1.0 * jax.random.uniform(splits[0], (3, NATOMS), jnp.float32) ** steps_of(splits[0], (3, NATOMS), ((1, 4),), -0.2, 0.2), 0.0, 1.0)
    features = scatter_about(splits[1], (C, NATOMS), 1.0, 6.0, ((1, 4),))
    species = plant(jax.random.randint(splits[2], (NATOMS,), 0, NSPEC), jax.random.fold_in(splits[2], 1), 0, NSPEC - 1).astype(jnp.int32)
    miller = plant(jax.random.randint(splits[3], (3, K), -8, 9), jax.random.fold_in(splits[3], 1), -8, 8).astype(jnp.int32)
    species_table = scatter_about(splits[4], (C, NSPEC), 1.0, 6.0, (), jnp.float32)
    filter_weight = scatter_about(splits[5], (C, NRBF), 1.0, 6.0, (), jnp.float32)
    norm_gain = jnp.clip(1.0 + 0.15 * jax.random.normal(splits[6], (C,), jnp.float32), 0.25, 1.75)
    up_weight = scatter_about(splits[7], (HID, C), C ** -0.5, 0.75)
    down_weight = scatter_about(splits[8], (C, HID), HID ** -0.5, 0.375)
    return dict(positions=positions, features=features, species=species, miller=miller, species_table=species_table, filter_weight=filter_weight, norm_gain=norm_gain, up_weight=up_weight, down_weight=down_weight)


two_pi = 2.0 * math.pi
k_cutoff = 14.0
block_width = 128

def phases(coords, vectors):
    values = vectors.astype(jnp.float32)
    angles = two_pi * (coords[0][:, None] * values[0][None, :] + coords[1][:, None] * values[1][None, :] + coords[2][:, None] * values[2][None, :])
    return (jnp.cos(angles).astype(jnp.bfloat16), jnp.sin(angles).astype(jnp.bfloat16))

def radial_filter(vectors, filter_weight):
    values = vectors.astype(jnp.float32)
    magnitude = jnp.sqrt(values[0] * values[0] + values[1] * values[1] + values[2] * values[2])
    centers = jnp.arange(NRBF, dtype=jnp.float32) * (k_cutoff / (NRBF - 1))
    basis = jnp.exp(-jnp.square((magnitude[None, :] - centers[:, None]) / (k_cutoff / NRBF)))
    return jnp.dot(filter_weight, basis, precision=lax.Precision.HIGHEST, preferred_element_type=jnp.float32)

def project_back(filtered, cosines, sines):
    dims = (((1,), (1,)), ((), ()))
    first = lax.dot_general(filtered[0], cosines, dims, preferred_element_type=jnp.float32)
    return first + lax.dot_general(filtered[1], sines, dims, preferred_element_type=jnp.float32)

def reference(positions, features, species, miller, species_table, filter_weight, norm_gain, up_weight, down_weight):
    source = (features.astype(jnp.float32) + species_table[:, species]).astype(jnp.bfloat16)
    blocks = miller.reshape(3, K // block_width, block_width).transpose(1, 0, 2)
    scaling = 1.0 / math.sqrt(NATOMS * K)

    def factor_block(vectors):
        cosines, sines = phases(positions, vectors)
        real_part = jnp.dot(source, cosines, preferred_element_type=jnp.float32)
        imag_part = jnp.dot(source, sines, preferred_element_type=jnp.float32)
        radial = radial_filter(vectors, filter_weight)
        return (jnp.stack([real_part, imag_part]) * radial[None] * scaling).astype(jnp.bfloat16)
    filtered = lax.map(factor_block, blocks)

    def back_step(running, inputs):
        vectors, factor_part = inputs
        cosines, sines = phases(positions, vectors)
        return (running + project_back(factor_part, cosines, sines), None)
    message, _ = lax.scan(back_step, jnp.zeros((C, NATOMS), jnp.float32), (blocks, filtered))
    mean_sq = lax.optimization_barrier(jnp.mean(message * message, axis=0, keepdims=True))
    normed = (message * lax.rsqrt(mean_sq + 1e-06) * norm_gain[:, None]).astype(jnp.bfloat16)
    hidden = jax.nn.silu(jnp.dot(up_weight, normed, preferred_element_type=jnp.float32)).astype(jnp.bfloat16)
    update = jnp.dot(down_weight, hidden, preferred_element_type=jnp.float32)
    return (features.astype(jnp.float32) + update).astype(jnp.bfloat16)
```

```python
import functools
import math

import jax
import jax.numpy as jnp
import numpy as np
from jax import lax
from jax.experimental import pallas as pl
from jax.experimental.pallas import tpu as pltpu
from jax.sharding import PartitionSpec as P

K = 4096
NRBF = 16
NSPEC = 8
MAXM = 8
GROUP = 8
ROWS = 304
LANES = 128
PAYLOAD = 400
k_cutoff = 14.0
f32 = jnp.float32
bf16 = jnp.bfloat16


def fit(function, terms, odd):
    nodes = np.cos((np.arange(64) + 0.5) * np.pi / 64) * 0.5
    nodes = np.abs(nodes)
    target = function(2.0 * np.pi * nodes)
    if odd:
        target = target / nodes
    series = np.polynomial.chebyshev.Chebyshev.fit(nodes * nodes, target, terms - 1, domain=[0, 0.25])
    return [float(v) for v in series.convert(kind=np.polynomial.Polynomial).coef]


SIN = fit(np.sin, 7, True)
COS = fit(np.cos, 7, False)


def horner(coefs, x):
    total = coefs[-1] * x + coefs[-2]
    for value in coefs[-3::-1]:
        total = total * x + value
    return total


def harmonics(x, multiples):
    turns = x * multiples
    turns = turns - jnp.floor(turns + 0.5)
    square = turns * turns
    return horner(COS, square), turns * horner(SIN, square)


def iota(shape, axis):
    return lax.broadcasted_iota(jnp.int32, shape, axis)


def factor_kernel(ka_split, sub, pos, feat, species, table, basis_out, z_out, acc_out, local_out, a_scr):
    step = pl.program_id(0)
    me = lax.axis_index("ka")
    group = me // ka_split
    width = pos.shape[1]
    first = pl.multiple_of((group // 2) * 16, 16)
    odd = (group % 2) == 1
    own_table = table[pl.ds(pl.multiple_of(group * GROUP, GROUP), GROUP), :]
    multiples = (iota((8, sub), 0) + 1).astype(f32)
    tail = (iota((16, sub), 0) == 0).astype(f32).astype(bf16)

    @pl.when(step == 0)
    def _():
        acc_out[...] = jnp.zeros_like(acc_out)

    @pl.when(step == me)
    def _():
        local_out[...] = feat[...]

    for start in range(0, width, sub):
        part = pl.ds(start, sub)
        c0, s0 = harmonics(pos[0:1, part], multiples)
        c1, s1 = harmonics(pos[1:2, part], multiples)
        c2, s2 = harmonics(pos[2:3, part], multiples)
        z_out[0:8, part] = c2
        z_out[8:16, part] = s2
        block = 0
        for left, right in ((c0, c1), (s0, s1), (s0, c1), (c0, s1)):
            for m in range(0, MAXM, 2):
                both = jnp.concatenate([left[m : m + 1] * right, left[m + 1 : m + 2] * right], 0)
                basis_out[block : block + 16, part] = both.astype(bf16)
                block += 16
        basis_out[256:272, part] = jnp.concatenate([c0, s0], 0).astype(bf16)
        basis_out[272:288, part] = jnp.concatenate([c1, s1], 0).astype(bf16)
        basis_out[288:304, part] = tail
        kinds = species[0:1, part]
        embedded = jnp.zeros((GROUP, sub), f32)
        for s in range(NSPEC):
            embedded = jnp.where(kinds == s, own_table[:, s : s + 1], embedded)
        wide = feat[pl.ds(first, 16), part].astype(f32)
        own = jnp.where(odd, wide[8:16], wide[0:8])
        source = (own + embedded).astype(bf16).astype(f32)
        for row, wave in ((0, c2), (64, s2)):
            for m in range(0, MAXM, 2):
                both = jnp.concatenate([source * wave[m : m + 1], source * wave[m + 1 : m + 2]], 0)
                a_scr[row + 8 * m : row + 8 * m + 16, part] = both.astype(bf16)
        a_scr[128:144, part] = jnp.concatenate([source, jnp.zeros_like(source)], 0).astype(bf16)
    acc_out[...] += lax.dot_general(
        basis_out[...], a_scr[...], (((1,), (1,)), ((), ())), preferred_element_type=f32
    )


def pack_kernel(acc, *refs):
    millers, out = refs[:-1], refs[-1]
    out[0:ROWS, :] = acc[:, 0:LANES].astype(bf16)
    tail = jnp.concatenate([acc[:, 128:144], jnp.zeros((ROWS, 112), f32)], 1)
    tail = jnp.concatenate([tail, jnp.zeros((384 - ROWS, LANES), f32)], 0)
    flat = tail.T
    zero = jnp.zeros((GROUP, LANES), f32)
    pieces = [flat[0:8, 0:128], flat[0:8, 128:256], flat[0:8, 256:384], zero]
    out[304:336, :] = jnp.concatenate(pieces, 0).astype(bf16)
    counts = jnp.zeros((32, 256), f32)
    for ref in millers:
        m0, m1, m2 = ref[0:1, :], ref[1:2, :], ref[2:3, :]
        sign = jnp.where(17 * m0 + m1 < 0, -1, 1)
        m0, m1, m2 = m0 * sign, m1 * sign, m2 * sign
        inner = jnp.where(
            m1 > 0, 8 * m0 + m1 - 9, jnp.where(m1 < 0, 55 + 8 * m0 - m1, 127 + m0)
        )
        row = jnp.where(m0 > 0, inner, jnp.where(m1 > 0, 135 + m1, 144))
        column = jnp.where(row == 144, jnp.abs(m2), m2) + MAXM
        size = row.shape[1]
        row_hot = (iota((256, size), 0) == row).astype(f32).astype(bf16)
        column_hot = (iota((32, size), 0) == column).astype(f32).astype(bf16)
        counts = counts + lax.dot_general(
            column_hot, row_hot, (((1,), (1,)), ((), ())), preferred_element_type=f32
        )
    out[336:368, :] = counts[:, 0:128].astype(bf16)
    out[368:400, :] = counts[:, 128:256].astype(bf16)


def radial_sum(square, weight_of):
    magnitude = jnp.sqrt(square)
    total = None
    for b in range(NRBF):
        offset = (magnitude - b * (k_cutoff / (NRBF - 1))) * (NRBF / k_cutoff)
        term = weight_of(b) * jnp.exp(-(offset * offset))
        total = term if total is None else total + term
    return total


def filter_rows(payload, weights, group, scaling, gt_scr):
    total = payload[0].astype(f32)
    for a in range(1, payload.shape[0]):
        total = total + payload[a].astype(f32)
    counts = jnp.concatenate([total[336:368], total[368:400]], 1)
    lane = iota((32, LANES), 1)
    index = iota((32, LANES), 0) - MAXM
    height = (lane % 64) // 8 + 1
    plus = jnp.where(jnp.abs(index) == height, 1.0, 0.0)
    minus = jnp.where(index == height, 1.0, jnp.where(index == -height, -1.0, 0.0))
    minus = jnp.where(lane < 64, -minus, minus)
    spread = jnp.concatenate([plus, minus], 1).astype(f32)
    wide = lax.dot_general(
        counts.T, spread, (((1,), (0,)), ((), ())),
        precision=lax.Precision.HIGHEST, preferred_element_type=f32,
    )
    pick = (iota((64, LANES), 0) == group * GROUP + iota((64, LANES), 1) % 8).astype(f32)
    across = lax.dot_general(
        weights[...].T, pick, (((1,), (0,)), ((), ())),
        precision=lax.Precision.HIGHEST, preferred_element_type=f32,
    )
    lane = iota((88, LANES), 1)
    row = iota((88, LANES), 0)
    third = (lane % 64) // 8 + 1
    first = row // 8 + 1
    second = row % 8 + 1
    planar = jnp.where(
        row < 64,
        first * first + second * second,
        jnp.where(row < 80, second * second, 0),
    )
    radial = radial_sum((planar + third * third).astype(f32), lambda b: across[b : b + 1, :]) * scaling
    radial = jnp.concatenate([radial[0:64], radial], 0)
    w_sum = wide[0:152, 0:128] * radial
    w_dif = wide[0:152, 128:256] * radial
    cc, ss, sc, cs = total[0:64], total[64:128], total[128:192], total[192:256]
    zero = jnp.zeros((8, LANES), f32)
    v_cos = jnp.concatenate([cc - ss, cc + ss, total[256:264], total[272:280], total[288:296]], 0)
    v_sin = jnp.concatenate([sc + cs, sc - cs, total[264:272], total[280:288], zero], 0)
    g_cos = w_sum * v_cos + w_dif * pltpu.roll(v_sin, 64, 1)
    g_sin = w_sum * v_sin - w_dif * pltpu.roll(v_cos, 64, 1)
    cp, cm, sp, sm = g_cos[0:64], g_cos[64:128], g_sin[0:64], g_sin[64:128]
    rows = [cp + cm, cm - cp, sp + sm, sp - sm, g_cos[128:136], g_sin[128:136]]
    rows += [g_cos[136:144], g_sin[136:144], g_cos[144:152], jnp.zeros((88, LANES), f32)]
    full = jnp.concatenate(rows, 0)
    gt_scr[0:128, :] = full.T.astype(bf16)

    lane = iota((8, LANES), 1)
    cell = lane % 64
    cell = (cell // 8 + 1) * (cell // 8 + 1) + (cell % 8 + 1) * (cell % 8 + 1)
    edge = jnp.where(lane < 32, (lane % 8 + 1) * (lane % 8 + 1), 0)
    own = weights[pl.ds(pl.multiple_of(group * GROUP, GROUP), GROUP), :]
    flat = radial_sum(
        jnp.concatenate([cell, edge], 1).astype(f32), lambda b: own[:, b : b + 1]
    ) * scaling
    count0 = jnp.broadcast_to(counts[8:9, 0:128], (8, LANES))
    count1 = jnp.broadcast_to(counts[8:9, 128:256], (8, LANES))
    side = jnp.where(
        lane < 8, count1,
        jnp.where(lane < 24, pltpu.roll(count1, 8, 1), jnp.where(lane < 33, pltpu.roll(count1, 16, 1), 0.0)),
    )
    sigma = jnp.where(lane < 64, 1.0, -1.0).astype(f32)
    even, uneven, rest = total[304:312], total[312:320], total[320:328]

    def mix(value):
        return pltpu.roll(value, 64, 1) + value * sigma

    even = mix(mix(even) * flat[:, 0:128] * pltpu.roll(count0, 64, 1))
    uneven = mix(mix(uneven) * flat[:, 0:128] * count0)
    rest = rest * flat[:, 128:256] * side
    low = jnp.concatenate([even, uneven, rest], 1)
    gt_scr[128:144, :] = jnp.concatenate([low, jnp.zeros_like(low)], 0).astype(bf16)


def back_kernel(ka_split, scaling, sub, payload, weights, basis, z, out, gt_scr):
    @pl.when(pl.program_id(0) == 0)
    def _():
        filter_rows(payload, weights, lax.axis_index("ka") // ka_split, scaling, gt_scr)

    table = gt_scr[:, 0:ROWS]
    for start in range(0, basis.shape[1], sub):
        part = pl.ds(start, sub)
        product = jnp.dot(table, basis[:, part], preferred_element_type=f32)
        message = product[128:136]
        for m in range(16):
            message = message + z[m : m + 1, part] * product[8 * m : 8 * m + 8]
        out[0, :, part] = message.astype(bf16)


def update_kernel(sub, message, feat, gain, up, down, out):
    width = feat.shape[1]
    eye = iota((64, 64), 0) == iota((64, 64), 1)
    column = jnp.sum(jnp.where(eye, jnp.broadcast_to(gain[...], (64, 64)), 0.0), axis=1, keepdims=True)
    for start in range(0, width, sub):
        part = pl.ds(start, sub)
        value = message[:, :, part].astype(f32).reshape(64, sub)
        mean_sq = jnp.mean(value * value, axis=0, keepdims=True)
        normed = (value * lax.rsqrt(mean_sq + 1e-06) * column).astype(bf16)
        pre = jnp.dot(up[...], normed, preferred_element_type=f32)
        hidden = (pre * (1.0 / (1.0 + jnp.exp(-pre)))).astype(bf16)
        update = jnp.dot(down[...], hidden, preferred_element_type=f32)
        out[:, part] = (feat[:, part].astype(f32) + update).astype(bf16)


def body(
    positions,
    features,
    species,
    miller,
    species_table,
    filter_weight,
    norm_gain,
    up_weight,
    down_weight,
):
    atoms_here = features.shape[1]
    channels = features.shape[0]
    n_atom = lax.axis_size("atom")
    n_ka = lax.axis_size("ka")
    ka_split = n_ka // (channels // GROUP)
    local_count = atoms_here // n_ka
    scaling = 1.0 / math.sqrt(atoms_here * n_atom * K)
    params = pltpu.CompilerParams(vmem_limit_bytes=48 * 1024 * 1024)

    blocks = n_ka // n_atom
    millers = []
    for j in range(blocks):
        pairs = []
        for a in range(n_atom):
            for b in range(n_ka):
                pairs.append((a * n_ka + (b ^ (blocks * a + j)), a * n_ka + b))
        millers.append(lax.ppermute(miller, ("atom", "ka"), pairs))

    whole = pl.BlockSpec(memory_space=pltpu.VMEM)
    basis, z, acc, local_features = pl.pallas_call(
        functools.partial(factor_kernel, ka_split, 512),
        grid=(n_ka,),
        in_specs=[
            pl.BlockSpec((3, local_count), lambda i: (0, i)),
            pl.BlockSpec((channels, local_count), lambda i: (0, i)),
            pl.BlockSpec((1, local_count), lambda i: (0, i)),
            whole,
        ],
        out_specs=[
            pl.BlockSpec((ROWS, local_count), lambda i: (0, i)),
            pl.BlockSpec((16, local_count), lambda i: (0, i)),
            pl.BlockSpec((ROWS, 144), lambda i: (0, 0)),
            pl.BlockSpec((channels, local_count), lambda i: (0, 0)),
        ],
        out_shape=[
            jax.ShapeDtypeStruct((ROWS, atoms_here), bf16),
            jax.ShapeDtypeStruct((16, atoms_here), f32),
            jax.ShapeDtypeStruct((ROWS, 144), f32),
            jax.ShapeDtypeStruct((channels, local_count), bf16),
        ],
        scratch_shapes=[pltpu.VMEM((144, local_count), bf16)],
        compiler_params=params,
        cost_estimate=pl.CostEstimate(flops=5 * 10**9, bytes_accessed=14 * 10**6, transcendentals=0),
        name="factors",
    )(positions, features, species.reshape(1, atoms_here), species_table)

    payload = pl.pallas_call(
        pack_kernel,
        in_specs=[whole] * (1 + blocks),
        out_specs=whole,
        out_shape=jax.ShapeDtypeStruct((PAYLOAD, LANES), bf16),
        compiler_params=params,
        name="pack",
    )(acc, *millers)
    gathered = lax.all_gather(payload, "atom")

    message = pl.pallas_call(
        functools.partial(back_kernel, ka_split, scaling, 512),
        grid=(n_ka,),
        in_specs=[
            whole,
            whole,
            pl.BlockSpec((ROWS, local_count), lambda i: (0, i)),
            pl.BlockSpec((16, local_count), lambda i: (0, i)),
        ],
        out_specs=pl.BlockSpec((1, GROUP, local_count), lambda i: (i, 0, 0)),
        out_shape=jax.ShapeDtypeStruct((n_ka, GROUP, local_count), bf16),
        scratch_shapes=[pltpu.VMEM((144, 384), bf16)],
        compiler_params=params,
        cost_estimate=pl.CostEstimate(flops=5 * 10**9, bytes_accessed=11 * 10**6, transcendentals=0),
        name="back",
    )(gathered, filter_weight, basis, z)

    groups = None
    if ka_split > 1:
        message = message.reshape(n_ka // ka_split, ka_split, GROUP, local_count)
        message = lax.dynamic_index_in_dim(message, lax.axis_index("ka") % ka_split, 1, False)
        groups = [[g * ka_split + s for g in range(n_ka // ka_split)] for s in range(ka_split)]
    message = lax.all_to_all(message, "ka", 0, 0, axis_index_groups=groups, tiled=True)

    return pl.pallas_call(
        functools.partial(update_kernel, 512),
        in_specs=[whole] * 5,
        out_specs=whole,
        out_shape=jax.ShapeDtypeStruct((channels, local_count), bf16),
        compiler_params=params,
        name="update",
    )(message, local_features, norm_gain.reshape(1, channels), up_weight, down_weight)


def solution(mesh):
    in_specs = (P(None, "atom"), P(None, "atom"), P("atom"), P(None, "ka"), P(), P(), P(), P(), P())
    out_specs = P(None, ("atom", "ka"))
    return jax.shard_map(body, mesh=mesh, in_specs=in_specs, out_specs=out_specs, check_vma=False)
```

```python
import functools
import math

import jax
import jax.numpy as jnp
import numpy as np
from jax import lax
from jax.experimental import pallas as pl
from jax.experimental.pallas import tpu as pltpu
from jax.sharding import PartitionSpec as P

K = 4096
NRBF = 16
NSPEC = 8
MAXM = 8
GROUP = 8
ROWS = 304
CHUNK = 1024
WIDE = 2048
LANES = 128
PAYLOAD = 400
k_cutoff = 14.0
f32 = jnp.float32
bf16 = jnp.bfloat16


def fit(function, terms, odd):
    nodes = np.cos((np.arange(64) + 0.5) * np.pi / 64) * 0.5
    nodes = np.abs(nodes)
    target = function(2.0 * np.pi * nodes)
    if odd:
        target = target / nodes
    series = np.polynomial.chebyshev.Chebyshev.fit(nodes * nodes, target, terms - 1, domain=[0, 0.25])
    return [float(v) for v in series.convert(kind=np.polynomial.Polynomial).coef]


SIN = fit(np.sin, 7, True)
COS = fit(np.cos, 7, False)


def horner(coefs, x):
    total = coefs[-1] * x + coefs[-2]
    for value in coefs[-3::-1]:
        total = total * x + value
    return total


def first_harmonic(x):
    turns = x - jnp.floor(x + 0.5)
    square = turns * turns
    return horner(COS, square), turns * horner(SIN, square)


def iota(shape, axis):
    return lax.broadcasted_iota(jnp.int32, shape, axis)


def waves_to(scr, x):
    cosine, sine = first_harmonic(x)
    twice = cosine + cosine
    lower_c, lower_s = jnp.ones_like(cosine), jnp.zeros_like(sine)
    upper_c, upper_s = cosine, sine
    for m in range(MAXM):
        scr[8 * m : 8 * m + 8, :] = upper_c
        scr[64 + 8 * m : 72 + 8 * m, :] = upper_s
        lower_c, upper_c = upper_c, twice * upper_c - lower_c
        lower_s, upper_s = upper_s, twice * upper_s - lower_s


def spread(scr, row):
    return jnp.broadcast_to(scr[row : row + 1, :], (8, LANES))


def factor_chunk(pos, feat, species, table, odd, start, full, terms, z_out, w0, w1, w2):
    for axis, scr in enumerate((w0, w1, w2)):
        rows = [pos[axis : axis + 1, pl.ds(start + LANES * k, LANES)] for k in range(8)]
        waves_to(scr, jnp.concatenate(rows, 0))
    for k in range(8):
        part = pl.ds(start + LANES * k, LANES)
        c1 = w1[pl.ds(k, 8, stride=8), :]
        s1 = w1[pl.ds(64 + k, 8, stride=8), :]
        for m in range(16):
            left = spread(w0, 8 * m + k)
            full[16 * m : 16 * m + 16, part] = jnp.concatenate([left * c1, left * s1], 0).astype(bf16)
        c0 = w0[pl.ds(k, 8, stride=8), :]
        s0 = w0[pl.ds(64 + k, 8, stride=8), :]
        full[256:272, part] = jnp.concatenate([c0, s0], 0).astype(bf16)
        full[272:288, part] = jnp.concatenate([c1, s1], 0).astype(bf16)
        z_out[0:8, part] = w2[pl.ds(k, 8, stride=8), :]
        z_out[8:16, part] = w2[pl.ds(64 + k, 8, stride=8), :]
        kinds = jnp.broadcast_to(species[0:1, part], (8, LANES))
        embedded = table[0]
        for s in range(1, NSPEC):
            embedded = jnp.where(kinds == s, table[s], embedded)
        wide = feat[:, part].astype(f32)
        own = jnp.where(odd, wide[8:16], wide[0:8])
        source = (own + embedded).astype(bf16).astype(f32)
        for m in range(0, 16, 2):
            pair = [source * spread(w2, 8 * m + k), source * spread(w2, 8 * m + 8 + k)]
            terms[8 * m : 8 * m + 16, part] = jnp.concatenate(pair, 0).astype(bf16)
        terms[128:144, part] = jnp.concatenate([source, jnp.zeros_like(source)], 0).astype(bf16)


def choose(group, count):
    return (iota((count, 64), 1) == group * GROUP + iota((count, 64), 0) % GROUP).astype(f32)


def exact_dot(left, right, left_dim, right_dim):
    return lax.dot_general(
        left, right, (((left_dim,), (right_dim,)), ((), ())),
        precision=lax.Precision.HIGHEST, preferred_element_type=f32,
    )


def factor_kernel(ka_split, pos_hbm, feat_hbm, species_hbm, table, basis, z_out, acc, local_out,
                  pos, feat, species, full, terms, w0, w1, w2, sems, out_sems):
    me = lax.axis_index("ka")
    group = me // ka_split
    atoms, width = feat.shape[1], local_out.shape[1]
    first = pl.multiple_of((group // 2) * 16, 16)
    copies = [
        pltpu.make_async_copy(pos_hbm, pos, sems.at[0]),
        pltpu.make_async_copy(species_hbm, species, sems.at[1]),
        pltpu.make_async_copy(feat_hbm.at[pl.ds(first, 16), :], feat, sems.at[2]),
        pltpu.make_async_copy(
            feat_hbm.at[:, pl.ds(pl.multiple_of(me * width, width), width)], local_out, sems.at[3]
        ),
    ]
    for copy in copies:
        copy.start()
    full[288:304, :] = (iota((16, atoms), 0) == 0).astype(f32).astype(bf16)
    odd = (group % 2) == 1
    own = exact_dot(choose(group, GROUP), table[...], 1, 1)
    columns = [jnp.broadcast_to(own[:, s : s + 1], (8, LANES)) for s in range(NSPEC)]
    for copy in copies:
        copy.wait()

    def store(j):
        part = pl.ds(pl.multiple_of(j * CHUNK, CHUNK), CHUNK)
        return pltpu.make_async_copy(full.at[:, part], basis.at[:, part], out_sems.at[j])

    def step(j, carry):
        start = pl.multiple_of(j * CHUNK, CHUNK)
        factor_chunk(pos, feat, species, columns, odd, start, full, terms, z_out, w0, w1, w2)
        store(j).start()
        return carry

    steps = atoms // CHUNK
    lax.fori_loop(0, steps, step, 0)
    acc[...] = lax.dot_general(
        full[...], terms[...], (((1,), (1,)), ((), ())), preferred_element_type=f32
    )
    for j in range(steps):
        store(j).wait()


def pack_kernel(acc, *refs):
    millers, out = refs[:-1], refs[-1]
    out[0:ROWS, :] = acc[:, 0:LANES].astype(bf16)
    tail = jnp.concatenate([acc[:, 128:144], jnp.zeros((ROWS, 112), f32)], 1)
    tail = jnp.concatenate([tail, jnp.zeros((384 - ROWS, LANES), f32)], 0)
    flat = tail.T
    zero = jnp.zeros((GROUP, LANES), f32)
    pieces = [flat[0:8, 0:128], flat[0:8, 128:256], flat[0:8, 256:384], zero]
    out[304:336, :] = jnp.concatenate(pieces, 0).astype(bf16)
    counts = jnp.zeros((32, 256), f32)
    for ref in millers:
        m0, m1, m2 = ref[0:1, :], ref[1:2, :], ref[2:3, :]
        sign = jnp.where(17 * m0 + m1 < 0, -1, 1)
        m0, m1, m2 = m0 * sign, m1 * sign, m2 * sign
        inner = jnp.where(
            m1 > 0, 16 * m0 + m1 - 17, jnp.where(m1 < 0, 16 * m0 - m1 - 9, 127 + m0)
        )
        row = jnp.where(m0 > 0, inner, jnp.where(m1 > 0, 143 + m1, 160))
        column = jnp.where(row == 160, jnp.abs(m2), m2) + MAXM
        size = row.shape[1]
        row_hot = (iota((256, size), 0) == row).astype(f32).astype(bf16)
        column_hot = (iota((32, size), 0) == column).astype(f32).astype(bf16)
        counts = counts + lax.dot_general(
            column_hot, row_hot, (((1,), (1,)), ((), ())), preferred_element_type=f32
        )
    out[336:368, :] = counts[:, 0:128].astype(bf16)
    out[368:400, :] = counts[:, 128:256].astype(bf16)


def radial_sum(square, weight_of):
    magnitude = jnp.sqrt(square)
    total = None
    for b in range(NRBF):
        offset = (magnitude - b * (k_cutoff / (NRBF - 1))) * (NRBF / k_cutoff)
        term = weight_of(b) * jnp.exp(-(offset * offset))
        total = term if total is None else total + term
    return total


def filter_rows(payload, weights, group, scaling, gt_scr):
    total = payload[0].astype(f32)
    for a in range(1, payload.shape[0]):
        total = total + payload[a].astype(f32)
    counts = jnp.concatenate([total[336:368], total[368:400]], 1)
    lane = iota((32, LANES), 1)
    index = iota((32, LANES), 0) - MAXM
    height = (lane % 64) // 8 + 1
    plus = jnp.where(jnp.abs(index) == height, 1.0, 0.0)
    minus = jnp.where(index == height, 1.0, jnp.where(index == -height, -1.0, 0.0))
    minus = jnp.where(lane < 64, -minus, minus)
    spread = jnp.concatenate([plus, minus], 1).astype(f32)
    wide = exact_dot(counts.T, spread, 1, 0)
    across = exact_dot(weights[...], choose(group, LANES), 1, 1)
    lane = iota((88, LANES), 1)
    row = iota((88, LANES), 0)
    third = (lane % 64) // 8 + 1
    first = row // 8 + 1
    second = row % 8 + 1
    planar = jnp.where(
        row < 64,
        first * first + second * second,
        jnp.where(row < 80, second * second, 0),
    )
    radial = radial_sum((planar + third * third).astype(f32), lambda b: across[b : b + 1, :]) * scaling
    radial = jnp.concatenate([radial[0:64], radial], 0)

    def by_rows(value):
        both = value[0:128].reshape(8, 2, 8, LANES)
        edges = [value[128:136], value[144:152], value[160:168]]
        return jnp.concatenate([both[:, 0].reshape(64, LANES), both[:, 1].reshape(64, LANES)] + edges, 0)

    w_sum = by_rows(wide[:, 0:128]) * radial
    w_dif = by_rows(wide[:, 128:256]) * radial
    upper = total[0:128].reshape(8, 2, 8, LANES)
    lower = total[128:256].reshape(8, 2, 8, LANES)
    cc, cs = upper[:, 0].reshape(64, LANES), upper[:, 1].reshape(64, LANES)
    sc, ss = lower[:, 0].reshape(64, LANES), lower[:, 1].reshape(64, LANES)
    zero = jnp.zeros((8, LANES), f32)
    v_cos = jnp.concatenate([cc - ss, cc + ss, total[256:264], total[272:280], total[288:296]], 0)
    v_sin = jnp.concatenate([sc + cs, sc - cs, total[264:272], total[280:288], zero], 0)
    g_cos = w_sum * v_cos + w_dif * pltpu.roll(v_sin, 64, 1)
    g_sin = w_sum * v_sin - w_dif * pltpu.roll(v_cos, 64, 1)
    cp, cm, sp, sm = g_cos[0:64], g_cos[64:128], g_sin[0:64], g_sin[64:128]

    def pair_up(left, right):
        both = [left.reshape(8, 1, 8, LANES), right.reshape(8, 1, 8, LANES)]
        return jnp.concatenate(both, 1).reshape(128, LANES)

    rows = [pair_up(cp + cm, sp - sm), pair_up(sp + sm, cm - cp), g_cos[128:136], g_sin[128:136]]
    rows += [g_cos[136:144], g_sin[136:144], g_cos[144:152], jnp.zeros((88, LANES), f32)]
    full = jnp.concatenate(rows, 0)
    gt_scr[0:128, :] = full.T.astype(bf16)

    lane = iota((8, LANES), 1)
    cell = (lane // 16 + 1) * (lane // 16 + 1) + (lane % 8 + 1) * (lane % 8 + 1)
    edge = jnp.where(lane < 32, (lane % 8 + 1) * (lane % 8 + 1), 0)
    own = exact_dot(choose(group, GROUP), weights[...], 1, 1)
    flat = radial_sum(
        jnp.concatenate([cell, edge], 1).astype(f32), lambda b: own[:, b : b + 1]
    ) * scaling
    count0 = jnp.broadcast_to(counts[8:9, 0:128], (8, LANES))
    count1 = jnp.broadcast_to(counts[8:9, 128:256], (8, LANES))
    left = (lane // 8) % 2 == 0
    sigma = jnp.where(left, 1.0, -1.0).astype(f32)

    def swap(value):
        return jnp.where(left, pltpu.roll(value, LANES - 8, 1), pltpu.roll(value, 8, 1))

    other = swap(count0)
    x, y, rest = total[304:312], swap(total[312:320]), total[320:328]
    plus = (x - sigma * y) * flat[:, 0:128] * jnp.where(left, count0, other)
    less = (y + sigma * x) * flat[:, 0:128] * jnp.where(left, other, count0)
    rest = rest * flat[:, 128:256] * (count1 + pltpu.roll(count1, 8, 1))
    low = jnp.concatenate([plus + sigma * less, swap(less - sigma * plus), rest], 1)
    gt_scr[128:144, :] = jnp.concatenate([low, jnp.zeros_like(low)], 0).astype(bf16)


def back_kernel(ka_split, scaling, sub, payload, weights, basis_hbm, z, out, gt_scr, basis, sems):
    width = out.shape[2]
    steps = basis.shape[1] // WIDE
    fetches = []
    for j in range(steps):
        part = pl.ds(j * WIDE, WIDE)
        fetches.append(pltpu.make_async_copy(basis_hbm.at[:, part], basis.at[:, part], sems.at[j]))
    for fetch in fetches:
        fetch.start()
    filter_rows(payload, weights, lax.axis_index("ka") // ka_split, scaling, gt_scr)
    for j in range(steps):
        fetches[j].wait()
        product = jnp.dot(
            gt_scr[:, 0:ROWS], basis[:, j * WIDE : (j + 1) * WIDE], preferred_element_type=f32
        )
        for start in range(0, WIDE, sub):
            place = j * WIDE + start
            message = product[128:136, start : start + sub]
            for m in range(16):
                part = product[8 * m : 8 * m + 8, start : start + sub]
                message = message + z[m : m + 1, place : place + sub] * part
            offset = place % width
            out[place // width, :, offset : offset + sub] = message.astype(bf16)


def update_kernel(sub, message, feat, gain, up, down, out):
    width = feat.shape[1]
    eye = iota((64, 64), 0) == iota((64, 64), 1)
    column = jnp.sum(jnp.where(eye, jnp.broadcast_to(gain[...], (64, 64)), 0.0), axis=1, keepdims=True)
    for start in range(0, width, sub):
        part = pl.ds(start, sub)
        value = message[:, :, part].astype(f32).reshape(64, sub)
        mean_sq = jnp.mean(value * value, axis=0, keepdims=True)
        normed = (value * lax.rsqrt(mean_sq + 1e-06) * column).astype(bf16)
        pre = lax.dot_general(up[...], normed, (((0,), (0,)), ((), ())), preferred_element_type=f32)
        half = 0.5 * pre
        hidden = (half + half * jnp.tanh(half)).astype(bf16)
        update = jnp.dot(down[...], hidden, preferred_element_type=f32)
        out[:, part] = (feat[:, part].astype(f32) + update).astype(bf16)


def body(
    positions,
    features,
    species,
    miller,
    species_table,
    filter_weight,
    norm_gain,
    up_weight,
    down_weight,
):
    atoms_here = features.shape[1]
    channels = features.shape[0]
    n_atom = lax.axis_size("atom")
    n_ka = lax.axis_size("ka")
    ka_split = n_ka // (channels // GROUP)
    local_count = atoms_here // n_ka
    scaling = 1.0 / math.sqrt(atoms_here * n_atom * K)
    params = pltpu.CompilerParams(vmem_limit_bytes=24 * 1024 * 1024)

    blocks = n_ka // n_atom
    millers = []
    for j in range(blocks):
        pairs = []
        for a in range(n_atom):
            for b in range(n_ka):
                pairs.append((a * n_ka + (b ^ (blocks * a + j)), a * n_ka + b))
        millers.append(lax.ppermute(miller, ("atom", "ka"), pairs))

    whole = pl.BlockSpec(memory_space=pltpu.VMEM)
    hbm = pl.BlockSpec(memory_space=pltpu.HBM)
    basis, z, acc, local_features = pl.pallas_call(
        functools.partial(factor_kernel, ka_split),
        in_specs=[hbm, hbm, hbm, whole],
        out_specs=[hbm, whole, whole, whole],
        out_shape=[
            pltpu.HBM((ROWS, atoms_here), bf16),
            jax.ShapeDtypeStruct((16, atoms_here), f32),
            jax.ShapeDtypeStruct((ROWS, 144), f32),
            jax.ShapeDtypeStruct((channels, local_count), bf16),
        ],
        scratch_shapes=[
            pltpu.VMEM((3, atoms_here), f32),
            pltpu.VMEM((16, atoms_here), bf16),
            pltpu.VMEM((1, atoms_here), jnp.int32),
            pltpu.VMEM((ROWS, atoms_here), bf16),
            pltpu.VMEM((144, atoms_here), bf16),
            pltpu.VMEM((LANES, LANES), f32),
            pltpu.VMEM((LANES, LANES), f32),
            pltpu.VMEM((LANES, LANES), f32),
            pltpu.SemaphoreType.DMA((4,)),
            pltpu.SemaphoreType.DMA((atoms_here // CHUNK,)),
        ],
        compiler_params=params,
        cost_estimate=pl.CostEstimate(flops=5 * 10**9, bytes_accessed=14 * 10**6, transcendentals=0),
        name="factors",
    )(
        pltpu.with_memory_space_constraint(positions, pltpu.HBM),
        pltpu.with_memory_space_constraint(features, pltpu.HBM),
        pltpu.with_memory_space_constraint(species.reshape(1, atoms_here), pltpu.HBM),
        species_table.T,
    )

    payload = pl.pallas_call(
        pack_kernel,
        in_specs=[whole] * (1 + blocks),
        out_specs=whole,
        out_shape=jax.ShapeDtypeStruct((PAYLOAD, LANES), bf16),
        compiler_params=params,
        name="pack",
    )(acc, *millers)
    gathered = lax.all_gather(payload, "atom")

    message = pl.pallas_call(
        functools.partial(back_kernel, ka_split, scaling, min(512, local_count)),
        in_specs=[whole, whole, hbm, whole],
        out_specs=whole,
        out_shape=jax.ShapeDtypeStruct((n_ka, GROUP, local_count), bf16),
        scratch_shapes=[
            pltpu.VMEM((144, 384), bf16),
            pltpu.VMEM(basis.shape, bf16),
            pltpu.SemaphoreType.DMA((atoms_here // WIDE,)),
        ],
        compiler_params=params,
        cost_estimate=pl.CostEstimate(flops=5 * 10**9, bytes_accessed=11 * 10**6, transcendentals=0),
        name="back",
    )(gathered, filter_weight.T, pltpu.with_memory_space_constraint(basis, pltpu.HBM), z)

    groups = None
    if ka_split > 1:
        message = message.reshape(n_ka // ka_split, ka_split, GROUP, local_count)
        message = lax.dynamic_index_in_dim(message, lax.axis_index("ka") % ka_split, 1, False)
        groups = [[g * ka_split + s for g in range(n_ka // ka_split)] for s in range(ka_split)]
    message = lax.all_to_all(message, "ka", 0, 0, axis_index_groups=groups, tiled=True)

    return pl.pallas_call(
        functools.partial(update_kernel, 512),
        in_specs=[whole] * 5,
        out_specs=whole,
        out_shape=jax.ShapeDtypeStruct((channels, local_count), bf16),
        compiler_params=params,
        name="update",
    )(message, local_features, norm_gain.reshape(1, channels), up_weight.T, down_weight)


def solution(mesh):
    in_specs = (P(None, "atom"), P(None, "atom"), P("atom"), P(None, "ka"), P(), P(), P(), P(), P())
    out_specs = P(None, ("atom", "ka"))
    return jax.shard_map(body, mesh=mesh, in_specs=in_specs, out_specs=out_specs, check_vma=False)
```

```python
import functools
import math

import jax
import jax.numpy as jnp
import numpy as np
from jax import lax
from jax.experimental import pallas as pl
from jax.experimental.pallas import tpu as pltpu
from jax.sharding import PartitionSpec as P

K = 4096
NRBF = 16
NSPEC = 8
MAXM = 8
GROUP = 8
ROWS = 304
CHUNK = 1024
SPAN = 4
PARTS = 4
LANES = 128
PAYLOAD = 400
k_cutoff = 14.0
f32 = jnp.float32
bf16 = jnp.bfloat16


def fit(function, terms, odd):
    nodes = np.cos((np.arange(64) + 0.5) * np.pi / 64) * 0.5
    nodes = np.abs(nodes)
    target = function(2.0 * np.pi * nodes)
    if odd:
        target = target / nodes
    series = np.polynomial.chebyshev.Chebyshev.fit(nodes * nodes, target, terms - 1, domain=[0, 0.25])
    return [float(v) for v in series.convert(kind=np.polynomial.Polynomial).coef]


SIN = fit(np.sin, 7, True)
COS = fit(np.cos, 7, False)


def horner(coefs, x):
    total = coefs[-1] * x + coefs[-2]
    for value in coefs[-3::-1]:
        total = total * x + value
    return total


def first_harmonic(x):
    turns = x - jnp.floor(x + 0.5)
    square = turns * turns
    return horner(COS, square), turns * horner(SIN, square)


def iota(shape, axis):
    return lax.broadcasted_iota(jnp.int32, shape, axis)


def waves_to(scr, x):
    cosine, sine = first_harmonic(x)
    twice = cosine + cosine
    lower_c, lower_s = jnp.ones_like(cosine), jnp.zeros_like(sine)
    upper_c, upper_s = cosine, sine
    for m in range(MAXM):
        scr[8 * m : 8 * m + 8, :] = upper_c
        scr[64 + 8 * m : 72 + 8 * m, :] = upper_s
        lower_c, upper_c = upper_c, twice * upper_c - lower_c
        lower_s, upper_s = upper_s, twice * upper_s - lower_s


def spread(scr, row):
    pieces = [jnp.broadcast_to(scr[row + k : row + k + 1, :], (8, LANES)) for k in range(SPAN)]
    return jnp.concatenate(pieces, 1)


def comb(scr, row):
    return jnp.concatenate([scr[pl.ds(row + k, 8, stride=8), :] for k in range(SPAN)], 1)


def factor_chunk(pos, feat, species, table, odd, start, here, full, terms, z_out, w0, w1, w2):
    for axis, scr in enumerate((w0, w1, w2)):
        rows = [pos[axis : axis + 1, pl.ds(start + LANES * k, LANES)] for k in range(8)]
        waves_to(scr, jnp.concatenate(rows, 0))
    for k in range(0, 8, SPAN):
        part = pl.ds(start + LANES * k, LANES * SPAN)
        local = pl.ds(here + LANES * k, LANES * SPAN)
        c1 = comb(w1, k)
        s1 = comb(w1, 64 + k)
        for m in range(16):
            left = spread(w0, 8 * m + k)
            full[16 * m : 16 * m + 16, local] = jnp.concatenate([left * c1, left * s1], 0).astype(bf16)
        full[256:272, local] = jnp.concatenate([comb(w0, k), comb(w0, 64 + k)], 0).astype(bf16)
        full[272:288, local] = jnp.concatenate([c1, s1], 0).astype(bf16)
        z_out[0:8, part] = comb(w2, k)
        z_out[8:16, part] = comb(w2, 64 + k)
        kinds = jnp.broadcast_to(species[0:1, part], (8, LANES * SPAN))
        embedded = table[0]
        for s in range(1, NSPEC):
            embedded = jnp.where(kinds == s, table[s], embedded)
        wide = feat[:, part].astype(f32)
        own = jnp.where(odd, wide[8:16], wide[0:8])
        source = (own + embedded).astype(bf16).astype(f32)
        for m in range(0, 16, 2):
            pair = [source * spread(w2, 8 * m + k), source * spread(w2, 8 * m + 8 + k)]
            terms[8 * m : 8 * m + 16, part] = jnp.concatenate(pair, 0).astype(bf16)
        terms[128:144, part] = jnp.concatenate([source, jnp.zeros_like(source)], 0).astype(bf16)


def choose(group, count):
    return (iota((count, 64), 1) == group * GROUP + iota((count, 64), 0) % GROUP).astype(f32)


def exact_dot(left, right, left_dim, right_dim):
    return lax.dot_general(
        left, right, (((left_dim,), (right_dim,)), ((), ())),
        precision=lax.Precision.HIGHEST, preferred_element_type=f32,
    )


def factor_kernel(ka_split, pos_hbm, feat_hbm, species_hbm, table, z_out, acc, local_out, *refs):
    basis = refs[:PARTS]
    pos, feat, species, terms, w0, w1, w2, sems = refs[PARTS:]
    me = lax.axis_index("ka")
    group = me // ka_split
    atoms, width = feat.shape[1], local_out.shape[1]
    first = pl.multiple_of((group // 2) * 16, 16)
    copies = [
        pltpu.make_async_copy(pos_hbm, pos, sems.at[0]),
        pltpu.make_async_copy(species_hbm, species, sems.at[1]),
        pltpu.make_async_copy(feat_hbm.at[pl.ds(first, 16), :], feat, sems.at[2]),
        pltpu.make_async_copy(
            feat_hbm.at[:, pl.ds(pl.multiple_of(me * width, width), width)], local_out, sems.at[3]
        ),
    ]
    for copy in copies:
        copy.start()
    size = atoms // PARTS
    for full in basis:
        full[288:304, :] = (iota((16, size), 0) == 0).astype(f32).astype(bf16)
    odd = (group % 2) == 1
    own = exact_dot(choose(group, GROUP), table[...], 1, 1)
    columns = [jnp.broadcast_to(own[:, s : s + 1], (8, LANES * SPAN)) for s in range(NSPEC)]
    for copy in copies:
        copy.wait()

    total = None
    for p, full in enumerate(basis):

        def step(j, carry):
            here = pl.multiple_of(j * CHUNK, CHUNK)
            factor_chunk(
                pos, feat, species, columns, odd, p * size + here, here, full, terms, z_out, w0, w1, w2
            )
            return carry

        lax.fori_loop(0, size // CHUNK, step, 0)
    for p, full in enumerate(basis):
        piece = lax.dot_general(
            full[...], terms[:, p * size : (p + 1) * size],
            (((1,), (1,)), ((), ())), preferred_element_type=f32,
        )
        total = piece if total is None else total + piece
    acc[...] = total


def pack_kernel(acc, *refs):
    millers, out = refs[:-1], refs[-1]
    out[0:ROWS, :] = acc[:, 0:LANES].astype(bf16)
    tail = jnp.concatenate([acc[:, 128:144], jnp.zeros((ROWS, 112), f32)], 1)
    tail = jnp.concatenate([tail, jnp.zeros((384 - ROWS, LANES), f32)], 0)
    flat = tail.T
    zero = jnp.zeros((GROUP, LANES), f32)
    pieces = [flat[0:8, 0:128], flat[0:8, 128:256], flat[0:8, 256:384], zero]
    out[304:336, :] = jnp.concatenate(pieces, 0).astype(bf16)
    counts = jnp.zeros((32, 256), f32)
    for ref in millers:
        m0, m1, m2 = ref[0:1, :], ref[1:2, :], ref[2:3, :]
        sign = jnp.where(17 * m0 + m1 < 0, -1, 1)
        m0, m1, m2 = m0 * sign, m1 * sign, m2 * sign
        inner = jnp.where(
            m1 > 0, 16 * m0 + m1 - 17, jnp.where(m1 < 0, 16 * m0 - m1 - 9, 127 + m0)
        )
        row = jnp.where(m0 > 0, inner, jnp.where(m1 > 0, 143 + m1, 160))
        column = jnp.where(row == 160, jnp.abs(m2), m2) + MAXM
        size = row.shape[1]
        row_hot = (iota((256, size), 0) == row).astype(f32).astype(bf16)
        column_hot = (iota((32, size), 0) == column).astype(f32).astype(bf16)
        counts = counts + lax.dot_general(
            column_hot, row_hot, (((1,), (1,)), ((), ())), preferred_element_type=f32
        )
    out[336:368, :] = counts[:, 0:128].astype(bf16)
    out[368:400, :] = counts[:, 128:256].astype(bf16)


def radial_sum(square, weight_of):
    magnitude = jnp.sqrt(square)
    total = None
    for b in range(NRBF):
        offset = (magnitude - b * (k_cutoff / (NRBF - 1))) * (NRBF / k_cutoff)
        term = weight_of(b) * jnp.exp(-(offset * offset))
        total = term if total is None else total + term
    return total


def filter_rows(payload, weights, group, scaling, gt_scr):
    total = payload[0].astype(f32)
    for a in range(1, payload.shape[0]):
        total = total + payload[a].astype(f32)
    counts = jnp.concatenate([total[336:368], total[368:400]], 1)
    lane = iota((32, LANES), 1)
    index = iota((32, LANES), 0) - MAXM
    height = (lane % 64) // 8 + 1
    plus = jnp.where(jnp.abs(index) == height, 1.0, 0.0)
    minus = jnp.where(index == height, 1.0, jnp.where(index == -height, -1.0, 0.0))
    minus = jnp.where(lane < 64, -minus, minus)
    spread = jnp.concatenate([plus, minus], 1).astype(f32)
    wide = exact_dot(counts.T, spread, 1, 0)
    across = exact_dot(weights[...], choose(group, LANES), 1, 1)
    lane = iota((88, LANES), 1)
    row = iota((88, LANES), 0)
    third = (lane % 64) // 8 + 1
    first = row // 8 + 1
    second = row % 8 + 1
    planar = jnp.where(
        row < 64,
        first * first + second * second,
        jnp.where(row < 80, second * second, 0),
    )
    radial = radial_sum((planar + third * third).astype(f32), lambda b: across[b : b + 1, :]) * scaling
    radial = jnp.concatenate([radial[0:64], radial], 0)

    def by_rows(value):
        both = value[0:128].reshape(8, 2, 8, LANES)
        edges = [value[128:136], value[144:152], value[160:168]]
        return jnp.concatenate([both[:, 0].reshape(64, LANES), both[:, 1].reshape(64, LANES)] + edges, 0)

    w_sum = by_rows(wide[:, 0:128]) * radial
    w_dif = by_rows(wide[:, 128:256]) * radial
    upper = total[0:128].reshape(8, 2, 8, LANES)
    lower = total[128:256].reshape(8, 2, 8, LANES)
    cc, cs = upper[:, 0].reshape(64, LANES), upper[:, 1].reshape(64, LANES)
    sc, ss = lower[:, 0].reshape(64, LANES), lower[:, 1].reshape(64, LANES)
    zero = jnp.zeros((8, LANES), f32)
    v_cos = jnp.concatenate([cc - ss, cc + ss, total[256:264], total[272:280], total[288:296]], 0)
    v_sin = jnp.concatenate([sc + cs, sc - cs, total[264:272], total[280:288], zero], 0)
    g_cos = w_sum * v_cos + w_dif * pltpu.roll(v_sin, 64, 1)
    g_sin = w_sum * v_sin - w_dif * pltpu.roll(v_cos, 64, 1)
    cp, cm, sp, sm = g_cos[0:64], g_cos[64:128], g_sin[0:64], g_sin[64:128]

    def pair_up(left, right):
        both = [left.reshape(8, 1, 8, LANES), right.reshape(8, 1, 8, LANES)]
        return jnp.concatenate(both, 1).reshape(128, LANES)

    rows = [pair_up(cp + cm, sp - sm), pair_up(sp + sm, cm - cp), g_cos[128:136], g_sin[128:136]]
    rows += [g_cos[136:144], g_sin[136:144], g_cos[144:152], jnp.zeros((88, LANES), f32)]
    full = jnp.concatenate(rows, 0)
    gt_scr[0:128, :] = full.T.astype(bf16)

    lane = iota((8, LANES), 1)
    cell = (lane // 16 + 1) * (lane // 16 + 1) + (lane % 8 + 1) * (lane % 8 + 1)
    edge = jnp.where(lane < 32, (lane % 8 + 1) * (lane % 8 + 1), 0)
    own = exact_dot(choose(group, GROUP), weights[...], 1, 1)
    flat = radial_sum(
        jnp.concatenate([cell, edge], 1).astype(f32), lambda b: own[:, b : b + 1]
    ) * scaling
    count0 = jnp.broadcast_to(counts[8:9, 0:128], (8, LANES))
    count1 = jnp.broadcast_to(counts[8:9, 128:256], (8, LANES))
    left = (lane // 8) % 2 == 0
    sigma = jnp.where(left, 1.0, -1.0).astype(f32)

    def swap(value):
        return jnp.where(left, pltpu.roll(value, LANES - 8, 1), pltpu.roll(value, 8, 1))

    other = swap(count0)
    x, y, rest = total[304:312], swap(total[312:320]), total[320:328]
    plus = (x - sigma * y) * flat[:, 0:128] * jnp.where(left, count0, other)
    less = (y + sigma * x) * flat[:, 0:128] * jnp.where(left, other, count0)
    rest = rest * flat[:, 128:256] * (count1 + pltpu.roll(count1, 8, 1))
    low = jnp.concatenate([plus + sigma * less, swap(less - sigma * plus), rest], 1)
    gt_scr[128:144, :] = jnp.concatenate([low, jnp.zeros_like(low)], 0).astype(bf16)


def back_kernel(ka_split, scaling, sub, payload, weights, z, *refs):
    basis, out, gt_scr = refs[:PARTS], refs[PARTS], refs[PARTS + 1]
    width = out.shape[2]
    filter_rows(payload, weights, lax.axis_index("ka") // ka_split, scaling, gt_scr)
    for j, piece in enumerate(basis):
        size = piece.shape[1]
        product = jnp.dot(gt_scr[:, 0:ROWS], piece[...], preferred_element_type=f32)
        for start in range(0, size, sub):
            place = j * size + start
            message = product[128:136, start : start + sub]
            for m in range(16):
                part = product[8 * m : 8 * m + 8, start : start + sub]
                message = message + z[m : m + 1, place : place + sub] * part
            offset = place % width
            out[place // width, :, offset : offset + sub] = message.astype(bf16)


def update_kernel(sub, message, feat, gain, up, down, out):
    width = feat.shape[1]
    eye = iota((64, 64), 0) == iota((64, 64), 1)
    column = jnp.sum(jnp.where(eye, jnp.broadcast_to(gain[...], (64, 64)), 0.0), axis=1, keepdims=True)
    for start in range(0, width, sub):
        part = pl.ds(start, sub)
        value = message[:, :, part].astype(f32).reshape(64, sub)
        mean_sq = jnp.mean(value * value, axis=0, keepdims=True)
        normed = (value * lax.rsqrt(mean_sq + 1e-06) * column).astype(bf16)
        pre = lax.dot_general(up[...], normed, (((0,), (0,)), ((), ())), preferred_element_type=f32)
        half = 0.5 * pre
        hidden = (half + half * jnp.tanh(half)).astype(bf16)
        update = jnp.dot(down[...], hidden, preferred_element_type=f32)
        out[:, part] = (feat[:, part].astype(f32) + update).astype(bf16)


def body(
    positions,
    features,
    species,
    miller,
    species_table,
    filter_weight,
    norm_gain,
    up_weight,
    down_weight,
):
    atoms_here = features.shape[1]
    channels = features.shape[0]
    n_atom = lax.axis_size("atom")
    n_ka = lax.axis_size("ka")
    ka_split = n_ka // (channels // GROUP)
    local_count = atoms_here // n_ka
    scaling = 1.0 / math.sqrt(atoms_here * n_atom * K)
    params = pltpu.CompilerParams(vmem_limit_bytes=24 * 1024 * 1024)

    blocks = n_ka // n_atom
    millers = []
    for j in range(blocks):
        pairs = []
        for a in range(n_atom):
            for b in range(n_ka):
                pairs.append((a * n_ka + (b ^ (blocks * a + j)), a * n_ka + b))
        millers.append(lax.ppermute(miller, ("atom", "ka"), pairs))

    whole = pl.BlockSpec(memory_space=pltpu.VMEM)
    hbm = pl.BlockSpec(memory_space=pltpu.HBM)
    hbm = pl.BlockSpec(memory_space=pltpu.HBM)
    z, acc, local_features, *basis = pl.pallas_call(
        functools.partial(factor_kernel, ka_split),
        in_specs=[hbm, hbm, hbm, whole],
        out_specs=[whole] * (3 + PARTS),
        out_shape=[
            jax.ShapeDtypeStruct((16, atoms_here), f32),
            jax.ShapeDtypeStruct((ROWS, 144), f32),
            jax.ShapeDtypeStruct((channels, local_count), bf16),
        ]
        + [jax.ShapeDtypeStruct((ROWS, atoms_here // PARTS), bf16)] * PARTS,
        scratch_shapes=[
            pltpu.VMEM((3, atoms_here), f32),
            pltpu.VMEM((16, atoms_here), bf16),
            pltpu.VMEM((1, atoms_here), jnp.int32),
            pltpu.VMEM((144, atoms_here), bf16),
            pltpu.VMEM((LANES, LANES), f32),
            pltpu.VMEM((LANES, LANES), f32),
            pltpu.VMEM((LANES, LANES), f32),
            pltpu.SemaphoreType.DMA((4,)),
        ],
        compiler_params=params,
        cost_estimate=pl.CostEstimate(flops=5 * 10**9, bytes_accessed=14 * 10**6, transcendentals=0),
        name="factors",
    )(
        pltpu.with_memory_space_constraint(positions, pltpu.HBM),
        pltpu.with_memory_space_constraint(features, pltpu.HBM),
        pltpu.with_memory_space_constraint(species.reshape(1, atoms_here), pltpu.HBM),
        species_table.T,
    )

    payload = pl.pallas_call(
        pack_kernel,
        in_specs=[whole] * (1 + blocks),
        out_specs=whole,
        out_shape=jax.ShapeDtypeStruct((PAYLOAD, LANES), bf16),
        compiler_params=params,
        name="pack",
    )(acc, *millers)
    gathered = lax.all_gather(payload, "atom")

    message = pl.pallas_call(
        functools.partial(back_kernel, ka_split, scaling, min(512, local_count)),
        in_specs=[whole] * (3 + PARTS),
        out_specs=whole,
        out_shape=jax.ShapeDtypeStruct((n_ka, GROUP, local_count), bf16),
        scratch_shapes=[pltpu.VMEM((144, 384), bf16)],
        compiler_params=params,
        cost_estimate=pl.CostEstimate(flops=5 * 10**9, bytes_accessed=11 * 10**6, transcendentals=0),
        name="back",
    )(gathered, filter_weight.T, z, *basis)

    groups = None
    if ka_split > 1:
        message = message.reshape(n_ka // ka_split, ka_split, GROUP, local_count)
        message = lax.dynamic_index_in_dim(message, lax.axis_index("ka") % ka_split, 1, False)
        groups = [[g * ka_split + s for g in range(n_ka // ka_split)] for s in range(ka_split)]
    message = lax.all_to_all(message, "ka", 0, 0, axis_index_groups=groups, tiled=True)

    return pl.pallas_call(
        functools.partial(update_kernel, 512),
        in_specs=[whole] * 5,
        out_specs=whole,
        out_shape=jax.ShapeDtypeStruct((channels, local_count), bf16),
        compiler_params=params,
        name="update",
    )(message, local_features, norm_gain.reshape(1, channels), up_weight.T, down_weight)


def solution(mesh):
    in_specs = (P(None, "atom"), P(None, "atom"), P("atom"), P(None, "ka"), P(), P(), P(), P(), P())
    out_specs = P(None, ("atom", "ka"))
    return jax.shard_map(body, mesh=mesh, in_specs=in_specs, out_specs=out_specs, check_vma=False)
```

```python
import functools
import math

import jax
import jax.numpy as jnp
import numpy as np
from jax import lax
from jax.experimental import pallas as pl
from jax.experimental.pallas import tpu as pltpu
from jax.sharding import PartitionSpec as P

K = 4096
NRBF = 16
NSPEC = 8
MAXM = 8
GROUP = 8
ROWS = 304
CHUNK = 1024
SPAN = 4
PARTS = 4
LANES = 128
PAYLOAD = 400
k_cutoff = 14.0
f32 = jnp.float32
bf16 = jnp.bfloat16


def fit(function, terms, odd):
    nodes = np.cos((np.arange(64) + 0.5) * np.pi / 64) * 0.5
    nodes = np.abs(nodes)
    target = function(2.0 * np.pi * nodes)
    if odd:
        target = target / nodes
    series = np.polynomial.chebyshev.Chebyshev.fit(nodes * nodes, target, terms - 1, domain=[0, 0.25])
    return [float(v) for v in series.convert(kind=np.polynomial.Polynomial).coef]


SIN = fit(np.sin, 7, True)
COS = fit(np.cos, 7, False)


def horner(coefs, x):
    total = coefs[-1] * x + coefs[-2]
    for value in coefs[-3::-1]:
        total = total * x + value
    return total


def first_harmonic(x):
    turns = x - jnp.floor(x + 0.5)
    square = turns * turns
    return horner(COS, square), turns * horner(SIN, square)


def iota(shape, axis):
    return lax.broadcasted_iota(jnp.int32, shape, axis)


def waves_to(scr, x):
    cosine, sine = first_harmonic(x)
    twice = cosine + cosine
    lower_c, lower_s = jnp.ones_like(cosine), jnp.zeros_like(sine)
    upper_c, upper_s = cosine, sine
    for m in range(MAXM):
        scr[8 * m : 8 * m + 8, :] = upper_c
        scr[64 + 8 * m : 72 + 8 * m, :] = upper_s
        lower_c, upper_c = upper_c, twice * upper_c - lower_c
        lower_s, upper_s = upper_s, twice * upper_s - lower_s


def spread(scr, row):
    pieces = [jnp.broadcast_to(scr[row + k : row + k + 1, :], (8, LANES)) for k in range(SPAN)]
    return jnp.concatenate(pieces, 1)


def comb(scr, row):
    return jnp.concatenate([scr[pl.ds(row + k, 8, stride=8), :] for k in range(SPAN)], 1)


def harmonics_chunk(pos, start, w0, w1, w2):
    for axis, scr in enumerate((w0, w1, w2)):
        rows = [pos[axis : axis + 1, pl.ds(start + LANES * k, LANES)] for k in range(8)]
        waves_to(scr, jnp.concatenate(rows, 0))


def factor_chunk(feat, species, table, odd, start, here, k, full, terms, z_out, w0, w1, w2):
    part = pl.ds(start, LANES * SPAN)
    local = pl.ds(here, LANES * SPAN)
    c1 = comb(w1, k)
    s1 = comb(w1, 64 + k)
    for m in range(16):
        left = spread(w0, 8 * m + k)
        full[16 * m : 16 * m + 16, local] = jnp.concatenate([left * c1, left * s1], 0).astype(bf16)
    full[256:272, local] = jnp.concatenate([comb(w0, k), comb(w0, 64 + k)], 0).astype(bf16)
    full[272:288, local] = jnp.concatenate([c1, s1], 0).astype(bf16)
    z_out[0:8, part] = comb(w2, k)
    z_out[8:16, part] = comb(w2, 64 + k)
    kinds = jnp.broadcast_to(species[0:1, part], (8, LANES * SPAN))
    embedded = table[0]
    for s in range(1, NSPEC):
        embedded = jnp.where(kinds == s, table[s], embedded)
    wide = feat[:, part].astype(f32)
    own = jnp.where(odd, wide[8:16], wide[0:8])
    source = (own + embedded).astype(bf16).astype(f32)
    for m in range(0, 16, 2):
        pair = [source * spread(w2, 8 * m + k), source * spread(w2, 8 * m + 8 + k)]
        terms[8 * m : 8 * m + 16, part] = jnp.concatenate(pair, 0).astype(bf16)
    terms[128:144, part] = jnp.concatenate([source, jnp.zeros_like(source)], 0).astype(bf16)


def choose(group, count):
    return (iota((count, 64), 1) == group * GROUP + iota((count, 64), 0) % GROUP).astype(f32)


def exact_dot(left, right, left_dim, right_dim):
    return lax.dot_general(
        left, right, (((left_dim,), (right_dim,)), ((), ())),
        precision=lax.Precision.HIGHEST, preferred_element_type=f32,
    )


def factor_kernel(ka_split, pos_hbm, feat_hbm, species_hbm, table_hbm, z_out, acc, local_out, *refs):
    basis = refs[:PARTS]
    pos, feat, species, table, terms, w0, w1, w2, sems = refs[PARTS:]
    me = lax.axis_index("ka")
    group = me // ka_split
    atoms, width = feat.shape[1], local_out.shape[1]
    first = pl.multiple_of((group // 2) * 16, 16)
    size = atoms // PARTS
    copies = [pltpu.make_async_copy(table_hbm, table, sems.at[0])]
    waits = []
    for p in range(PARTS):
        cut = pl.ds(p * size, size)
        waits.append(
            [
                pltpu.make_async_copy(pos_hbm.at[:, cut], pos.at[:, cut], sems.at[3 * p + 2]),
                pltpu.make_async_copy(species_hbm.at[:, cut], species.at[:, cut], sems.at[3 * p + 3]),
                pltpu.make_async_copy(
                    feat_hbm.at[pl.ds(first, 16), cut], feat.at[:, cut], sems.at[3 * p + 4]
                ),
            ]
        )
        copies += waits[p]
    keep = pltpu.make_async_copy(
        feat_hbm.at[:, pl.ds(pl.multiple_of(me * width, width), width)], local_out, sems.at[1]
    )
    for copy in copies + [keep]:
        copy.start()
    for full in basis:
        full[288:304, :] = (iota((16, size), 0) == 0).astype(f32).astype(bf16)
    odd = (group % 2) == 1
    copies[0].wait()
    own = exact_dot(choose(group, GROUP), table[...], 1, 1)
    columns = [jnp.broadcast_to(own[:, s : s + 1], (8, LANES * SPAN)) for s in range(NSPEC)]

    def step(p, j):
        here = pl.multiple_of(j * CHUNK, CHUNK)
        harmonics_chunk(pos, p * size + here, w0, w1, w2)
        for k in range(0, 8, SPAN):
            factor_chunk(
                feat, species, columns, odd, p * size + here + k * LANES, here + k * LANES, k,
                basis[p], terms, z_out, w0, w1, w2,
            )

    for p in range(PARTS):
        for copy in waits[p]:
            copy.wait()
        lax.fori_loop(0, size // CHUNK, lambda j, carry: step(p, j), None, unroll=4)
    total = None
    for p, full in enumerate(basis):
        piece = lax.dot_general(
            full[...], terms[:, p * size : (p + 1) * size],
            (((1,), (1,)), ((), ())), preferred_element_type=f32,
        )
        total = piece if total is None else total + piece
    acc[...] = total
    keep.wait()


def pack_kernel(acc, *refs):
    millers, out = refs[:-1], refs[-1]
    out[0:ROWS, :] = acc[:, 0:LANES].astype(bf16)
    tail = jnp.concatenate([acc[:, 128:144], jnp.zeros((ROWS, 112), f32)], 1)
    tail = jnp.concatenate([tail, jnp.zeros((384 - ROWS, LANES), f32)], 0)
    flat = tail.T
    zero = jnp.zeros((GROUP, LANES), f32)
    pieces = [flat[0:8, 0:128], flat[0:8, 128:256], flat[0:8, 256:384], zero]
    out[304:336, :] = jnp.concatenate(pieces, 0).astype(bf16)
    counts = jnp.zeros((32, 256), f32)
    for ref in millers:
        m0, m1, m2 = ref[0:1, :], ref[1:2, :], ref[2:3, :]
        sign = jnp.where(17 * m0 + m1 < 0, -1, 1)
        m0, m1, m2 = m0 * sign, m1 * sign, m2 * sign
        inner = jnp.where(
            m1 > 0, 16 * m0 + m1 - 17, jnp.where(m1 < 0, 16 * m0 - m1 - 9, 127 + m0)
        )
        row = jnp.where(m0 > 0, inner, jnp.where(m1 > 0, 143 + m1, 160))
        column = jnp.where(row == 160, jnp.abs(m2), m2) + MAXM
        size = row.shape[1]
        row_hot = (iota((256, size), 0) == row).astype(f32).astype(bf16)
        column_hot = (iota((32, size), 0) == column).astype(f32).astype(bf16)
        counts = counts + lax.dot_general(
            column_hot, row_hot, (((1,), (1,)), ((), ())), preferred_element_type=f32
        )
    out[336:368, :] = counts[:, 0:128].astype(bf16)
    out[368:400, :] = counts[:, 128:256].astype(bf16)


def fold_kernel(left, right, out):
    out[...] = (left[...].astype(f32) + right[...].astype(f32)).astype(bf16)


def radial_sum(square, weight_of):
    magnitude = jnp.sqrt(square)
    total = None
    for b in range(NRBF):
        offset = (magnitude - b * (k_cutoff / (NRBF - 1))) * (NRBF / k_cutoff)
        term = weight_of(b) * jnp.exp(-(offset * offset))
        total = term if total is None else total + term
    return total


def filter_rows(payload, weights, group, scaling, gt_scr):
    total = payload[0][...].astype(f32)
    for part in payload[1:]:
        total = total + part[...].astype(f32)
    counts = jnp.concatenate([total[336:368], total[368:400]], 1)
    lane = iota((32, LANES), 1)
    index = iota((32, LANES), 0) - MAXM
    height = (lane % 64) // 8 + 1
    plus = jnp.where(jnp.abs(index) == height, 1.0, 0.0)
    minus = jnp.where(index == height, 1.0, jnp.where(index == -height, -1.0, 0.0))
    minus = jnp.where(lane < 64, -minus, minus)
    spread = jnp.concatenate([plus, minus], 1).astype(f32)
    wide = exact_dot(counts.T, spread, 1, 0)
    across = exact_dot(weights[...], choose(group, LANES), 1, 1)
    lane = iota((88, LANES), 1)
    row = iota((88, LANES), 0)
    third = (lane % 64) // 8 + 1
    first = row // 8 + 1
    second = row % 8 + 1
    planar = jnp.where(
        row < 64,
        first * first + second * second,
        jnp.where(row < 80, second * second, 0),
    )
    radial = radial_sum((planar + third * third).astype(f32), lambda b: across[b : b + 1, :]) * scaling
    radial = jnp.concatenate([radial[0:64], radial], 0)

    def by_rows(value):
        both = value[0:128].reshape(8, 2, 8, LANES)
        edges = [value[128:136], value[144:152], value[160:168]]
        return jnp.concatenate([both[:, 0].reshape(64, LANES), both[:, 1].reshape(64, LANES)] + edges, 0)

    w_sum = by_rows(wide[:, 0:128]) * radial
    w_dif = by_rows(wide[:, 128:256]) * radial
    upper = total[0:128].reshape(8, 2, 8, LANES)
    lower = total[128:256].reshape(8, 2, 8, LANES)
    cc, cs = upper[:, 0].reshape(64, LANES), upper[:, 1].reshape(64, LANES)
    sc, ss = lower[:, 0].reshape(64, LANES), lower[:, 1].reshape(64, LANES)
    zero = jnp.zeros((8, LANES), f32)
    v_cos = jnp.concatenate([cc - ss, cc + ss, total[256:264], total[272:280], total[288:296]], 0)
    v_sin = jnp.concatenate([sc + cs, sc - cs, total[264:272], total[280:288], zero], 0)
    g_cos = w_sum * v_cos + w_dif * pltpu.roll(v_sin, 64, 1)
    g_sin = w_sum * v_sin - w_dif * pltpu.roll(v_cos, 64, 1)
    cp, cm, sp, sm = g_cos[0:64], g_cos[64:128], g_sin[0:64], g_sin[64:128]

    def pair_up(left, right):
        both = [left.reshape(8, 1, 8, LANES), right.reshape(8, 1, 8, LANES)]
        return jnp.concatenate(both, 1).reshape(128, LANES)

    rows = [pair_up(cp + cm, sp - sm), pair_up(sp + sm, cm - cp), g_cos[128:136], g_sin[128:136]]
    rows += [g_cos[136:144], g_sin[136:144], g_cos[144:152], jnp.zeros((88, LANES), f32)]
    full = jnp.concatenate(rows, 0)
    gt_scr[0:128, :] = full.T.astype(bf16)

    lane = iota((8, LANES), 1)
    cell = (lane // 16 + 1) * (lane // 16 + 1) + (lane % 8 + 1) * (lane % 8 + 1)
    edge = jnp.where(lane < 32, (lane % 8 + 1) * (lane % 8 + 1), 0)
    own = exact_dot(choose(group, GROUP), weights[...], 1, 1)
    flat = radial_sum(
        jnp.concatenate([cell, edge], 1).astype(f32), lambda b: own[:, b : b + 1]
    ) * scaling
    count0 = jnp.broadcast_to(counts[8:9, 0:128], (8, LANES))
    count1 = jnp.broadcast_to(counts[8:9, 128:256], (8, LANES))
    left = (lane // 8) % 2 == 0
    sigma = jnp.where(left, 1.0, -1.0).astype(f32)

    def swap(value):
        return jnp.where(left, pltpu.roll(value, LANES - 8, 1), pltpu.roll(value, 8, 1))

    other = swap(count0)
    x, y, rest = total[304:312], swap(total[312:320]), total[320:328]
    plus = (x - sigma * y) * flat[:, 0:128] * jnp.where(left, count0, other)
    less = (y + sigma * x) * flat[:, 0:128] * jnp.where(left, other, count0)
    rest = rest * flat[:, 128:256] * (count1 + pltpu.roll(count1, 8, 1))
    low = jnp.concatenate([plus + sigma * less, swap(less - sigma * plus), rest], 1)
    gt_scr[128:144, :] = jnp.concatenate([low, jnp.zeros_like(low)], 0).astype(bf16)


def back_kernel(ka_split, scaling, sub, weights, z, *refs):
    basis, payload, out, gt_scr = refs[:PARTS], refs[PARTS:-2], refs[-2], refs[-1]
    width = out.shape[2]
    filter_rows(payload, weights, lax.axis_index("ka") // ka_split, scaling, gt_scr)
    for j, piece in enumerate(basis):
        size = piece.shape[1]
        product = jnp.dot(gt_scr[:, 0:ROWS], piece[...], preferred_element_type=f32)
        for start in range(0, size, sub):
            place = j * size + start
            message = product[128:136, start : start + sub]
            for m in range(16):
                part = product[8 * m : 8 * m + 8, start : start + sub]
                message = message + z[m : m + 1, place : place + sub] * part
            offset = place % width
            out[place // width, :, offset : offset + sub] = message.astype(bf16)


def update_kernel(sub, message, feat, gain, up, down, out):
    width = feat.shape[1]
    eye = iota((64, 64), 0) == iota((64, 64), 1)
    column = jnp.sum(jnp.where(eye, jnp.broadcast_to(gain[...], (64, 64)), 0.0), axis=1, keepdims=True)
    for start in range(0, width, sub):
        part = pl.ds(start, sub)
        value = message[:, :, part].astype(f32).reshape(64, sub)
        mean_sq = jnp.mean(value * value, axis=0, keepdims=True)
        normed = (value * lax.rsqrt(mean_sq + 1e-06) * column).astype(bf16)
        pre = lax.dot_general(up[...], normed, (((0,), (0,)), ((), ())), preferred_element_type=f32)
        half = 0.5 * pre
        hidden = (half + half * jnp.tanh(half)).astype(bf16)
        update = jnp.dot(down[...], hidden, preferred_element_type=f32)
        out[:, part] = (feat[:, part].astype(f32) + update).astype(bf16)


def body(
    positions,
    features,
    species,
    miller,
    species_table,
    filter_weight,
    norm_gain,
    up_weight,
    down_weight,
):
    atoms_here = features.shape[1]
    channels = features.shape[0]
    n_atom = lax.axis_size("atom")
    n_ka = lax.axis_size("ka")
    ka_split = n_ka // (channels // GROUP)
    local_count = atoms_here // n_ka
    scaling = 1.0 / math.sqrt(atoms_here * n_atom * K)
    params = pltpu.CompilerParams(vmem_limit_bytes=24 * 1024 * 1024)

    blocks = n_ka // n_atom
    near = blocks // 2
    flips = [
        [near * a + j for j in range(near)] + [n_ka - 1 - near * a - j for j in range(blocks - near)]
        for a in range(n_atom)
    ]
    millers = []
    for j in range(blocks):
        pairs = []
        for a in range(n_atom):
            for b in range(n_ka):
                pairs.append((a * n_ka + (b ^ flips[a][j]), a * n_ka + b))
        millers.append(lax.ppermute(miller, ("atom", "ka"), pairs))

    whole = pl.BlockSpec(memory_space=pltpu.VMEM)
    hbm = pl.BlockSpec(memory_space=pltpu.HBM)
    hbm = pl.BlockSpec(memory_space=pltpu.HBM)
    z, acc, local_features, *basis = pl.pallas_call(
        functools.partial(factor_kernel, ka_split),
        in_specs=[hbm] * 4,
        out_specs=[whole] * (3 + PARTS),
        out_shape=[
            jax.ShapeDtypeStruct((16, atoms_here), f32),
            jax.ShapeDtypeStruct((ROWS, 144), f32),
            jax.ShapeDtypeStruct((channels, local_count), bf16),
        ]
        + [jax.ShapeDtypeStruct((ROWS, atoms_here // PARTS), bf16)] * PARTS,
        scratch_shapes=[
            pltpu.VMEM((3, atoms_here), f32),
            pltpu.VMEM((16, atoms_here), bf16),
            pltpu.VMEM((1, atoms_here), jnp.int32),
            pltpu.VMEM((NSPEC, channels), f32),
            pltpu.VMEM((144, atoms_here), bf16),
            pltpu.VMEM((LANES, LANES), f32),
            pltpu.VMEM((LANES, LANES), f32),
            pltpu.VMEM((LANES, LANES), f32),
            pltpu.SemaphoreType.DMA((2 + 3 * PARTS,)),
        ],
        compiler_params=params,
        cost_estimate=pl.CostEstimate(flops=5 * 10**9, bytes_accessed=14 * 10**6, transcendentals=0),
        name="factors",
    )(
        pltpu.with_memory_space_constraint(positions, pltpu.HBM),
        pltpu.with_memory_space_constraint(features, pltpu.HBM),
        pltpu.with_memory_space_constraint(species.reshape(1, atoms_here), pltpu.HBM),
        pltpu.with_memory_space_constraint(species_table.T, pltpu.HBM),
    )

    payload = pl.pallas_call(
        pack_kernel,
        in_specs=[whole] * (1 + blocks),
        out_specs=whole,
        out_shape=jax.ShapeDtypeStruct((PAYLOAD, LANES), bf16),
        compiler_params=params,
        name="pack",
    )(acc, *millers)
    if n_atom == 4:
        across = lax.ppermute(payload, "atom", [(a, a ^ 2) for a in range(4)])
        payload = pl.pallas_call(
            fold_kernel,
            in_specs=[whole] * 2,
            out_specs=whole,
            out_shape=jax.ShapeDtypeStruct((PAYLOAD, LANES), bf16),
            compiler_params=params,
            name="fold",
        )(payload, across)
        gathered = [payload, lax.ppermute(payload, "atom", [(a, a ^ 1) for a in range(4)])]
    else:
        gathered = list(lax.all_gather(payload, "atom"))

    message = pl.pallas_call(
        functools.partial(back_kernel, ka_split, scaling, min(512, local_count)),
        in_specs=[whole] * (2 + PARTS + len(gathered)),
        out_specs=whole,
        out_shape=jax.ShapeDtypeStruct((n_ka, GROUP, local_count), bf16),
        scratch_shapes=[pltpu.VMEM((144, 384), bf16)],
        compiler_params=params,
        cost_estimate=pl.CostEstimate(flops=5 * 10**9, bytes_accessed=11 * 10**6, transcendentals=0),
        name="back",
    )(filter_weight.T, z, *basis, *gathered)

    groups = None
    if ka_split > 1:
        message = message.reshape(n_ka // ka_split, ka_split, GROUP, local_count)
        message = lax.dynamic_index_in_dim(message, lax.axis_index("ka") % ka_split, 1, False)
        groups = [[g * ka_split + s for g in range(n_ka // ka_split)] for s in range(ka_split)]
    message = lax.all_to_all(message, "ka", 0, 0, axis_index_groups=groups, tiled=True)

    return pl.pallas_call(
        functools.partial(update_kernel, local_count),
        in_specs=[whole] * 5,
        out_specs=whole,
        out_shape=jax.ShapeDtypeStruct((channels, local_count), bf16),
        compiler_params=params,
        name="update",
    )(message, local_features, norm_gain.reshape(1, channels), up_weight.T, down_weight)


def solution(mesh):
    in_specs = (P(None, "atom"), P(None, "atom"), P("atom"), P(None, "ka"), P(), P(), P(), P(), P())
    out_specs = P(None, ("atom", "ka"))
    return jax.shard_map(body, mesh=mesh, in_specs=in_specs, out_specs=out_specs, check_vma=False)
```

```python
import functools
import math

import jax
import jax.numpy as jnp
import numpy as np
from jax import lax
from jax.experimental import pallas as pl
from jax.experimental.pallas import tpu as pltpu
from jax.sharding import PartitionSpec as P

K = 4096
NRBF = 16
NSPEC = 8
MAXM = 8
GROUP = 8
ROWS = 304
CHUNK = 1024
SPAN = 4
PARTS = 4
LANES = 128
PAYLOAD = 400
k_cutoff = 14.0
f32 = jnp.float32
bf16 = jnp.bfloat16


def fit(function, terms, odd):
    nodes = np.cos((np.arange(64) + 0.5) * np.pi / 64) * 0.5
    nodes = np.abs(nodes)
    target = function(2.0 * np.pi * nodes)
    if odd:
        target = target / nodes
    series = np.polynomial.chebyshev.Chebyshev.fit(nodes * nodes, target, terms - 1, domain=[0, 0.25])
    return [float(v) for v in series.convert(kind=np.polynomial.Polynomial).coef]


SIN = fit(np.sin, 7, True)
COS = fit(np.cos, 7, False)


def horner(coefs, x):
    total = coefs[-1] * x + coefs[-2]
    for value in coefs[-3::-1]:
        total = total * x + value
    return total


def first_harmonic(x):
    turns = x - jnp.floor(x + 0.5)
    square = turns * turns
    return horner(COS, square), turns * horner(SIN, square)


def iota(shape, axis):
    return lax.broadcasted_iota(jnp.int32, shape, axis)


def waves_to(scr, x):
    cosine, sine = first_harmonic(x)
    twice = cosine + cosine
    lower_c, lower_s = jnp.ones_like(cosine), jnp.zeros_like(sine)
    upper_c, upper_s = cosine, sine
    for m in range(MAXM):
        scr[8 * m : 8 * m + 8, :] = upper_c
        scr[64 + 8 * m : 72 + 8 * m, :] = upper_s
        lower_c, upper_c = upper_c, twice * upper_c - lower_c
        lower_s, upper_s = upper_s, twice * upper_s - lower_s


def spread(scr, row):
    pieces = [jnp.broadcast_to(scr[row + k : row + k + 1, :], (8, LANES)) for k in range(SPAN)]
    return jnp.concatenate(pieces, 1)


def comb(scr, row):
    return jnp.concatenate([scr[pl.ds(row + k, 8, stride=8), :] for k in range(SPAN)], 1)


def harmonics_chunk(pos, start, w0, w1, w2):
    for axis, scr in enumerate((w0, w1, w2)):
        rows = [pos[axis : axis + 1, pl.ds(start + LANES * k, LANES)] for k in range(8)]
        waves_to(scr, jnp.concatenate(rows, 0))


def factor_chunk(feat, species, table, odd, start, here, k, full, terms, z_out, w0, w1, w2):
    part = pl.ds(start, LANES * SPAN)
    local = pl.ds(here, LANES * SPAN)
    c1 = comb(w1, k)
    s1 = comb(w1, 64 + k)
    for m in range(16):
        left = spread(w0, 8 * m + k)
        full[16 * m : 16 * m + 16, local] = jnp.concatenate([left * c1, left * s1], 0).astype(bf16)
    full[256:272, local] = jnp.concatenate([comb(w0, k), comb(w0, 64 + k)], 0).astype(bf16)
    full[272:288, local] = jnp.concatenate([c1, s1], 0).astype(bf16)
    z_out[0:8, part] = comb(w2, k)
    z_out[8:16, part] = comb(w2, 64 + k)
    kinds = jnp.broadcast_to(species[0:1, part], (8, LANES * SPAN))
    embedded = table[0]
    for s in range(1, NSPEC):
        embedded = jnp.where(kinds == s, table[s], embedded)
    wide = feat[:, part].astype(f32)
    own = jnp.where(odd, wide[8:16], wide[0:8])
    source = (own + embedded).astype(bf16).astype(f32)
    for m in range(0, 16, 2):
        pair = [source * spread(w2, 8 * m + k), source * spread(w2, 8 * m + 8 + k)]
        terms[8 * m : 8 * m + 16, part] = jnp.concatenate(pair, 0).astype(bf16)
    terms[128:144, part] = jnp.concatenate([source, jnp.zeros_like(source)], 0).astype(bf16)


def choose(group, count):
    return (iota((count, 64), 1) == group * GROUP + iota((count, 64), 0) % GROUP).astype(f32)


def exact_dot(left, right, left_dim, right_dim):
    return lax.dot_general(
        left, right, (((left_dim,), (right_dim,)), ((), ())),
        precision=lax.Precision.HIGHEST, preferred_element_type=f32,
    )


def factor_kernel(ka_split, pos_hbm, feat_hbm, species_hbm, table_hbm, z_out, acc, local_out, *refs):
    basis = refs[:PARTS]
    pos, feat, species, table, terms, w0, w1, w2, sems = refs[PARTS:]
    me = lax.axis_index("ka")
    group = me // ka_split
    atoms, width = feat.shape[1], local_out.shape[1]
    first = pl.multiple_of((group // 2) * 16, 16)
    size = atoms // PARTS
    copies = [pltpu.make_async_copy(table_hbm, table, sems.at[0])]
    waits = []
    for p in range(PARTS):
        cut = pl.ds(p * size, size)
        waits.append(
            [
                pltpu.make_async_copy(pos_hbm.at[:, cut], pos.at[:, cut], sems.at[3 * p + 2]),
                pltpu.make_async_copy(species_hbm.at[:, cut], species.at[:, cut], sems.at[3 * p + 3]),
                pltpu.make_async_copy(
                    feat_hbm.at[pl.ds(first, 16), cut], feat.at[:, cut], sems.at[3 * p + 4]
                ),
            ]
        )
        copies += waits[p]
    keep = pltpu.make_async_copy(
        feat_hbm.at[:, pl.ds(pl.multiple_of(me * width, width), width)], local_out, sems.at[1]
    )
    for copy in copies + [keep]:
        copy.start()
    for full in basis:
        full[288:304, :] = (iota((16, size), 0) == 0).astype(f32).astype(bf16)
    odd = (group % 2) == 1
    copies[0].wait()
    own = exact_dot(choose(group, GROUP), table[...], 1, 1)
    columns = [jnp.broadcast_to(own[:, s : s + 1], (8, LANES * SPAN)) for s in range(NSPEC)]

    def step(p, j):
        here = pl.multiple_of(j * CHUNK, CHUNK)
        harmonics_chunk(pos, p * size + here, w0, w1, w2)
        for k in range(0, 8, SPAN):
            factor_chunk(
                feat, species, columns, odd, p * size + here + k * LANES, here + k * LANES, k,
                basis[p], terms, z_out, w0, w1, w2,
            )

    for p in range(PARTS):
        for copy in waits[p]:
            copy.wait()
        lax.fori_loop(0, size // CHUNK, lambda j, carry: step(p, j), None, unroll=4)
    total = None
    for p, full in enumerate(basis):
        piece = lax.dot_general(
            full[...], terms[:, p * size : (p + 1) * size],
            (((1,), (1,)), ((), ())), preferred_element_type=f32,
        )
        total = piece if total is None else total + piece
    acc[...] = total
    keep.wait()


def pack_kernel(acc, own, *refs):
    millers, out = refs[:-1], refs[-1]
    out[0:ROWS, :] = acc[:, 0:LANES].astype(bf16)
    tail = jnp.concatenate([acc[:, 128:144], jnp.zeros((ROWS, 112), f32)], 1)
    tail = jnp.concatenate([tail, jnp.zeros((384 - ROWS, LANES), f32)], 0)
    flat = tail.T
    zero = jnp.zeros((GROUP, LANES), f32)
    pieces = [flat[0:8, 0:128], flat[0:8, 128:256], flat[0:8, 256:384], zero]
    out[304:336, :] = jnp.concatenate(pieces, 0).astype(bf16)
    counts = jnp.zeros((32, 256), f32)
    at_first = lax.axis_index("atom") == 0
    for j, ref in enumerate(millers[::-1]):
        value = jnp.where(at_first, own[...], ref[...]) if j == 0 else ref[...]
        m0, m1, m2 = value[0:1, :], value[1:2, :], value[2:3, :]
        sign = jnp.where(17 * m0 + m1 < 0, -1, 1)
        m0, m1, m2 = m0 * sign, m1 * sign, m2 * sign
        inner = jnp.where(
            m1 > 0, 16 * m0 + m1 - 17, jnp.where(m1 < 0, 16 * m0 - m1 - 9, 127 + m0)
        )
        row = jnp.where(m0 > 0, inner, jnp.where(m1 > 0, 143 + m1, 160))
        column = jnp.where(row == 160, jnp.abs(m2), m2) + MAXM
        size = row.shape[1]
        row_hot = (iota((256, size), 0) == row).astype(f32).astype(bf16)
        column_hot = (iota((32, size), 0) == column).astype(f32).astype(bf16)
        counts = counts + lax.dot_general(
            column_hot, row_hot, (((1,), (1,)), ((), ())), preferred_element_type=f32
        )
    out[336:368, :] = counts[:, 0:128].astype(bf16)
    out[368:400, :] = counts[:, 128:256].astype(bf16)


def fold_kernel(left, right, out):
    out[...] = (left[...].astype(f32) + right[...].astype(f32)).astype(bf16)


def radial_sum(square, weight_of):
    magnitude = jnp.sqrt(square)
    total = None
    for b in range(NRBF):
        offset = (magnitude - b * (k_cutoff / (NRBF - 1))) * (NRBF / k_cutoff)
        term = weight_of(b) * jnp.exp(-(offset * offset))
        total = term if total is None else total + term
    return total


def tables_kernel(ka_split, scaling, weights, token, radial_out, flat_out):
    del token
    group = lax.axis_index("ka") // ka_split
    across = exact_dot(weights[...], choose(group, LANES), 1, 1)
    lane = iota((88, LANES), 1)
    row = iota((88, LANES), 0)
    third = (lane % 64) // 8 + 1
    first = row // 8 + 1
    second = row % 8 + 1
    planar = jnp.where(
        row < 64,
        first * first + second * second,
        jnp.where(row < 80, second * second, 0),
    )
    radial = radial_sum((planar + third * third).astype(f32), lambda b: across[b : b + 1, :]) * scaling
    radial = jnp.concatenate([radial[0:64], radial], 0)

    radial_out[...] = radial

    lane = iota((8, LANES), 1)
    cell = (lane // 16 + 1) * (lane // 16 + 1) + (lane % 8 + 1) * (lane % 8 + 1)
    edge = jnp.where(lane < 32, (lane % 8 + 1) * (lane % 8 + 1), 0)
    own = exact_dot(choose(group, GROUP), weights[...], 1, 1)
    flat_out[...] = radial_sum(
        jnp.concatenate([cell, edge], 1).astype(f32), lambda b: own[:, b : b + 1]
    ) * scaling


def filter_rows(payload, radial, flat, gt_scr):
    total = payload[0][...].astype(f32)
    for part in payload[1:]:
        total = total + part[...].astype(f32)
    counts = jnp.concatenate([total[336:368], total[368:400]], 1)
    lane = iota((32, LANES), 1)
    index = iota((32, LANES), 0) - MAXM
    height = (lane % 64) // 8 + 1
    plus = jnp.where(jnp.abs(index) == height, 1.0, 0.0)
    minus = jnp.where(index == height, 1.0, jnp.where(index == -height, -1.0, 0.0))
    minus = jnp.where(lane < 64, -minus, minus)
    spread = jnp.concatenate([plus, minus], 1).astype(f32)
    high = jnp.floor(counts * (1.0 / 64.0))
    split = jnp.concatenate([high, counts - 64.0 * high], 0).astype(bf16)
    scale = jnp.concatenate([64.0 * spread, spread], 0).astype(bf16)
    wide = lax.dot_general(split, scale, (((0,), (0,)), ((), ())), preferred_element_type=f32)
    def by_rows(value):
        both = value[0:128].reshape(8, 2, 8, LANES)
        edges = [value[128:136], value[144:152], value[160:168]]
        return jnp.concatenate([both[:, 0].reshape(64, LANES), both[:, 1].reshape(64, LANES)] + edges, 0)

    w_sum = by_rows(wide[:, 0:128]) * radial[...]
    w_dif = by_rows(wide[:, 128:256]) * radial[...]
    upper = total[0:128].reshape(8, 2, 8, LANES)
    lower = total[128:256].reshape(8, 2, 8, LANES)
    cc, cs = upper[:, 0].reshape(64, LANES), upper[:, 1].reshape(64, LANES)
    sc, ss = lower[:, 0].reshape(64, LANES), lower[:, 1].reshape(64, LANES)
    zero = jnp.zeros((8, LANES), f32)
    v_cos = jnp.concatenate([cc - ss, cc + ss, total[256:264], total[272:280], total[288:296]], 0)
    v_sin = jnp.concatenate([sc + cs, sc - cs, total[264:272], total[280:288], zero], 0)
    g_cos = w_sum * v_cos + w_dif * pltpu.roll(v_sin, 64, 1)
    g_sin = w_sum * v_sin - w_dif * pltpu.roll(v_cos, 64, 1)
    cp, cm, sp, sm = g_cos[0:64], g_cos[64:128], g_sin[0:64], g_sin[64:128]

    def pair_up(left, right):
        both = [left.reshape(8, 1, 8, LANES), right.reshape(8, 1, 8, LANES)]
        return jnp.concatenate(both, 1).reshape(128, LANES)

    rows = [pair_up(cp + cm, sp - sm), pair_up(sp + sm, cm - cp), g_cos[128:136], g_sin[128:136]]
    rows += [g_cos[136:144], g_sin[136:144], g_cos[144:152], jnp.zeros((88, LANES), f32)]
    full = jnp.concatenate(rows, 0)
    gt_scr[0:128, :] = full.T.astype(bf16)

    lane = iota((8, LANES), 1)
    count0 = jnp.broadcast_to(counts[8:9, 0:128], (8, LANES))
    count1 = jnp.broadcast_to(counts[8:9, 128:256], (8, LANES))
    left = (lane // 8) % 2 == 0
    sigma = jnp.where(left, 1.0, -1.0).astype(f32)

    def swap(value):
        return jnp.where(left, pltpu.roll(value, LANES - 8, 1), pltpu.roll(value, 8, 1))

    other = swap(count0)
    x, y, rest = total[304:312], swap(total[312:320]), total[320:328]
    plus = (x - sigma * y) * flat[:, 0:128] * jnp.where(left, count0, other)
    less = (y + sigma * x) * flat[:, 0:128] * jnp.where(left, other, count0)
    rest = rest * flat[:, 128:256] * (count1 + pltpu.roll(count1, 8, 1))
    low = jnp.concatenate([plus + sigma * less, swap(less - sigma * plus), rest], 1)
    gt_scr[128:144, :] = jnp.concatenate([low, jnp.zeros_like(low)], 0).astype(bf16)


def back_kernel(sub, radial, flat, z, *refs):
    basis, payload, out, gt_scr = refs[:PARTS], refs[PARTS:-2], refs[-2], refs[-1]
    width = out.shape[2]
    filter_rows(payload, radial, flat, gt_scr)
    for j, piece in enumerate(basis):
        size = piece.shape[1]
        product = jnp.dot(gt_scr[:, 0:ROWS], piece[...], preferred_element_type=f32)
        for start in range(0, size, sub):
            place = j * size + start
            message = product[128:136, start : start + sub]
            for m in range(16):
                part = product[8 * m : 8 * m + 8, start : start + sub]
                message = message + z[m : m + 1, place : place + sub] * part
            offset = place % width
            out[place // width, :, offset : offset + sub] = message.astype(bf16)


def update_kernel(sub, message, feat, gain, up, down, out):
    width = feat.shape[1]
    eye = iota((64, 64), 0) == iota((64, 64), 1)
    column = jnp.sum(jnp.where(eye, jnp.broadcast_to(gain[...], (64, 64)), 0.0), axis=1, keepdims=True)
    for start in range(0, width, sub):
        part = pl.ds(start, sub)
        value = message[:, :, part].astype(f32).reshape(64, sub)
        mean_sq = jnp.mean(value * value, axis=0, keepdims=True)
        normed = (value * lax.rsqrt(mean_sq + 1e-06) * column).astype(bf16)
        pre = lax.dot_general(up[...], normed, (((0,), (0,)), ((), ())), preferred_element_type=f32)
        half = 0.5 * pre
        hidden = (half + half * jnp.tanh(half)).astype(bf16)
        update = jnp.dot(down[...], hidden, preferred_element_type=f32)
        out[:, part] = (feat[:, part].astype(f32) + update).astype(bf16)


def body(
    positions,
    features,
    species,
    miller,
    species_table,
    filter_weight,
    norm_gain,
    up_weight,
    down_weight,
):
    atoms_here = features.shape[1]
    channels = features.shape[0]
    n_atom = lax.axis_size("atom")
    n_ka = lax.axis_size("ka")
    ka_split = n_ka // (channels // GROUP)
    local_count = atoms_here // n_ka
    scaling = 1.0 / math.sqrt(atoms_here * n_atom * K)
    params = pltpu.CompilerParams(vmem_limit_bytes=24 * 1024 * 1024)

    blocks = n_ka // n_atom
    near = blocks // 2
    flips = [
        [near * a + j for j in range(near)] + [n_ka - 1 - near * a - j for j in range(blocks - near)]
        for a in range(n_atom)
    ]
    millers = []
    for j in range(blocks):
        pairs = []
        for a in range(n_atom):
            for b in range(n_ka):
                if flips[a][j]:
                    pairs.append((a * n_ka + (b ^ flips[a][j]), a * n_ka + b))
        millers.append(lax.ppermute(miller, ("atom", "ka"), pairs))

    whole = pl.BlockSpec(memory_space=pltpu.VMEM)
    hbm = pl.BlockSpec(memory_space=pltpu.HBM)
    hbm = pl.BlockSpec(memory_space=pltpu.HBM)
    z, acc, local_features, *basis = pl.pallas_call(
        functools.partial(factor_kernel, ka_split),
        in_specs=[hbm] * 4,
        out_specs=[whole] * (3 + PARTS),
        out_shape=[
            jax.ShapeDtypeStruct((16, atoms_here), f32),
            jax.ShapeDtypeStruct((ROWS, 144), f32),
            jax.ShapeDtypeStruct((channels, local_count), bf16),
        ]
        + [jax.ShapeDtypeStruct((ROWS, atoms_here // PARTS), bf16)] * PARTS,
        scratch_shapes=[
            pltpu.VMEM((3, atoms_here), f32),
            pltpu.VMEM((16, atoms_here), bf16),
            pltpu.VMEM((1, atoms_here), jnp.int32),
            pltpu.VMEM((NSPEC, channels), f32),
            pltpu.VMEM((144, atoms_here), bf16),
            pltpu.VMEM((LANES, LANES), f32),
            pltpu.VMEM((LANES, LANES), f32),
            pltpu.VMEM((LANES, LANES), f32),
            pltpu.SemaphoreType.DMA((2 + 3 * PARTS,)),
        ],
        compiler_params=params,
        cost_estimate=pl.CostEstimate(flops=5 * 10**9, bytes_accessed=14 * 10**6, transcendentals=0),
        name="factors",
    )(
        pltpu.with_memory_space_constraint(positions, pltpu.HBM),
        pltpu.with_memory_space_constraint(features, pltpu.HBM),
        pltpu.with_memory_space_constraint(species.reshape(1, atoms_here), pltpu.HBM),
        pltpu.with_memory_space_constraint(species_table.T, pltpu.HBM),
    )

    payload = pl.pallas_call(
        pack_kernel,
        in_specs=[whole] * (2 + blocks),
        out_specs=whole,
        out_shape=jax.ShapeDtypeStruct((PAYLOAD, LANES), bf16),
        compiler_params=params,
        name="pack",
    )(acc, miller, *millers[::-1])
    radial, flat = pl.pallas_call(
        functools.partial(tables_kernel, ka_split, scaling),
        in_specs=[whole, pl.BlockSpec(memory_space=pl.ANY)],
        out_specs=[whole, whole],
        out_shape=[
            jax.ShapeDtypeStruct((152, LANES), f32),
            jax.ShapeDtypeStruct((GROUP, 2 * LANES), f32),
        ],
        compiler_params=params,
        cost_estimate=pl.CostEstimate(flops=10**9, bytes_accessed=10**6, transcendentals=10**6),
        name="tables",
    )(filter_weight.T, payload)
    if n_atom == 4:
        across = lax.ppermute(payload, "atom", [(a, a ^ 2) for a in range(4)])
        payload = pl.pallas_call(
            fold_kernel,
            in_specs=[whole] * 2,
            out_specs=whole,
            out_shape=jax.ShapeDtypeStruct((PAYLOAD, LANES), bf16),
            compiler_params=params,
            name="fold",
        )(payload, across)
        gathered = [payload, lax.ppermute(payload, "atom", [(a, a ^ 1) for a in range(4)])]
    else:
        gathered = list(lax.all_gather(payload, "atom"))

    message = pl.pallas_call(
        functools.partial(back_kernel, min(512, local_count)),
        in_specs=[whole] * (3 + PARTS + len(gathered)),
        out_specs=whole,
        out_shape=jax.ShapeDtypeStruct((n_ka, GROUP, local_count), bf16),
        scratch_shapes=[pltpu.VMEM((144, 384), bf16)],
        compiler_params=params,
        cost_estimate=pl.CostEstimate(flops=5 * 10**9, bytes_accessed=11 * 10**6, transcendentals=0),
        name="back",
    )(radial, flat, z, *basis, *gathered)

    groups = None
    if ka_split > 1:
        message = message.reshape(n_ka // ka_split, ka_split, GROUP, local_count)
        message = lax.dynamic_index_in_dim(message, lax.axis_index("ka") % ka_split, 1, False)
        groups = [[g * ka_split + s for g in range(n_ka // ka_split)] for s in range(ka_split)]
    message = lax.all_to_all(message, "ka", 0, 0, axis_index_groups=groups, tiled=True)

    return pl.pallas_call(
        functools.partial(update_kernel, local_count),
        in_specs=[whole] * 5,
        out_specs=whole,
        out_shape=jax.ShapeDtypeStruct((channels, local_count), bf16),
        compiler_params=params,
        name="update",
    )(message, local_features, norm_gain.reshape(1, channels), up_weight.T, down_weight)


def solution(mesh):
    in_specs = (P(None, "atom"), P(None, "atom"), P("atom"), P(None, "ka"), P(), P(), P(), P(), P())
    out_specs = P(None, ("atom", "ka"))
    return jax.shard_map(body, mesh=mesh, in_specs=in_specs, out_specs=out_specs, check_vma=False)
```

```python
import functools
import math

import jax
import jax.numpy as jnp
import numpy as np
from jax import lax
from jax.experimental import pallas as pl
from jax.experimental.pallas import tpu as pltpu
from jax.sharding import PartitionSpec as P

K = 4096
NRBF = 16
NSPEC = 8
MAXM = 8
GROUP = 8
ROWS = 304
CHUNK = 1024
SPAN = 4
PARTS = 4
LANES = 128
PAYLOAD = 400
k_cutoff = 14.0
FAR = (6, 3, 4, 5)
NEAR = (1, 2, 1, 2)
f32 = jnp.float32
bf16 = jnp.bfloat16


def fit(function, terms, odd):
    nodes = np.cos((np.arange(64) + 0.5) * np.pi / 64) * 0.5
    nodes = np.abs(nodes)
    target = function(2.0 * np.pi * nodes)
    if odd:
        target = target / nodes
    series = np.polynomial.chebyshev.Chebyshev.fit(nodes * nodes, target, terms - 1, domain=[0, 0.25])
    return [float(v) for v in series.convert(kind=np.polynomial.Polynomial).coef]


SIN = fit(np.sin, 7, True)
COS = fit(np.cos, 7, False)


def horner(coefs, x):
    total = coefs[-1] * x + coefs[-2]
    for value in coefs[-3::-1]:
        total = total * x + value
    return total


def first_harmonic(x):
    turns = x - jnp.floor(x + 0.5)
    square = turns * turns
    return horner(COS, square), turns * horner(SIN, square)


def iota(shape, axis):
    return lax.broadcasted_iota(jnp.int32, shape, axis)


def waves_to(scr, x):
    cosine, sine = first_harmonic(x)
    twice = cosine + cosine
    lower_c, lower_s = jnp.ones_like(cosine), jnp.zeros_like(sine)
    upper_c, upper_s = cosine, sine
    for m in range(MAXM):
        scr[8 * m : 8 * m + 8, :] = upper_c
        scr[64 + 8 * m : 72 + 8 * m, :] = upper_s
        lower_c, upper_c = upper_c, twice * upper_c - lower_c
        lower_s, upper_s = upper_s, twice * upper_s - lower_s


def spread(scr, row):
    pieces = [jnp.broadcast_to(scr[row + k : row + k + 1, :], (8, LANES)) for k in range(SPAN)]
    return jnp.concatenate(pieces, 1)


def comb(scr, row):
    return jnp.concatenate([scr[pl.ds(row + k, 8, stride=8), :] for k in range(SPAN)], 1)


def harmonics_chunk(pos, start, w0, w1, w2):
    for axis, scr in enumerate((w0, w1, w2)):
        rows = [pos[axis : axis + 1, pl.ds(start + LANES * k, LANES)] for k in range(8)]
        waves_to(scr, jnp.concatenate(rows, 0))


def factor_chunk(feat, species, table, odd, start, here, k, full, terms, z_out, w0, w1, w2):
    part = pl.ds(start, LANES * SPAN)
    local = pl.ds(here, LANES * SPAN)
    c1 = comb(w1, k)
    s1 = comb(w1, 64 + k)
    for m in range(16):
        left = spread(w0, 8 * m + k)
        full[16 * m : 16 * m + 16, local] = jnp.concatenate([left * c1, left * s1], 0).astype(bf16)
    full[256:272, local] = jnp.concatenate([comb(w0, k), comb(w0, 64 + k)], 0).astype(bf16)
    full[272:288, local] = jnp.concatenate([c1, s1], 0).astype(bf16)
    z_out[0:8, part] = comb(w2, k)
    z_out[8:16, part] = comb(w2, 64 + k)
    kinds = jnp.broadcast_to(species[0:1, part], (8, LANES * SPAN))
    embedded = table[0]
    for s in range(1, NSPEC):
        embedded = jnp.where(kinds == s, table[s], embedded)
    wide = feat[:, part].astype(f32)
    own = jnp.where(odd, wide[8:16], wide[0:8])
    source = (own + embedded).astype(bf16).astype(f32)
    for m in range(0, 16, 2):
        pair = [source * spread(w2, 8 * m + k), source * spread(w2, 8 * m + 8 + k)]
        terms[8 * m : 8 * m + 16, part] = jnp.concatenate(pair, 0).astype(bf16)
    terms[128:144, part] = jnp.concatenate([source, jnp.zeros_like(source)], 0).astype(bf16)


def choose(group, count):
    return (iota((count, 64), 1) == group * GROUP + iota((count, 64), 0) % GROUP).astype(f32)


def exact_dot(left, right, left_dim, right_dim):
    return lax.dot_general(
        left, right, (((left_dim,), (right_dim,)), ((), ())),
        precision=lax.Precision.HIGHEST, preferred_element_type=f32,
    )


def factor_kernel(ka_split, pos_hbm, feat_hbm, species_hbm, table_hbm, z_out, acc, local_out, *refs):
    basis = refs[:PARTS]
    pos, feat, species, table, terms, w0, w1, w2, sems = refs[PARTS:]
    me = lax.axis_index("ka")
    group = me // ka_split
    atoms, width = feat.shape[1], local_out.shape[1]
    first = pl.multiple_of((group // 2) * 16, 16)
    size = atoms // PARTS
    copies = [pltpu.make_async_copy(table_hbm, table, sems.at[0])]
    waits = []
    for p in range(PARTS):
        cut = pl.ds(p * size, size)
        waits.append(
            [
                pltpu.make_async_copy(pos_hbm.at[:, cut], pos.at[:, cut], sems.at[3 * p + 2]),
                pltpu.make_async_copy(species_hbm.at[:, cut], species.at[:, cut], sems.at[3 * p + 3]),
                pltpu.make_async_copy(
                    feat_hbm.at[pl.ds(first, 16), cut], feat.at[:, cut], sems.at[3 * p + 4]
                ),
            ]
        )
        copies += waits[p]
    keep = pltpu.make_async_copy(
        feat_hbm.at[:, pl.ds(pl.multiple_of(me * width, width), width)], local_out, sems.at[1]
    )
    for copy in copies + [keep]:
        copy.start()
    for full in basis:
        full[288:304, :] = (iota((16, size), 0) == 0).astype(f32).astype(bf16)
    odd = (group % 2) == 1
    copies[0].wait()
    own = exact_dot(choose(group, GROUP), table[...], 1, 1)
    columns = [jnp.broadcast_to(own[:, s : s + 1], (8, LANES * SPAN)) for s in range(NSPEC)]

    def step(p, j):
        here = pl.multiple_of(j * CHUNK, CHUNK)
        harmonics_chunk(pos, p * size + here, w0, w1, w2)
        for k in range(0, 8, SPAN):
            factor_chunk(
                feat, species, columns, odd, p * size + here + k * LANES, here + k * LANES, k,
                basis[p], terms, z_out, w0, w1, w2,
            )

    for p in range(PARTS):
        for copy in waits[p]:
            copy.wait()
        lax.fori_loop(0, size // CHUNK, lambda j, carry: step(p, j), None, unroll=4)
    total = None
    for p, full in enumerate(basis):
        piece = lax.dot_general(
            full[...], terms[:, p * size : (p + 1) * size],
            (((1,), (1,)), ((), ())), preferred_element_type=f32,
        )
        total = piece if total is None else total + piece
    acc[...] = total
    keep.wait()


def histogram(value):
    m0, m1, m2 = value[0:1, :], value[1:2, :], value[2:3, :]
    sign = jnp.where(17 * m0 + m1 < 0, -1, 1)
    m0, m1, m2 = m0 * sign, m1 * sign, m2 * sign
    inner = jnp.where(
        m1 > 0, 16 * m0 + m1 - 17, jnp.where(m1 < 0, 16 * m0 - m1 - 9, 127 + m0)
    )
    row = jnp.where(m0 > 0, inner, jnp.where(m1 > 0, 143 + m1, 160))
    column = jnp.where(row == 160, jnp.abs(m2), m2) + MAXM
    size = row.shape[1]
    row_hot = (iota((256, size), 0) == row).astype(f32).astype(bf16)
    column_hot = (iota((32, size), 0) == column).astype(f32).astype(bf16)
    return lax.dot_general(
        column_hot, row_hot, (((1,), (1,)), ((), ())), preferred_element_type=f32
    )


def pack_kernel(chained, acc, own, *refs):
    if chained:
        (first,), (out, pair_out) = refs[:1], refs[1:]
        pair_out[0:3, :] = own[...]
        pair_out[3:6, :] = first[...]
        at_start = jnp.where(lax.axis_index("atom") == 0, 1.0, 0.0)
        counts = histogram(first[...]) + at_start * histogram(own[...])
    else:
        millers, out = refs[:-1], refs[-1]
        at_start = lax.axis_index("atom") == 0
        counts = jnp.zeros((32, 256), f32)
        for j, ref in enumerate(millers[::-1]):
            value = jnp.where(at_start, own[...], ref[...]) if j == 0 else ref[...]
            counts = counts + histogram(value)
    out[0:ROWS, :] = acc[:, 0:LANES].astype(bf16)
    tail = jnp.concatenate([acc[:, 128:144], jnp.zeros((ROWS, 112), f32)], 1)
    tail = jnp.concatenate([tail, jnp.zeros((384 - ROWS, LANES), f32)], 0)
    flat = tail.T
    zero = jnp.zeros((GROUP, LANES), f32)
    pieces = [flat[0:8, 0:128], flat[0:8, 128:256], flat[0:8, 256:384], zero]
    out[304:336, :] = jnp.concatenate(pieces, 0).astype(bf16)
    out[336:368, :] = counts[:, 0:128].astype(bf16)
    out[368:400, :] = counts[:, 128:256].astype(bf16)


def fold_kernel(left, right, pair, out):
    out[0:336, :] = (left[0:336, :].astype(f32) + right[0:336, :].astype(f32)).astype(bf16)
    atom = lax.axis_index("atom")
    last = jnp.where(atom // 2 == atom % 2, 1.0, 0.0)
    extra = histogram(pair[0:3, :]) + last * histogram(pair[3:6, :])
    counts = left[336:400, :].astype(f32) + right[336:400, :].astype(f32)
    out[336:400, :] = (counts + jnp.concatenate([extra[:, 0:128], extra[:, 128:256]], 0)).astype(bf16)


def radial_sum(square, weight_of):
    magnitude = jnp.sqrt(square)
    total = None
    for b in range(NRBF):
        offset = (magnitude - b * (k_cutoff / (NRBF - 1))) * (NRBF / k_cutoff)
        term = weight_of(b) * jnp.exp(-(offset * offset))
        total = term if total is None else total + term
    return total


def tables_kernel(ka_split, scaling, weights, token, radial_out, flat_out):
    del token
    group = lax.axis_index("ka") // ka_split
    across = exact_dot(weights[...], choose(group, LANES), 1, 1)
    lane = iota((88, LANES), 1)
    row = iota((88, LANES), 0)
    third = (lane % 64) // 8 + 1
    first = row // 8 + 1
    second = row % 8 + 1
    planar = jnp.where(
        row < 64,
        first * first + second * second,
        jnp.where(row < 80, second * second, 0),
    )
    radial = radial_sum((planar + third * third).astype(f32), lambda b: across[b : b + 1, :]) * scaling
    radial = jnp.concatenate([radial[0:64], radial], 0)

    radial_out[...] = radial

    lane = iota((8, LANES), 1)
    cell = (lane // 16 + 1) * (lane // 16 + 1) + (lane % 8 + 1) * (lane % 8 + 1)
    edge = jnp.where(lane < 32, (lane % 8 + 1) * (lane % 8 + 1), 0)
    own = exact_dot(choose(group, GROUP), weights[...], 1, 1)
    flat_out[...] = radial_sum(
        jnp.concatenate([cell, edge], 1).astype(f32), lambda b: own[:, b : b + 1]
    ) * scaling


def filter_rows(payload, radial, flat, gt_scr):
    total = payload[0][...].astype(f32)
    for part in payload[1:]:
        total = total + part[...].astype(f32)
    counts = jnp.concatenate([total[336:368], total[368:400]], 1)
    lane = iota((32, LANES), 1)
    index = iota((32, LANES), 0) - MAXM
    height = (lane % 64) // 8 + 1
    plus = jnp.where(jnp.abs(index) == height, 1.0, 0.0)
    minus = jnp.where(index == height, 1.0, jnp.where(index == -height, -1.0, 0.0))
    minus = jnp.where(lane < 64, -minus, minus)
    spread = jnp.concatenate([plus, minus], 1).astype(f32)
    high = jnp.floor(counts * (1.0 / 64.0))
    split = jnp.concatenate([high, counts - 64.0 * high], 0).astype(bf16)
    scale = jnp.concatenate([64.0 * spread, spread], 0).astype(bf16)
    wide = lax.dot_general(split, scale, (((0,), (0,)), ((), ())), preferred_element_type=f32)
    def by_rows(value):
        both = value[0:128].reshape(8, 2, 8, LANES)
        edges = [value[128:136], value[144:152], value[160:168]]
        return jnp.concatenate([both[:, 0].reshape(64, LANES), both[:, 1].reshape(64, LANES)] + edges, 0)

    w_sum = by_rows(wide[:, 0:128]) * radial[...]
    w_dif = by_rows(wide[:, 128:256]) * radial[...]
    upper = total[0:128].reshape(8, 2, 8, LANES)
    lower = total[128:256].reshape(8, 2, 8, LANES)
    cc, cs = upper[:, 0].reshape(64, LANES), upper[:, 1].reshape(64, LANES)
    sc, ss = lower[:, 0].reshape(64, LANES), lower[:, 1].reshape(64, LANES)
    zero = jnp.zeros((8, LANES), f32)
    v_cos = jnp.concatenate([cc - ss, cc + ss, total[256:264], total[272:280], total[288:296]], 0)
    v_sin = jnp.concatenate([sc + cs, sc - cs, total[264:272], total[280:288], zero], 0)
    g_cos = w_sum * v_cos + w_dif * pltpu.roll(v_sin, 64, 1)
    g_sin = w_sum * v_sin - w_dif * pltpu.roll(v_cos, 64, 1)
    cp, cm, sp, sm = g_cos[0:64], g_cos[64:128], g_sin[0:64], g_sin[64:128]

    def pair_up(left, right):
        both = [left.reshape(8, 1, 8, LANES), right.reshape(8, 1, 8, LANES)]
        return jnp.concatenate(both, 1).reshape(128, LANES)

    rows = [pair_up(cp + cm, sp - sm), pair_up(sp + sm, cm - cp), g_cos[128:136], g_sin[128:136]]
    rows += [g_cos[136:144], g_sin[136:144], g_cos[144:152], jnp.zeros((88, LANES), f32)]
    full = jnp.concatenate(rows, 0)
    gt_scr[0:128, :] = full.T.astype(bf16)

    lane = iota((8, LANES), 1)
    count0 = jnp.broadcast_to(counts[8:9, 0:128], (8, LANES))
    count1 = jnp.broadcast_to(counts[8:9, 128:256], (8, LANES))
    left = (lane // 8) % 2 == 0
    sigma = jnp.where(left, 1.0, -1.0).astype(f32)

    def swap(value):
        return jnp.where(left, pltpu.roll(value, LANES - 8, 1), pltpu.roll(value, 8, 1))

    other = swap(count0)
    x, y, rest = total[304:312], swap(total[312:320]), total[320:328]
    plus = (x - sigma * y) * flat[:, 0:128] * jnp.where(left, count0, other)
    less = (y + sigma * x) * flat[:, 0:128] * jnp.where(left, other, count0)
    rest = rest * flat[:, 128:256] * (count1 + pltpu.roll(count1, 8, 1))
    low = jnp.concatenate([plus + sigma * less, swap(less - sigma * plus), rest], 1)
    gt_scr[128:144, :] = jnp.concatenate([low, jnp.zeros_like(low)], 0).astype(bf16)


def back_kernel(sub, radial, flat, z, *refs):
    basis, payload, out, gt_scr = refs[:PARTS], refs[PARTS:-2], refs[-2], refs[-1]
    width = out.shape[2]
    filter_rows(payload, radial, flat, gt_scr)
    for j, piece in enumerate(basis):
        size = piece.shape[1]
        product = jnp.dot(gt_scr[:, 0:ROWS], piece[...], preferred_element_type=f32)
        for start in range(0, size, sub):
            place = j * size + start
            message = product[128:136, start : start + sub]
            for m in range(16):
                part = product[8 * m : 8 * m + 8, start : start + sub]
                message = message + z[m : m + 1, place : place + sub] * part
            offset = place % width
            out[place // width, :, offset : offset + sub] = message.astype(bf16)


def update_kernel(sub, message, feat, gain, up, down, out):
    width = feat.shape[1]
    eye = iota((64, 64), 0) == iota((64, 64), 1)
    column = jnp.sum(jnp.where(eye, jnp.broadcast_to(gain[...], (64, 64)), 0.0), axis=1, keepdims=True)
    for start in range(0, width, sub):
        part = pl.ds(start, sub)
        value = message[:, :, part].astype(f32).reshape(64, sub)
        mean_sq = jnp.mean(value * value, axis=0, keepdims=True)
        normed = (value * lax.rsqrt(mean_sq + 1e-06) * column).astype(bf16)
        pre = lax.dot_general(up[...], normed, (((0,), (0,)), ((), ())), preferred_element_type=f32)
        half = 0.5 * pre
        hidden = (half + half * jnp.tanh(half)).astype(bf16)
        update = jnp.dot(down[...], hidden, preferred_element_type=f32)
        out[:, part] = (feat[:, part].astype(f32) + update).astype(bf16)


def body(
    positions,
    features,
    species,
    miller,
    species_table,
    filter_weight,
    norm_gain,
    up_weight,
    down_weight,
):
    atoms_here = features.shape[1]
    channels = features.shape[0]
    n_atom = lax.axis_size("atom")
    n_ka = lax.axis_size("ka")
    ka_split = n_ka // (channels // GROUP)
    local_count = atoms_here // n_ka
    scaling = 1.0 / math.sqrt(atoms_here * n_atom * K)
    params = pltpu.CompilerParams(vmem_limit_bytes=24 * 1024 * 1024)

    def exchange(value, flips):
        pairs = []
        for a in range(n_atom):
            for b in range(n_ka):
                if flips[a]:
                    pairs.append((a * n_ka + (b ^ flips[a]), a * n_ka + b))
        return lax.ppermute(value, ("atom", "ka"), pairs)

    chained = (n_atom, n_ka) == (4, 8)
    if chained:
        millers = [exchange(miller, FAR)]
    else:
        blocks = n_ka // n_atom
        near = blocks // 2
        flips = [
            [near * a + j for j in range(near)] + [n_ka - 1 - near * a - j for j in range(blocks - near)]
            for a in range(n_atom)
        ]
        millers = [exchange(miller, [row[j] for row in flips]) for j in range(blocks)]

    whole = pl.BlockSpec(memory_space=pltpu.VMEM)
    hbm = pl.BlockSpec(memory_space=pltpu.HBM)
    hbm = pl.BlockSpec(memory_space=pltpu.HBM)
    z, acc, local_features, *basis = pl.pallas_call(
        functools.partial(factor_kernel, ka_split),
        in_specs=[hbm] * 4,
        out_specs=[whole] * (3 + PARTS),
        out_shape=[
            jax.ShapeDtypeStruct((16, atoms_here), f32),
            jax.ShapeDtypeStruct((ROWS, 144), f32),
            jax.ShapeDtypeStruct((channels, local_count), bf16),
        ]
        + [jax.ShapeDtypeStruct((ROWS, atoms_here // PARTS), bf16)] * PARTS,
        scratch_shapes=[
            pltpu.VMEM((3, atoms_here), f32),
            pltpu.VMEM((16, atoms_here), bf16),
            pltpu.VMEM((1, atoms_here), jnp.int32),
            pltpu.VMEM((NSPEC, channels), f32),
            pltpu.VMEM((144, atoms_here), bf16),
            pltpu.VMEM((LANES, LANES), f32),
            pltpu.VMEM((LANES, LANES), f32),
            pltpu.VMEM((LANES, LANES), f32),
            pltpu.SemaphoreType.DMA((2 + 3 * PARTS,)),
        ],
        compiler_params=params,
        cost_estimate=pl.CostEstimate(flops=5 * 10**9, bytes_accessed=14 * 10**6, transcendentals=0),
        name="factors",
    )(
        pltpu.with_memory_space_constraint(positions, pltpu.HBM),
        pltpu.with_memory_space_constraint(features, pltpu.HBM),
        pltpu.with_memory_space_constraint(species.reshape(1, atoms_here), pltpu.HBM),
        pltpu.with_memory_space_constraint(species_table.T, pltpu.HBM),
    )

    packed = [jax.ShapeDtypeStruct((PAYLOAD, LANES), bf16)]
    if chained:
        packed.append(jax.ShapeDtypeStruct((6, miller.shape[1]), jnp.int32))
    payload, *pair = pl.pallas_call(
        functools.partial(pack_kernel, chained),
        in_specs=[whole] * (2 + len(millers)),
        out_specs=[whole] * len(packed),
        out_shape=packed,
        compiler_params=params,
        name="pack",
    )(acc, miller, *millers[::-1])
    radial, flat = pl.pallas_call(
        functools.partial(tables_kernel, ka_split, scaling),
        in_specs=[whole, pl.BlockSpec(memory_space=pl.ANY)],
        out_specs=[whole, whole],
        out_shape=[
            jax.ShapeDtypeStruct((152, LANES), f32),
            jax.ShapeDtypeStruct((GROUP, 2 * LANES), f32),
        ],
        compiler_params=params,
        cost_estimate=pl.CostEstimate(flops=10**9, bytes_accessed=10**6, transcendentals=10**6),
        name="tables",
    )(filter_weight.T, payload)
    if chained:
        across = lax.ppermute(payload, "atom", [(a, a ^ 2) for a in range(4)])
        payload = pl.pallas_call(
            fold_kernel,
            in_specs=[whole] * 3,
            out_specs=whole,
            out_shape=jax.ShapeDtypeStruct((PAYLOAD, LANES), bf16),
            compiler_params=params,
            name="fold",
        )(payload, across, exchange(pair[0], NEAR))
        gathered = [payload, lax.ppermute(payload, "atom", [(a, a ^ 1) for a in range(4)])]
    else:
        gathered = list(lax.all_gather(payload, "atom"))

    message = pl.pallas_call(
        functools.partial(back_kernel, min(512, local_count)),
        in_specs=[whole] * (3 + PARTS + len(gathered)),
        out_specs=whole,
        out_shape=jax.ShapeDtypeStruct((n_ka, GROUP, local_count), bf16),
        scratch_shapes=[pltpu.VMEM((144, 384), bf16)],
        compiler_params=params,
        cost_estimate=pl.CostEstimate(flops=5 * 10**9, bytes_accessed=11 * 10**6, transcendentals=0),
        name="back",
    )(radial, flat, z, *basis, *gathered)

    groups = None
    if ka_split > 1:
        message = message.reshape(n_ka // ka_split, ka_split, GROUP, local_count)
        message = lax.dynamic_index_in_dim(message, lax.axis_index("ka") % ka_split, 1, False)
        groups = [[g * ka_split + s for g in range(n_ka // ka_split)] for s in range(ka_split)]
    message = lax.all_to_all(message, "ka", 0, 0, axis_index_groups=groups, tiled=True)

    return pl.pallas_call(
        functools.partial(update_kernel, local_count),
        in_specs=[whole] * 5,
        out_specs=whole,
        out_shape=jax.ShapeDtypeStruct((channels, local_count), bf16),
        compiler_params=params,
        name="update",
    )(message, local_features, norm_gain.reshape(1, channels), up_weight.T, down_weight)


def solution(mesh):
    in_specs = (P(None, "atom"), P(None, "atom"), P("atom"), P(None, "ka"), P(), P(), P(), P(), P())
    out_specs = P(None, ("atom", "ka"))
    return jax.shard_map(body, mesh=mesh, in_specs=in_specs, out_specs=out_specs, check_vma=False)
```

```python
import functools
import math

import jax
import jax.numpy as jnp
import numpy as np
from jax import lax
from jax.experimental import pallas as pl
from jax.experimental.pallas import tpu as pltpu
from jax.sharding import PartitionSpec as P

K = 4096
NRBF = 16
NSPEC = 8
MAXM = 8
GROUP = 8
ROWS = 304
CHUNK = 1024
SPAN = 4
PARTS = 4
LANES = 128
PAYLOAD = 400
k_cutoff = 14.0
FAR = (6, 3, 4, 5)
NEAR = (1, 2, 1, 2)
f32 = jnp.float32
bf16 = jnp.bfloat16


def fit(function, terms, odd):
    nodes = np.cos((np.arange(64) + 0.5) * np.pi / 64) * 0.5
    nodes = np.abs(nodes)
    target = function(2.0 * np.pi * nodes)
    if odd:
        target = target / nodes
    series = np.polynomial.chebyshev.Chebyshev.fit(nodes * nodes, target, terms - 1, domain=[0, 0.25])
    return [float(v) for v in series.convert(kind=np.polynomial.Polynomial).coef]


SIN = fit(np.sin, 7, True)
COS = fit(np.cos, 7, False)


def horner(coefs, x):
    total = coefs[-1] * x + coefs[-2]
    for value in coefs[-3::-1]:
        total = total * x + value
    return total


def first_harmonic(x):
    turns = x - jnp.floor(x + 0.5)
    square = turns * turns
    return horner(COS, square), turns * horner(SIN, square)


def iota(shape, axis):
    return lax.broadcasted_iota(jnp.int32, shape, axis)


def waves_to(scr, x):
    cosine, sine = first_harmonic(x)
    twice = cosine + cosine
    lower_c, lower_s = jnp.ones_like(cosine), jnp.zeros_like(sine)
    upper_c, upper_s = cosine, sine
    for m in range(MAXM):
        scr[8 * m : 8 * m + 8, :] = upper_c
        scr[64 + 8 * m : 72 + 8 * m, :] = upper_s
        lower_c, upper_c = upper_c, twice * upper_c - lower_c
        lower_s, upper_s = upper_s, twice * upper_s - lower_s


def spread(scr, row):
    pieces = [scr[pl.ds(row + k, 8, stride=0), :] for k in range(SPAN)]
    return jnp.concatenate(pieces, 1)


def comb(scr, row):
    return jnp.concatenate([scr[pl.ds(row + k, 8, stride=8), :] for k in range(SPAN)], 1)


def harmonics_chunk(pos, start, w0, w1, w2):
    for axis, scr in enumerate((w0, w1, w2)):
        rows = [pos[axis : axis + 1, pl.ds(start + LANES * k, LANES)] for k in range(8)]
        waves_to(scr, jnp.concatenate(rows, 0))


def factor_chunk(feat, species, table, odd, start, here, k, full, terms, z_out, w0, w1, w2):
    part = pl.ds(start, LANES * SPAN)
    local = pl.ds(here, LANES * SPAN)
    c1 = comb(w1, k)
    s1 = comb(w1, 64 + k)
    for m in range(16):
        left = spread(w0, 8 * m + k)
        full[16 * m : 16 * m + 16, local] = jnp.concatenate([left * c1, left * s1], 0).astype(bf16)
    full[256:272, local] = jnp.concatenate([comb(w0, k), comb(w0, 64 + k)], 0).astype(bf16)
    full[272:288, local] = jnp.concatenate([c1, s1], 0).astype(bf16)
    z_out[0:8, part] = comb(w2, k)
    z_out[8:16, part] = comb(w2, 64 + k)
    kinds = jnp.broadcast_to(species[0:1, part], (8, LANES * SPAN))
    embedded = table[0]
    for s in range(1, NSPEC):
        embedded = jnp.where(kinds == s, table[s], embedded)
    wide = feat[:, part].astype(f32)
    own = jnp.where(odd, wide[8:16], wide[0:8])
    source = (own + embedded).astype(bf16).astype(f32)
    for m in range(0, 16, 2):
        pair = [source * spread(w2, 8 * m + k), source * spread(w2, 8 * m + 8 + k)]
        terms[8 * m : 8 * m + 16, part] = jnp.concatenate(pair, 0).astype(bf16)
    terms[128:144, part] = jnp.concatenate([source, jnp.zeros_like(source)], 0).astype(bf16)


def choose(group, count):
    return (iota((count, 64), 1) == group * GROUP + iota((count, 64), 0) % GROUP).astype(f32)


def exact_dot(left, right, left_dim, right_dim):
    return lax.dot_general(
        left, right, (((left_dim,), (right_dim,)), ((), ())),
        precision=lax.Precision.HIGHEST, preferred_element_type=f32,
    )


def factor_kernel(ka_split, pos_hbm, feat_hbm, species_hbm, table_hbm, z_out, acc, local_out, *refs):
    basis = refs[:PARTS]
    pos, feat, species, table, terms, w0, w1, w2, sems = refs[PARTS:]
    me = lax.axis_index("ka")
    group = me // ka_split
    atoms, width = feat.shape[1], local_out.shape[1]
    first = pl.multiple_of((group // 2) * 16, 16)
    size = atoms // PARTS
    copies = [pltpu.make_async_copy(table_hbm, table, sems.at[0])]
    waits = []
    for p in range(PARTS):
        cut = pl.ds(p * size, size)
        waits.append(
            [
                pltpu.make_async_copy(pos_hbm.at[:, cut], pos.at[:, cut], sems.at[3 * p + 2]),
                pltpu.make_async_copy(species_hbm.at[:, cut], species.at[:, cut], sems.at[3 * p + 3]),
                pltpu.make_async_copy(
                    feat_hbm.at[pl.ds(first, 16), cut], feat.at[:, cut], sems.at[3 * p + 4]
                ),
            ]
        )
        copies += waits[p]
    keep = pltpu.make_async_copy(
        feat_hbm.at[:, pl.ds(pl.multiple_of(me * width, width), width)], local_out, sems.at[1]
    )
    for copy in copies + [keep]:
        copy.start()
    for full in basis:
        full[288:304, :] = (iota((16, size), 0) == 0).astype(f32).astype(bf16)
    odd = (group % 2) == 1
    copies[0].wait()
    mask = iota((8, 64), 1) == group * GROUP + iota((8, 64), 0)
    columns = []
    for s in range(NSPEC):
        own = jnp.sum(jnp.where(mask, table[s : s + 1, :], 0.0), axis=1, keepdims=True)
        columns.append(jnp.broadcast_to(own, (8, LANES * SPAN)))

    def step(p, j):
        here = pl.multiple_of(j * CHUNK, CHUNK)
        harmonics_chunk(pos, p * size + here, w0, w1, w2)
        for k in range(0, 8, SPAN):
            factor_chunk(
                feat, species, columns, odd, p * size + here + k * LANES, here + k * LANES, k,
                basis[p], terms, z_out, w0, w1, w2,
            )

    for p in range(PARTS):
        for copy in waits[p]:
            copy.wait()
        lax.fori_loop(0, size // CHUNK, lambda j, carry: step(p, j), None, unroll=4)
    total = None
    for p, full in enumerate(basis):
        piece = lax.dot_general(
            full[...], terms[:, p * size : (p + 1) * size],
            (((1,), (1,)), ((), ())), preferred_element_type=f32,
        )
        total = piece if total is None else total + piece
    acc[...] = total
    keep.wait()


def histogram(value):
    m0, m1, m2 = value[0:1, :], value[1:2, :], value[2:3, :]
    sign = jnp.where(17 * m0 + m1 < 0, -1, 1)
    m0, m1, m2 = m0 * sign, m1 * sign, m2 * sign
    inner = jnp.where(
        m1 > 0, 16 * m0 + m1 - 17, jnp.where(m1 < 0, 16 * m0 - m1 - 9, 127 + m0)
    )
    row = jnp.where(m0 > 0, inner, jnp.where(m1 > 0, 143 + m1, 160))
    column = jnp.where(row == 160, jnp.abs(m2), m2) + MAXM
    size = row.shape[1]
    row_hot = (iota((256, size), 0) == row).astype(f32).astype(bf16)
    column_hot = (iota((32, size), 0) == column).astype(f32).astype(bf16)
    return lax.dot_general(
        column_hot, row_hot, (((1,), (1,)), ((), ())), preferred_element_type=f32
    )


def pack_kernel(chained, acc, own, *refs):
    if chained:
        (first,), (out, pair_out) = refs[:1], refs[1:]
        pair_out[0:3, :] = own[...]
        pair_out[3:6, :] = first[...]
        at_start = jnp.where(lax.axis_index("atom") == 0, 1.0, 0.0)
        counts = histogram(first[...]) + at_start * histogram(own[...])
    else:
        millers, out = refs[:-1], refs[-1]
        at_start = lax.axis_index("atom") == 0
        counts = jnp.zeros((32, 256), f32)
        for j, ref in enumerate(millers[::-1]):
            value = jnp.where(at_start, own[...], ref[...]) if j == 0 else ref[...]
            counts = counts + histogram(value)
    out[0:ROWS, :] = acc[:, 0:LANES].astype(bf16)
    tail = jnp.concatenate([acc[:, 128:144], jnp.zeros((ROWS, 112), f32)], 1)
    tail = jnp.concatenate([tail, jnp.zeros((384 - ROWS, LANES), f32)], 0)
    flat = tail.T
    zero = jnp.zeros((GROUP, LANES), f32)
    pieces = [flat[0:8, 0:128], flat[0:8, 128:256], flat[0:8, 256:384], zero]
    out[304:336, :] = jnp.concatenate(pieces, 0).astype(bf16)
    out[336:368, :] = counts[:, 0:128].astype(bf16)
    out[368:400, :] = counts[:, 128:256].astype(bf16)


def fold_kernel(left, right, pair, out):
    out[0:336, :] = (left[0:336, :].astype(f32) + right[0:336, :].astype(f32)).astype(bf16)
    atom = lax.axis_index("atom")
    last = jnp.where(atom // 2 == atom % 2, 1.0, 0.0)
    extra = histogram(pair[0:3, :]) + last * histogram(pair[3:6, :])
    counts = left[336:400, :].astype(f32) + right[336:400, :].astype(f32)
    out[336:400, :] = (counts + jnp.concatenate([extra[:, 0:128], extra[:, 128:256]], 0)).astype(bf16)


def radial_sum(square, weight_of):
    magnitude = jnp.sqrt(square)
    total = None
    for b in range(NRBF):
        offset = (magnitude - b * (k_cutoff / (NRBF - 1))) * (NRBF / k_cutoff)
        term = weight_of(b) * jnp.exp(-(offset * offset))
        total = term if total is None else total + term
    return total


def tables_kernel(ka_split, scaling, weights, token, radial_out, flat_out):
    del token
    group = lax.axis_index("ka") // ka_split
    across = exact_dot(weights[...], choose(group, LANES), 1, 1)
    lane = iota((88, LANES), 1)
    row = iota((88, LANES), 0)
    third = (lane % 64) // 8 + 1
    first = row // 8 + 1
    second = row % 8 + 1
    planar = jnp.where(
        row < 64,
        first * first + second * second,
        jnp.where(row < 80, second * second, 0),
    )
    radial = radial_sum((planar + third * third).astype(f32), lambda b: across[b : b + 1, :]) * scaling
    radial = jnp.concatenate([radial[0:64], radial], 0)

    radial_out[...] = radial

    lane = iota((8, LANES), 1)
    cell = (lane // 16 + 1) * (lane // 16 + 1) + (lane % 8 + 1) * (lane % 8 + 1)
    edge = jnp.where(lane < 32, (lane % 8 + 1) * (lane % 8 + 1), 0)
    own = exact_dot(choose(group, GROUP), weights[...], 1, 1)
    flat_out[...] = radial_sum(
        jnp.concatenate([cell, edge], 1).astype(f32), lambda b: own[:, b : b + 1]
    ) * scaling


def filter_rows(payload, radial, flat, gt_scr):
    total = payload[0][...].astype(f32)
    for part in payload[1:]:
        total = total + part[...].astype(f32)
    counts = jnp.concatenate([total[336:368], total[368:400]], 1)
    lane = iota((32, LANES), 1)
    index = iota((32, LANES), 0) - MAXM
    height = (lane % 64) // 8 + 1
    plus = jnp.where(jnp.abs(index) == height, 1.0, 0.0)
    minus = jnp.where(index == height, 1.0, jnp.where(index == -height, -1.0, 0.0))
    minus = jnp.where(lane < 64, -minus, minus)
    spread = jnp.concatenate([plus, minus], 1).astype(f32)
    high = jnp.floor(counts * (1.0 / 64.0))
    split = jnp.concatenate([high, counts - 64.0 * high], 0).astype(bf16)
    scale = jnp.concatenate([64.0 * spread, spread], 0).astype(bf16)
    wide = lax.dot_general(split, scale, (((0,), (0,)), ((), ())), preferred_element_type=f32)
    def by_rows(value):
        both = value[0:128].reshape(8, 2, 8, LANES)
        edges = [value[128:136], value[144:152], value[160:168]]
        return jnp.concatenate([both[:, 0].reshape(64, LANES), both[:, 1].reshape(64, LANES)] + edges, 0)

    w_sum = by_rows(wide[:, 0:128]) * radial[...]
    w_dif = by_rows(wide[:, 128:256]) * radial[...]
    upper = total[0:128].reshape(8, 2, 8, LANES)
    lower = total[128:256].reshape(8, 2, 8, LANES)
    cc, cs = upper[:, 0].reshape(64, LANES), upper[:, 1].reshape(64, LANES)
    sc, ss = lower[:, 0].reshape(64, LANES), lower[:, 1].reshape(64, LANES)
    zero = jnp.zeros((8, LANES), f32)
    v_cos = jnp.concatenate([cc - ss, cc + ss, total[256:264], total[272:280], total[288:296]], 0)
    v_sin = jnp.concatenate([sc + cs, sc - cs, total[264:272], total[280:288], zero], 0)
    g_cos = w_sum * v_cos + w_dif * pltpu.roll(v_sin, 64, 1)
    g_sin = w_sum * v_sin - w_dif * pltpu.roll(v_cos, 64, 1)
    cp, cm, sp, sm = g_cos[0:64], g_cos[64:128], g_sin[0:64], g_sin[64:128]

    def pair_up(left, right):
        both = [left.reshape(8, 1, 8, LANES), right.reshape(8, 1, 8, LANES)]
        return jnp.concatenate(both, 1).reshape(128, LANES)

    rows = [pair_up(cp + cm, sp - sm), pair_up(sp + sm, cm - cp), g_cos[128:136], g_sin[128:136]]
    rows += [g_cos[136:144], g_sin[136:144], g_cos[144:152], jnp.zeros((88, LANES), f32)]
    full = jnp.concatenate(rows, 0)
    gt_scr[0:128, :] = full.T.astype(bf16)

    lane = iota((8, LANES), 1)
    count0 = jnp.broadcast_to(counts[8:9, 0:128], (8, LANES))
    count1 = jnp.broadcast_to(counts[8:9, 128:256], (8, LANES))
    left = (lane // 8) % 2 == 0
    sigma = jnp.where(left, 1.0, -1.0).astype(f32)

    def swap(value):
        return jnp.where(left, pltpu.roll(value, LANES - 8, 1), pltpu.roll(value, 8, 1))

    other = swap(count0)
    x, y, rest = total[304:312], swap(total[312:320]), total[320:328]
    plus = (x - sigma * y) * flat[:, 0:128] * jnp.where(left, count0, other)
    less = (y + sigma * x) * flat[:, 0:128] * jnp.where(left, other, count0)
    rest = rest * flat[:, 128:256] * (count1 + pltpu.roll(count1, 8, 1))
    low = jnp.concatenate([plus + sigma * less, swap(less - sigma * plus), rest], 1)
    gt_scr[128:144, :] = jnp.concatenate([low, jnp.zeros_like(low)], 0).astype(bf16)


def back_kernel(sub, radial, flat, z, *refs):
    basis, payload, out, gt_scr = refs[:PARTS], refs[PARTS:-2], refs[-2], refs[-1]
    width = out.shape[2]
    filter_rows(payload, radial, flat, gt_scr)
    for j, piece in enumerate(basis):
        size = piece.shape[1]
        product = jnp.dot(gt_scr[:, 0:ROWS], piece[...], preferred_element_type=f32)
        for start in range(0, size, sub):
            place = j * size + start
            message = product[128:136, start : start + sub]
            for m in range(16):
                part = product[8 * m : 8 * m + 8, start : start + sub]
                message = message + z[m : m + 1, place : place + sub] * part
            offset = place % width
            out[place // width, :, offset : offset + sub] = message.astype(bf16)


def update_kernel(sub, message, feat, gain, up, down, out):
    width = feat.shape[1]
    eye = iota((64, 64), 0) == iota((64, 64), 1)
    column = jnp.sum(jnp.where(eye, jnp.broadcast_to(gain[...], (64, 64)), 0.0), axis=1, keepdims=True)
    for start in range(0, width, sub):
        part = pl.ds(start, sub)
        value = message[:, :, part].astype(f32).reshape(64, sub)
        mean_sq = jnp.mean(value * value, axis=0, keepdims=True)
        normed = (value * lax.rsqrt(mean_sq + 1e-06) * column).astype(bf16)
        pre = lax.dot_general(up[...], normed, (((0,), (0,)), ((), ())), preferred_element_type=f32)
        half = 0.5 * pre
        hidden = (half + half * jnp.tanh(half)).astype(bf16)
        update = jnp.dot(down[...], hidden, preferred_element_type=f32)
        out[:, part] = (feat[:, part].astype(f32) + update).astype(bf16)


def body(
    positions,
    features,
    species,
    miller,
    species_table,
    filter_weight,
    norm_gain,
    up_weight,
    down_weight,
):
    atoms_here = features.shape[1]
    channels = features.shape[0]
    n_atom = lax.axis_size("atom")
    n_ka = lax.axis_size("ka")
    ka_split = n_ka // (channels // GROUP)
    local_count = atoms_here // n_ka
    scaling = 1.0 / math.sqrt(atoms_here * n_atom * K)
    params = pltpu.CompilerParams(vmem_limit_bytes=24 * 1024 * 1024)

    def exchange(value, flips):
        pairs = []
        for a in range(n_atom):
            for b in range(n_ka):
                if flips[a]:
                    pairs.append((a * n_ka + (b ^ flips[a]), a * n_ka + b))
        return lax.ppermute(value, ("atom", "ka"), pairs)

    chained = (n_atom, n_ka) == (4, 8)
    if chained:
        millers = [exchange(miller, FAR)]
    else:
        blocks = n_ka // n_atom
        near = blocks // 2
        flips = [
            [near * a + j for j in range(near)] + [n_ka - 1 - near * a - j for j in range(blocks - near)]
            for a in range(n_atom)
        ]
        millers = [exchange(miller, [row[j] for row in flips]) for j in range(blocks)]

    whole = pl.BlockSpec(memory_space=pltpu.VMEM)
    hbm = pl.BlockSpec(memory_space=pltpu.HBM)
    hbm = pl.BlockSpec(memory_space=pltpu.HBM)
    z, acc, local_features, *basis = pl.pallas_call(
        functools.partial(factor_kernel, ka_split),
        in_specs=[hbm] * 4,
        out_specs=[whole] * (3 + PARTS),
        out_shape=[
            jax.ShapeDtypeStruct((16, atoms_here), f32),
            jax.ShapeDtypeStruct((ROWS, 144), f32),
            jax.ShapeDtypeStruct((channels, local_count), bf16),
        ]
        + [jax.ShapeDtypeStruct((ROWS, atoms_here // PARTS), bf16)] * PARTS,
        scratch_shapes=[
            pltpu.VMEM((3, atoms_here), f32),
            pltpu.VMEM((16, atoms_here), bf16),
            pltpu.VMEM((1, atoms_here), jnp.int32),
            pltpu.VMEM((NSPEC, channels), f32),
            pltpu.VMEM((144, atoms_here), bf16),
            pltpu.VMEM((LANES, LANES), f32),
            pltpu.VMEM((LANES, LANES), f32),
            pltpu.VMEM((LANES, LANES), f32),
            pltpu.SemaphoreType.DMA((2 + 3 * PARTS,)),
        ],
        compiler_params=params,
        cost_estimate=pl.CostEstimate(flops=5 * 10**9, bytes_accessed=14 * 10**6, transcendentals=0),
        name="factors",
    )(
        pltpu.with_memory_space_constraint(positions, pltpu.HBM),
        pltpu.with_memory_space_constraint(features, pltpu.HBM),
        pltpu.with_memory_space_constraint(species.reshape(1, atoms_here), pltpu.HBM),
        pltpu.with_memory_space_constraint(species_table.T, pltpu.HBM),
    )

    packed = [jax.ShapeDtypeStruct((PAYLOAD, LANES), bf16)]
    if chained:
        packed.append(jax.ShapeDtypeStruct((6, miller.shape[1]), jnp.int32))
    payload, *pair = pl.pallas_call(
        functools.partial(pack_kernel, chained),
        in_specs=[whole] * (2 + len(millers)),
        out_specs=[whole] * len(packed),
        out_shape=packed,
        compiler_params=params,
        name="pack",
    )(acc, miller, *millers[::-1])
    radial, flat = pl.pallas_call(
        functools.partial(tables_kernel, ka_split, scaling),
        in_specs=[whole, pl.BlockSpec(memory_space=pl.ANY)],
        out_specs=[whole, whole],
        out_shape=[
            jax.ShapeDtypeStruct((152, LANES), f32),
            jax.ShapeDtypeStruct((GROUP, 2 * LANES), f32),
        ],
        compiler_params=params,
        cost_estimate=pl.CostEstimate(flops=10**9, bytes_accessed=10**6, transcendentals=10**6),
        name="tables",
    )(filter_weight.T, payload)
    if chained:
        across = lax.ppermute(payload, "atom", [(a, a ^ 2) for a in range(4)])
        payload = pl.pallas_call(
            fold_kernel,
            in_specs=[whole] * 3,
            out_specs=whole,
            out_shape=jax.ShapeDtypeStruct((PAYLOAD, LANES), bf16),
            compiler_params=params,
            name="fold",
        )(payload, across, exchange(pair[0], NEAR))
        gathered = [payload, lax.ppermute(payload, "atom", [(a, a ^ 1) for a in range(4)])]
    else:
        gathered = list(lax.all_gather(payload, "atom"))

    message = pl.pallas_call(
        functools.partial(back_kernel, min(512, local_count)),
        in_specs=[whole] * (3 + PARTS + len(gathered)),
        out_specs=whole,
        out_shape=jax.ShapeDtypeStruct((n_ka, GROUP, local_count), bf16),
        scratch_shapes=[pltpu.VMEM((144, 384), bf16)],
        compiler_params=params,
        cost_estimate=pl.CostEstimate(flops=5 * 10**9, bytes_accessed=11 * 10**6, transcendentals=0),
        name="back",
    )(radial, flat, z, *basis, *gathered)

    groups = None
    if ka_split > 1:
        message = message.reshape(n_ka // ka_split, ka_split, GROUP, local_count)
        message = lax.dynamic_index_in_dim(message, lax.axis_index("ka") % ka_split, 1, False)
        groups = [[g * ka_split + s for g in range(n_ka // ka_split)] for s in range(ka_split)]
    message = lax.all_to_all(message, "ka", 0, 0, axis_index_groups=groups, tiled=True)

    return pl.pallas_call(
        functools.partial(update_kernel, local_count),
        in_specs=[whole] * 5,
        out_specs=whole,
        out_shape=jax.ShapeDtypeStruct((channels, local_count), bf16),
        compiler_params=params,
        name="update",
    )(message, local_features, norm_gain.reshape(1, channels), up_weight.T, down_weight)


def solution(mesh):
    in_specs = (P(None, "atom"), P(None, "atom"), P("atom"), P(None, "ka"), P(), P(), P(), P(), P())
    out_specs = P(None, ("atom", "ka"))
    return jax.shard_map(body, mesh=mesh, in_specs=in_specs, out_specs=out_specs, check_vma=False)
```

```python
import functools
import math

import jax
import jax.numpy as jnp
import numpy as np
from jax import lax
from jax.experimental import pallas as pl
from jax.experimental.pallas import tpu as pltpu
from jax.sharding import PartitionSpec as P

K = 4096
NRBF = 16
NSPEC = 8
MAXM = 8
GROUP = 8
ROWS = 304
CHUNK = 1024
SPAN = 4
PARTS = 4
LANES = 128
PAYLOAD = 400
k_cutoff = 14.0
FAR = (6, 3, 4, 5)
NEAR = (1, 2, 1, 2)
f32 = jnp.float32
bf16 = jnp.bfloat16


def fit(function, terms, odd):
    nodes = np.cos((np.arange(64) + 0.5) * np.pi / 64) * 0.5
    nodes = np.abs(nodes)
    target = function(2.0 * np.pi * nodes)
    if odd:
        target = target / nodes
    series = np.polynomial.chebyshev.Chebyshev.fit(nodes * nodes, target, terms - 1, domain=[0, 0.25])
    return [float(v) for v in series.convert(kind=np.polynomial.Polynomial).coef]


SIN = fit(np.sin, 7, True)
COS = fit(np.cos, 7, False)


def horner(coefs, x):
    total = coefs[-1] * x + coefs[-2]
    for value in coefs[-3::-1]:
        total = total * x + value
    return total


def first_harmonic(x):
    turns = x - jnp.floor(x + 0.5)
    square = turns * turns
    return horner(COS, square), turns * horner(SIN, square)


def iota(shape, axis):
    return lax.broadcasted_iota(jnp.int32, shape, axis)


def waves_to(scr, x):
    cosine, sine = first_harmonic(x)
    twice = cosine + cosine
    lower_c, lower_s = jnp.ones_like(cosine), jnp.zeros_like(sine)
    upper_c, upper_s = cosine, sine
    for m in range(MAXM):
        scr[8 * m : 8 * m + 8, :] = upper_c
        scr[64 + 8 * m : 72 + 8 * m, :] = upper_s
        lower_c, upper_c = upper_c, twice * upper_c - lower_c
        lower_s, upper_s = upper_s, twice * upper_s - lower_s


def spread(scr, row):
    pieces = [scr[pl.ds(row + k, 8, stride=0), :] for k in range(SPAN)]
    return jnp.concatenate(pieces, 1)


def comb(scr, row):
    return jnp.concatenate([scr[pl.ds(row + k, 8, stride=8), :] for k in range(SPAN)], 1)


def harmonics_chunk(pos, start, w0, w1, w2):
    for axis, scr in enumerate((w0, w1, w2)):
        rows = [pos[axis : axis + 1, pl.ds(start + LANES * k, LANES)] for k in range(8)]
        waves_to(scr, jnp.concatenate(rows, 0))


def factor_chunk(feat, species, table, odd, start, here, k, full, terms, z_out, w0, w1, w2):
    part = pl.ds(start, LANES * SPAN)
    local = pl.ds(here, LANES * SPAN)
    c1 = comb(w1, k)
    s1 = comb(w1, 64 + k)
    for m in range(16):
        left = spread(w0, 8 * m + k)
        full[16 * m : 16 * m + 16, local] = jnp.concatenate([left * c1, left * s1], 0).astype(bf16)
    full[256:272, local] = jnp.concatenate([comb(w0, k), comb(w0, 64 + k)], 0).astype(bf16)
    full[272:288, local] = jnp.concatenate([c1, s1], 0).astype(bf16)
    z_out[0:8, part] = comb(w2, k)
    z_out[8:16, part] = comb(w2, 64 + k)
    kinds = jnp.broadcast_to(species[0:1, part], (8, LANES * SPAN))
    embedded = table[0]
    for s in range(1, NSPEC):
        embedded = jnp.where(kinds == s, table[s], embedded)
    wide = feat[:, part].astype(f32)
    own = jnp.where(odd, wide[8:16], wide[0:8])
    source = (own + embedded).astype(bf16).astype(f32)
    for m in range(0, 16, 2):
        pair = [source * spread(w2, 8 * m + k), source * spread(w2, 8 * m + 8 + k)]
        terms[8 * m : 8 * m + 16, part] = jnp.concatenate(pair, 0).astype(bf16)
    terms[128:144, part] = jnp.concatenate([source, jnp.zeros_like(source)], 0).astype(bf16)


def choose(group, count):
    return (iota((count, 64), 1) == group * GROUP + iota((count, 64), 0) % GROUP).astype(f32)


def exact_dot(left, right, left_dim, right_dim):
    return lax.dot_general(
        left, right, (((left_dim,), (right_dim,)), ((), ())),
        precision=lax.Precision.HIGHEST, preferred_element_type=f32,
    )


def factor_kernel(ka_split, pos_hbm, feat_hbm, species_hbm, table_hbm, z_out, acc, local_out, *refs):
    basis = refs[:PARTS]
    pos, feat, species, table, terms, w0, w1, w2, sems = refs[PARTS:]
    me = lax.axis_index("ka")
    group = me // ka_split
    atoms, width = feat.shape[1], local_out.shape[1]
    first = pl.multiple_of((group // 2) * 16, 16)
    size = atoms // PARTS
    copies = [pltpu.make_async_copy(table_hbm, table, sems.at[0])]
    waits = []
    for p in range(PARTS):
        cut = pl.ds(p * size, size)
        waits.append(
            [
                pltpu.make_async_copy(pos_hbm.at[:, cut], pos.at[:, cut], sems.at[3 * p + 2]),
                pltpu.make_async_copy(species_hbm.at[:, cut], species.at[:, cut], sems.at[3 * p + 3]),
                pltpu.make_async_copy(
                    feat_hbm.at[pl.ds(first, 16), cut], feat.at[:, cut], sems.at[3 * p + 4]
                ),
            ]
        )
        copies += waits[p]
    keep = pltpu.make_async_copy(
        feat_hbm.at[:, pl.ds(pl.multiple_of(me * width, width), width)], local_out, sems.at[1]
    )
    for copy in copies + [keep]:
        copy.start()
    for full in basis:
        full[288:304, :] = (iota((16, size), 0) == 0).astype(f32).astype(bf16)
    odd = (group % 2) == 1
    copies[0].wait()
    mask = iota((8, 64), 1) == group * GROUP + iota((8, 64), 0)
    columns = []
    for s in range(NSPEC):
        own = jnp.sum(jnp.where(mask, table[s : s + 1, :], 0.0), axis=1, keepdims=True)
        columns.append(jnp.broadcast_to(own, (8, LANES * SPAN)))

    def step(p, j):
        here = pl.multiple_of(j * CHUNK, CHUNK)
        harmonics_chunk(pos, p * size + here, w0, w1, w2)
        for k in range(0, 8, SPAN):
            factor_chunk(
                feat, species, columns, odd, p * size + here + k * LANES, here + k * LANES, k,
                basis[p], terms, z_out, w0, w1, w2,
            )

    for p in range(PARTS):
        for copy in waits[p]:
            copy.wait()
        lax.fori_loop(0, size // CHUNK, lambda j, carry: step(p, j), None, unroll=4)
    total = None
    for p, full in enumerate(basis):
        piece = lax.dot_general(
            full[...], terms[:, p * size : (p + 1) * size],
            (((1,), (1,)), ((), ())), preferred_element_type=f32,
        )
        total = piece if total is None else total + piece
    acc[...] = total
    keep.wait()


def histogram(value):
    m0, m1, m2 = value[0:1, :], value[1:2, :], value[2:3, :]
    sign = jnp.where(17 * m0 + m1 < 0, -1, 1)
    m0, m1, m2 = m0 * sign, m1 * sign, m2 * sign
    inner = jnp.where(
        m1 > 0, 16 * m0 + m1 - 17, jnp.where(m1 < 0, 16 * m0 - m1 - 9, 127 + m0)
    )
    row = jnp.where(m0 > 0, inner, jnp.where(m1 > 0, 143 + m1, 160))
    column = jnp.where(row == 160, jnp.abs(m2), m2) + MAXM
    size = row.shape[1]
    row_hot = (iota((256, size), 0) == row).astype(f32).astype(bf16)
    column_hot = (iota((32, size), 0) == column).astype(f32).astype(bf16)
    return lax.dot_general(
        column_hot, row_hot, (((1,), (1,)), ((), ())), preferred_element_type=f32
    )


def pack_kernel(chained, acc, own, *refs):
    if chained:
        (first,), (out, pair_out) = refs[:1], refs[1:]
        pair_out[0:3, :] = own[...]
        pair_out[3:6, :] = first[...]
        at_start = jnp.where(lax.axis_index("atom") == 0, 1.0, 0.0)
        counts = histogram(first[...]) + at_start * histogram(own[...])
    else:
        millers, out = refs[:-1], refs[-1]
        at_start = lax.axis_index("atom") == 0
        counts = jnp.zeros((32, 256), f32)
        for j, ref in enumerate(millers[::-1]):
            value = jnp.where(at_start, own[...], ref[...]) if j == 0 else ref[...]
            counts = counts + histogram(value)
    out[0:ROWS, :] = acc[:, 0:LANES].astype(bf16)
    tail = jnp.concatenate([acc[:, 128:144], jnp.zeros((ROWS, 112), f32)], 1)
    tail = jnp.concatenate([tail, jnp.zeros((384 - ROWS, LANES), f32)], 0)
    flat = tail.T
    zero = jnp.zeros((GROUP, LANES), f32)
    pieces = [flat[0:8, 0:128], flat[0:8, 128:256], flat[0:8, 256:384], zero]
    out[304:336, :] = jnp.concatenate(pieces, 0).astype(bf16)
    out[336:368, :] = counts[:, 0:128].astype(bf16)
    out[368:400, :] = counts[:, 128:256].astype(bf16)


def fold_kernel(left, right, pair, out):
    out[0:336, :] = (left[0:336, :].astype(f32) + right[0:336, :].astype(f32)).astype(bf16)
    atom = lax.axis_index("atom")
    last = jnp.where(atom // 2 == atom % 2, 1.0, 0.0)
    extra = histogram(pair[0:3, :]) + last * histogram(pair[3:6, :])
    counts = left[336:400, :].astype(f32) + right[336:400, :].astype(f32)
    out[336:400, :] = (counts + jnp.concatenate([extra[:, 0:128], extra[:, 128:256]], 0)).astype(bf16)


def radial_sum(square, weight_of):
    magnitude = jnp.sqrt(square)
    total = None
    for b in range(NRBF):
        offset = (magnitude - b * (k_cutoff / (NRBF - 1))) * (NRBF / k_cutoff)
        term = weight_of(b) * jnp.exp(-(offset * offset))
        total = term if total is None else total + term
    return total


def tables_kernel(ka_split, scaling, weights, token, radial_out, flat_out):
    del token
    group = lax.axis_index("ka") // ka_split
    across = exact_dot(weights[...], choose(group, LANES), 1, 1)
    lane = iota((88, LANES), 1)
    row = iota((88, LANES), 0)
    third = (lane % 64) // 8 + 1
    first = row // 8 + 1
    second = row % 8 + 1
    planar = jnp.where(
        row < 64,
        first * first + second * second,
        jnp.where(row < 80, second * second, 0),
    )
    radial = radial_sum((planar + third * third).astype(f32), lambda b: across[b : b + 1, :]) * scaling
    radial = jnp.concatenate([radial[0:64], radial], 0)

    radial_out[...] = radial

    lane = iota((8, LANES), 1)
    cell = (lane // 16 + 1) * (lane // 16 + 1) + (lane % 8 + 1) * (lane % 8 + 1)
    edge = jnp.where(lane < 32, (lane % 8 + 1) * (lane % 8 + 1), 0)
    own = exact_dot(choose(group, GROUP), weights[...], 1, 1)
    flat_out[...] = radial_sum(
        jnp.concatenate([cell, edge], 1).astype(f32), lambda b: own[:, b : b + 1]
    ) * scaling


def filter_rows(payload, radial, flat, gt_scr):
    total = payload[0][...].astype(f32)
    for part in payload[1:]:
        total = total + part[...].astype(f32)
    counts = jnp.concatenate([total[336:368], total[368:400]], 1)
    lane = iota((32, LANES), 1)
    index = iota((32, LANES), 0) - MAXM
    height = (lane % 64) // 8 + 1
    plus = jnp.where(jnp.abs(index) == height, 1.0, 0.0)
    minus = jnp.where(index == height, 1.0, jnp.where(index == -height, -1.0, 0.0))
    minus = jnp.where(lane < 64, -minus, minus)
    spread = jnp.concatenate([plus, minus], 1).astype(f32)
    high = jnp.floor(counts * (1.0 / 64.0))
    split = jnp.concatenate([high, counts - 64.0 * high], 0).astype(bf16)
    scale = jnp.concatenate([64.0 * spread, spread], 0).astype(bf16)
    wide = lax.dot_general(split, scale, (((0,), (0,)), ((), ())), preferred_element_type=f32)
    def by_rows(value):
        both = value[0:128].reshape(8, 2, 8, LANES)
        edges = [value[128:136], value[144:152], value[160:168]]
        return jnp.concatenate([both[:, 0].reshape(64, LANES), both[:, 1].reshape(64, LANES)] + edges, 0)

    w_sum = by_rows(wide[:, 0:128]) * radial[...]
    w_dif = by_rows(wide[:, 128:256]) * radial[...]
    upper = total[0:128].reshape(8, 2, 8, LANES)
    lower = total[128:256].reshape(8, 2, 8, LANES)
    cc, cs = upper[:, 0].reshape(64, LANES), upper[:, 1].reshape(64, LANES)
    sc, ss = lower[:, 0].reshape(64, LANES), lower[:, 1].reshape(64, LANES)
    zero = jnp.zeros((8, LANES), f32)
    v_cos = jnp.concatenate([cc - ss, cc + ss, total[256:264], total[272:280], total[288:296]], 0)
    v_sin = jnp.concatenate([sc + cs, sc - cs, total[264:272], total[280:288], zero], 0)
    g_cos = w_sum * v_cos + w_dif * pltpu.roll(v_sin, 64, 1)
    g_sin = w_sum * v_sin - w_dif * pltpu.roll(v_cos, 64, 1)
    cp, cm, sp, sm = g_cos[0:64], g_cos[64:128], g_sin[0:64], g_sin[64:128]

    def pair_up(left, right):
        both = [left.reshape(8, 1, 8, LANES), right.reshape(8, 1, 8, LANES)]
        return jnp.concatenate(both, 1).reshape(128, LANES)

    rows = [pair_up(cp + cm, sp - sm), pair_up(sp + sm, cm - cp), g_cos[128:136], g_sin[128:136]]
    rows += [g_cos[136:144], g_sin[136:144], g_cos[144:152], jnp.zeros((88, LANES), f32)]
    full = jnp.concatenate(rows, 0)
    gt_scr[0:128, :] = full.T.astype(bf16)

    lane = iota((8, LANES), 1)
    count0 = jnp.broadcast_to(counts[8:9, 0:128], (8, LANES))
    count1 = jnp.broadcast_to(counts[8:9, 128:256], (8, LANES))
    left = (lane // 8) % 2 == 0
    sigma = jnp.where(left, 1.0, -1.0).astype(f32)

    def swap(value):
        return jnp.where(left, pltpu.roll(value, LANES - 8, 1), pltpu.roll(value, 8, 1))

    other = swap(count0)
    x, y, rest = total[304:312], swap(total[312:320]), total[320:328]
    plus = (x - sigma * y) * flat[:, 0:128] * jnp.where(left, count0, other)
    less = (y + sigma * x) * flat[:, 0:128] * jnp.where(left, other, count0)
    rest = rest * flat[:, 128:256] * (count1 + pltpu.roll(count1, 8, 1))
    low = jnp.concatenate([plus + sigma * less, swap(less - sigma * plus), rest], 1)
    gt_scr[128:144, :] = jnp.concatenate([low, jnp.zeros_like(low)], 0).astype(bf16)


def back_kernel(sub, radial, flat, z, *refs):
    basis, payload, out, gt_scr = refs[:PARTS], refs[PARTS:-2], refs[-2], refs[-1]
    width = out.shape[2]
    filter_rows(payload, radial, flat, gt_scr)
    for j, piece in enumerate(basis):
        size = piece.shape[1]
        product = jnp.dot(gt_scr[:, 0:ROWS], piece[...], preferred_element_type=f32)
        for start in range(0, size, sub):
            place = j * size + start
            message = product[128:136, start : start + sub]
            for m in range(16):
                part = product[8 * m : 8 * m + 8, start : start + sub]
                message = message + z[m : m + 1, place : place + sub] * part
            offset = place % width
            out[place // width, :, offset : offset + sub] = message.astype(bf16)


def update_kernel(sub, message, feat, gain, up, down, out):
    width = feat.shape[1]
    eye = iota((64, 64), 0) == iota((64, 64), 1)
    column = jnp.sum(jnp.where(eye, jnp.broadcast_to(gain[...], (64, 64)), 0.0), axis=1, keepdims=True)
    for start in range(0, width, sub):
        part = pl.ds(start, sub)
        value = message[:, :, part].astype(f32).reshape(64, sub)
        mean_sq = jnp.mean(value * value, axis=0, keepdims=True)
        normed = (value * lax.rsqrt(mean_sq + 1e-06) * column).astype(bf16)
        pre = lax.dot_general(up[...], normed, (((0,), (0,)), ((), ())), preferred_element_type=f32)
        half = 0.5 * pre
        hidden = (half + half * jnp.tanh(half)).astype(bf16)
        update = jnp.dot(down[...], hidden, preferred_element_type=f32)
        out[:, part] = (feat[:, part].astype(f32) + update).astype(bf16)


def body(
    positions,
    features,
    species,
    miller,
    species_table,
    filter_weight,
    norm_gain,
    up_weight,
    down_weight,
):
    atoms_here = features.shape[1]
    channels = features.shape[0]
    n_atom = lax.axis_size("atom")
    n_ka = lax.axis_size("ka")
    ka_split = n_ka // (channels // GROUP)
    local_count = atoms_here // n_ka
    scaling = 1.0 / math.sqrt(atoms_here * n_atom * K)
    params = pltpu.CompilerParams(vmem_limit_bytes=24 * 1024 * 1024)

    def exchange(value, flips):
        pairs = []
        for a in range(n_atom):
            for b in range(n_ka):
                if flips[a]:
                    pairs.append((a * n_ka + (b ^ flips[a]), a * n_ka + b))
        return lax.ppermute(value, ("atom", "ka"), pairs)

    chained = (n_atom, n_ka) == (4, 8)
    if chained:
        millers = [exchange(miller, FAR)]
    else:
        blocks = n_ka // n_atom
        near = blocks // 2
        flips = [
            [near * a + j for j in range(near)] + [n_ka - 1 - near * a - j for j in range(blocks - near)]
            for a in range(n_atom)
        ]
        millers = [exchange(miller, [row[j] for row in flips]) for j in range(blocks)]

    whole = pl.BlockSpec(memory_space=pltpu.VMEM)
    hbm = pl.BlockSpec(memory_space=pltpu.HBM)
    hbm = pl.BlockSpec(memory_space=pltpu.HBM)
    z, acc, local_features, *basis = pl.pallas_call(
        functools.partial(factor_kernel, ka_split),
        in_specs=[hbm] * 4,
        out_specs=[whole] * (3 + PARTS),
        out_shape=[
            jax.ShapeDtypeStruct((16, atoms_here), f32),
            jax.ShapeDtypeStruct((ROWS, 144), f32),
            jax.ShapeDtypeStruct((channels, local_count), bf16),
        ]
        + [jax.ShapeDtypeStruct((ROWS, atoms_here // PARTS), bf16)] * PARTS,
        scratch_shapes=[
            pltpu.VMEM((3, atoms_here), f32),
            pltpu.VMEM((16, atoms_here), bf16),
            pltpu.VMEM((1, atoms_here), jnp.int32),
            pltpu.VMEM((NSPEC, channels), f32),
            pltpu.VMEM((144, atoms_here), bf16),
            pltpu.VMEM((LANES + 8, LANES), f32),
            pltpu.VMEM((LANES + 8, LANES), f32),
            pltpu.VMEM((LANES + 8, LANES), f32),
            pltpu.SemaphoreType.DMA((2 + 3 * PARTS,)),
        ],
        compiler_params=params,
        cost_estimate=pl.CostEstimate(flops=5 * 10**9, bytes_accessed=14 * 10**6, transcendentals=0),
        name="factors",
    )(
        pltpu.with_memory_space_constraint(positions, pltpu.HBM),
        pltpu.with_memory_space_constraint(features, pltpu.HBM),
        pltpu.with_memory_space_constraint(species.reshape(1, atoms_here), pltpu.HBM),
        pltpu.with_memory_space_constraint(species_table.T, pltpu.HBM),
    )

    packed = [jax.ShapeDtypeStruct((PAYLOAD, LANES), bf16)]
    if chained:
        packed.append(jax.ShapeDtypeStruct((6, miller.shape[1]), jnp.int32))
    payload, *pair = pl.pallas_call(
        functools.partial(pack_kernel, chained),
        in_specs=[whole] * (2 + len(millers)),
        out_specs=[whole] * len(packed),
        out_shape=packed,
        compiler_params=params,
        name="pack",
    )(acc, miller, *millers[::-1])
    radial, flat = pl.pallas_call(
        functools.partial(tables_kernel, ka_split, scaling),
        in_specs=[whole, pl.BlockSpec(memory_space=pl.ANY)],
        out_specs=[whole, whole],
        out_shape=[
            jax.ShapeDtypeStruct((152, LANES), f32),
            jax.ShapeDtypeStruct((GROUP, 2 * LANES), f32),
        ],
        compiler_params=params,
        cost_estimate=pl.CostEstimate(flops=10**9, bytes_accessed=10**6, transcendentals=10**6),
        name="tables",
    )(filter_weight.T, payload)
    if chained:
        across = lax.ppermute(payload, "atom", [(a, a ^ 2) for a in range(4)])
        payload = pl.pallas_call(
            fold_kernel,
            in_specs=[whole] * 3,
            out_specs=whole,
            out_shape=jax.ShapeDtypeStruct((PAYLOAD, LANES), bf16),
            compiler_params=params,
            name="fold",
        )(payload, across, exchange(pair[0], NEAR))
        gathered = [payload, lax.ppermute(payload, "atom", [(a, a ^ 1) for a in range(4)])]
    else:
        gathered = list(lax.all_gather(payload, "atom"))

    message = pl.pallas_call(
        functools.partial(back_kernel, min(512, local_count)),
        in_specs=[whole] * (3 + PARTS + len(gathered)),
        out_specs=whole,
        out_shape=jax.ShapeDtypeStruct((n_ka, GROUP, local_count), bf16),
        scratch_shapes=[pltpu.VMEM((144, 384), bf16)],
        compiler_params=params,
        cost_estimate=pl.CostEstimate(flops=5 * 10**9, bytes_accessed=11 * 10**6, transcendentals=0),
        name="back",
    )(radial, flat, z, *basis, *gathered)

    groups = None
    if ka_split > 1:
        message = message.reshape(n_ka // ka_split, ka_split, GROUP, local_count)
        message = lax.dynamic_index_in_dim(message, lax.axis_index("ka") % ka_split, 1, False)
        groups = [[g * ka_split + s for g in range(n_ka // ka_split)] for s in range(ka_split)]
    message = lax.all_to_all(message, "ka", 0, 0, axis_index_groups=groups, tiled=True)

    return pl.pallas_call(
        functools.partial(update_kernel, local_count),
        in_specs=[whole] * 5,
        out_specs=whole,
        out_shape=jax.ShapeDtypeStruct((channels, local_count), bf16),
        compiler_params=params,
        name="update",
    )(message, local_features, norm_gain.reshape(1, channels), up_weight.T, down_weight)


def solution(mesh):
    in_specs = (P(None, "atom"), P(None, "atom"), P("atom"), P(None, "ka"), P(), P(), P(), P(), P())
    out_specs = P(None, ("atom", "ka"))
    return jax.shard_map(body, mesh=mesh, in_specs=in_specs, out_specs=out_specs, check_vma=False)
```

```python
import functools
import math

import jax
import jax.numpy as jnp
import numpy as np
from jax import lax
from jax.experimental import pallas as pl
from jax.experimental.pallas import tpu as pltpu
from jax.sharding import PartitionSpec as P

K = 4096
NRBF = 16
NSPEC = 8
MAXM = 8
GROUP = 8
ROWS = 304
CHUNK = 1024
SPAN = 4
PARTS = 4
LANES = 128
PAYLOAD = 400
k_cutoff = 14.0
FAR = (6, 3, 4, 5)
NEAR = (1, 2, 1, 2)
f32 = jnp.float32
bf16 = jnp.bfloat16


def fit(function, terms, odd):
    nodes = np.cos((np.arange(64) + 0.5) * np.pi / 64) * 0.5
    nodes = np.abs(nodes)
    target = function(2.0 * np.pi * nodes)
    if odd:
        target = target / nodes
    series = np.polynomial.chebyshev.Chebyshev.fit(nodes * nodes, target, terms - 1, domain=[0, 0.25])
    return [float(v) for v in series.convert(kind=np.polynomial.Polynomial).coef]


SIN = fit(np.sin, 7, True)
COS = fit(np.cos, 7, False)


def horner(coefs, x):
    total = coefs[-1] * x + coefs[-2]
    for value in coefs[-3::-1]:
        total = total * x + value
    return total


def first_harmonic(x):
    turns = x - jnp.floor(x + 0.5)
    square = turns * turns
    return horner(COS, square), turns * horner(SIN, square)


def iota(shape, axis):
    return lax.broadcasted_iota(jnp.int32, shape, axis)


def waves_to(scr, x):
    cosine, sine = first_harmonic(x)
    twice = cosine + cosine
    lower_c, lower_s = jnp.ones_like(cosine), jnp.zeros_like(sine)
    upper_c, upper_s = cosine, sine
    for m in range(MAXM):
        scr[8 * m : 8 * m + 8, :] = upper_c
        scr[64 + 8 * m : 72 + 8 * m, :] = upper_s
        lower_c, upper_c = upper_c, twice * upper_c - lower_c
        lower_s, upper_s = upper_s, twice * upper_s - lower_s


def spread(scr, row):
    pieces = [scr[pl.ds(row + k, 8, stride=0), :] for k in range(SPAN)]
    return jnp.concatenate(pieces, 1)


def comb(scr, row):
    return jnp.concatenate([scr[pl.ds(row + k, 8, stride=8), :] for k in range(SPAN)], 1)


def harmonics_chunk(pos, start, w0, w1, w2):
    for axis, scr in enumerate((w0, w1, w2)):
        rows = [pos[axis : axis + 1, pl.ds(start + LANES * k, LANES)] for k in range(8)]
        waves_to(scr, jnp.concatenate(rows, 0))


def factor_chunk(feat, species, table, odd, start, here, k, full, terms, z_out, w0, w1, w2):
    part = pl.ds(start, LANES * SPAN)
    local = pl.ds(here, LANES * SPAN)
    c1 = comb(w1, k)
    s1 = comb(w1, 64 + k)
    for m in range(16):
        left = spread(w0, 8 * m + k)
        full[16 * m : 16 * m + 16, local] = jnp.concatenate([left * c1, left * s1], 0).astype(bf16)
    full[256:272, local] = jnp.concatenate([comb(w0, k), comb(w0, 64 + k)], 0).astype(bf16)
    full[272:288, local] = jnp.concatenate([c1, s1], 0).astype(bf16)
    z_out[0:8, part] = comb(w2, k)
    z_out[8:16, part] = comb(w2, 64 + k)
    kinds = jnp.broadcast_to(species[0:1, part], (8, LANES * SPAN))
    embedded = table[0]
    for s in range(1, NSPEC):
        embedded = jnp.where(kinds == s, table[s], embedded)
    wide = feat[:, part].astype(f32)
    own = jnp.where(odd, wide[8:16], wide[0:8])
    source = (own + embedded).astype(bf16).astype(f32)
    for m in range(0, 16, 2):
        pair = [source * spread(w2, 8 * m + k), source * spread(w2, 8 * m + 8 + k)]
        terms[8 * m : 8 * m + 16, part] = jnp.concatenate(pair, 0).astype(bf16)
    terms[128:144, part] = jnp.concatenate([source, jnp.zeros_like(source)], 0).astype(bf16)


def choose(group, count):
    return (iota((count, 64), 1) == group * GROUP + iota((count, 64), 0) % GROUP).astype(f32)


def exact_dot(left, right, left_dim, right_dim):
    return lax.dot_general(
        left, right, (((left_dim,), (right_dim,)), ((), ())),
        precision=lax.Precision.HIGHEST, preferred_element_type=f32,
    )


def factor_kernel(ka_split, pos_hbm, feat_hbm, species_hbm, table_hbm, z_out, acc, local_out, *refs):
    basis = refs[:PARTS]
    pos, feat, species, table, terms, w0, w1, w2, sems = refs[PARTS:]
    me = lax.axis_index("ka")
    group = me // ka_split
    atoms, width = feat.shape[1], local_out.shape[1]
    first = pl.multiple_of((group // 2) * 16, 16)
    size = atoms // PARTS
    copies = [pltpu.make_async_copy(table_hbm, table, sems.at[0])]
    waits = []
    for p in range(PARTS):
        cut = pl.ds(p * size, size)
        waits.append(
            [
                pltpu.make_async_copy(pos_hbm.at[:, cut], pos.at[:, cut], sems.at[3 * p + 2]),
                pltpu.make_async_copy(species_hbm.at[:, cut], species.at[:, cut], sems.at[3 * p + 3]),
                pltpu.make_async_copy(
                    feat_hbm.at[pl.ds(first, 16), cut], feat.at[:, cut], sems.at[3 * p + 4]
                ),
            ]
        )
        copies += waits[p]
    keep = pltpu.make_async_copy(
        feat_hbm.at[:, pl.ds(pl.multiple_of(me * width, width), width)], local_out, sems.at[1]
    )
    for copy in copies + [keep]:
        copy.start()
    for full in basis:
        full[288:304, :] = (iota((16, size), 0) == 0).astype(f32).astype(bf16)
    odd = (group % 2) == 1
    copies[0].wait()
    mask = iota((8, 64), 1) == group * GROUP + iota((8, 64), 0)
    columns = []
    for s in range(NSPEC):
        own = jnp.sum(jnp.where(mask, table[s : s + 1, :], 0.0), axis=1, keepdims=True)
        columns.append(jnp.broadcast_to(own, (8, LANES * SPAN)))

    def step(p, j):
        here = pl.multiple_of(j * CHUNK, CHUNK)
        harmonics_chunk(pos, p * size + here, w0, w1, w2)
        for k in range(0, 8, SPAN):
            factor_chunk(
                feat, species, columns, odd, p * size + here + k * LANES, here + k * LANES, k,
                basis[p], terms, z_out, w0, w1, w2,
            )

    for p in range(PARTS):
        for copy in waits[p]:
            copy.wait()
        lax.fori_loop(0, size // CHUNK, lambda j, carry: step(p, j), None, unroll=4)
    total = None
    for p, full in enumerate(basis):
        piece = lax.dot_general(
            full[...], terms[:, p * size : (p + 1) * size],
            (((1,), (1,)), ((), ())), preferred_element_type=f32,
        )
        total = piece if total is None else total + piece
    acc[...] = total
    keep.wait()


def histogram(value):
    m0, m1, m2 = value[0:1, :], value[1:2, :], value[2:3, :]
    sign = jnp.where(17 * m0 + m1 < 0, -1, 1)
    m0, m1, m2 = m0 * sign, m1 * sign, m2 * sign
    inner = jnp.where(
        m1 > 0, 16 * m0 + m1 - 17, jnp.where(m1 < 0, 16 * m0 - m1 - 9, 127 + m0)
    )
    row = jnp.where(m0 > 0, inner, jnp.where(m1 > 0, 143 + m1, 160))
    column = jnp.where(row == 160, jnp.abs(m2), m2) + MAXM
    size = row.shape[1]
    row_hot = (iota((256, size), 0) == row).astype(f32).astype(bf16)
    column_hot = (iota((32, size), 0) == column).astype(f32).astype(bf16)
    return lax.dot_general(
        column_hot, row_hot, (((1,), (1,)), ((), ())), preferred_element_type=f32
    )


def pack_kernel(chained, acc, own, *refs):
    if chained:
        (first,), (out, pair_out) = refs[:1], refs[1:]
        pair_out[0:3, :] = own[...]
        pair_out[3:6, :] = first[...]
        counts = histogram(first[...])
    else:
        millers, out = refs[:-1], refs[-1]
        at_start = lax.axis_index("atom") == 0
        counts = jnp.zeros((32, 256), f32)
        for j, ref in enumerate(millers[::-1]):
            value = jnp.where(at_start, own[...], ref[...]) if j == 0 else ref[...]
            counts = counts + histogram(value)
    out[0:ROWS, :] = acc[:, 0:LANES].astype(bf16)
    tail = jnp.concatenate([acc[:, 128:144], jnp.zeros((ROWS, 112), f32)], 1)
    tail = jnp.concatenate([tail, jnp.zeros((384 - ROWS, LANES), f32)], 0)
    flat = tail.T
    zero = jnp.zeros((GROUP, LANES), f32)
    pieces = [flat[0:8, 0:128], flat[0:8, 128:256], flat[0:8, 256:384], zero]
    out[304:336, :] = jnp.concatenate(pieces, 0).astype(bf16)
    out[336:368, :] = counts[:, 0:128].astype(bf16)
    out[368:400, :] = counts[:, 128:256].astype(bf16)


def fold_kernel(left, right, pair, own_counts, out):
    out[0:336, :] = (left[0:336, :].astype(f32) + right[0:336, :].astype(f32)).astype(bf16)
    atom = lax.axis_index("atom")
    last = jnp.where(atom // 2 == atom % 2, 1.0, 0.0)
    extra = histogram(pair[0:3, :]) + last * histogram(pair[3:6, :])
    counts = left[336:400, :].astype(f32) + right[336:400, :].astype(f32)
    counts = counts + jnp.where(atom % 2 == 0, 1.0, 0.0) * own_counts[...]
    out[336:400, :] = (counts + jnp.concatenate([extra[:, 0:128], extra[:, 128:256]], 0)).astype(bf16)


def radial_sum(square, weight_of):
    magnitude = jnp.sqrt(square)
    total = None
    for b in range(NRBF):
        offset = (magnitude - b * (k_cutoff / (NRBF - 1))) * (NRBF / k_cutoff)
        term = weight_of(b) * jnp.exp(-(offset * offset))
        total = term if total is None else total + term
    return total


def tables_kernel(ka_split, scaling, weights, own, token, radial_out, flat_out, counts_out):
    del token
    counts = histogram(own[...])
    counts_out[...] = jnp.concatenate([counts[:, 0:128], counts[:, 128:256]], 0)
    group = lax.axis_index("ka") // ka_split
    across = exact_dot(weights[...], choose(group, LANES), 1, 1)
    lane = iota((88, LANES), 1)
    row = iota((88, LANES), 0)
    third = (lane % 64) // 8 + 1
    first = row // 8 + 1
    second = row % 8 + 1
    planar = jnp.where(
        row < 64,
        first * first + second * second,
        jnp.where(row < 80, second * second, 0),
    )
    radial = radial_sum((planar + third * third).astype(f32), lambda b: across[b : b + 1, :]) * scaling
    radial = jnp.concatenate([radial[0:64], radial], 0)

    radial_out[...] = radial

    lane = iota((8, LANES), 1)
    cell = (lane // 16 + 1) * (lane // 16 + 1) + (lane % 8 + 1) * (lane % 8 + 1)
    edge = jnp.where(lane < 32, (lane % 8 + 1) * (lane % 8 + 1), 0)
    own = exact_dot(choose(group, GROUP), weights[...], 1, 1)
    flat_out[...] = radial_sum(
        jnp.concatenate([cell, edge], 1).astype(f32), lambda b: own[:, b : b + 1]
    ) * scaling


def filter_rows(payload, radial, flat, gt_scr):
    total = payload[0][...].astype(f32)
    for part in payload[1:]:
        total = total + part[...].astype(f32)
    counts = jnp.concatenate([total[336:368], total[368:400]], 1)
    lane = iota((32, LANES), 1)
    index = iota((32, LANES), 0) - MAXM
    height = (lane % 64) // 8 + 1
    plus = jnp.where(jnp.abs(index) == height, 1.0, 0.0)
    minus = jnp.where(index == height, 1.0, jnp.where(index == -height, -1.0, 0.0))
    minus = jnp.where(lane < 64, -minus, minus)
    spread = jnp.concatenate([plus, minus], 1).astype(f32)
    high = jnp.floor(counts * (1.0 / 64.0))
    split = jnp.concatenate([high, counts - 64.0 * high], 0).astype(bf16)
    scale = jnp.concatenate([64.0 * spread, spread], 0).astype(bf16)
    wide = lax.dot_general(split, scale, (((0,), (0,)), ((), ())), preferred_element_type=f32)
    def by_rows(value):
        both = value[0:128].reshape(8, 2, 8, LANES)
        edges = [value[128:136], value[144:152], value[160:168]]
        return jnp.concatenate([both[:, 0].reshape(64, LANES), both[:, 1].reshape(64, LANES)] + edges, 0)

    w_sum = by_rows(wide[:, 0:128]) * radial[...]
    w_dif = by_rows(wide[:, 128:256]) * radial[...]
    upper = total[0:128].reshape(8, 2, 8, LANES)
    lower = total[128:256].reshape(8, 2, 8, LANES)
    cc, cs = upper[:, 0].reshape(64, LANES), upper[:, 1].reshape(64, LANES)
    sc, ss = lower[:, 0].reshape(64, LANES), lower[:, 1].reshape(64, LANES)
    zero = jnp.zeros((8, LANES), f32)
    v_cos = jnp.concatenate([cc - ss, cc + ss, total[256:264], total[272:280], total[288:296]], 0)
    v_sin = jnp.concatenate([sc + cs, sc - cs, total[264:272], total[280:288], zero], 0)
    g_cos = w_sum * v_cos + w_dif * pltpu.roll(v_sin, 64, 1)
    g_sin = w_sum * v_sin - w_dif * pltpu.roll(v_cos, 64, 1)
    cp, cm, sp, sm = g_cos[0:64], g_cos[64:128], g_sin[0:64], g_sin[64:128]

    def pair_up(left, right):
        both = [left.reshape(8, 1, 8, LANES), right.reshape(8, 1, 8, LANES)]
        return jnp.concatenate(both, 1).reshape(128, LANES)

    rows = [pair_up(cp + cm, sp - sm), pair_up(sp + sm, cm - cp), g_cos[128:136], g_sin[128:136]]
    rows += [g_cos[136:144], g_sin[136:144], g_cos[144:152], jnp.zeros((88, LANES), f32)]
    full = jnp.concatenate(rows, 0)
    gt_scr[0:128, :] = full.T.astype(bf16)

    lane = iota((8, LANES), 1)
    count0 = jnp.broadcast_to(counts[8:9, 0:128], (8, LANES))
    count1 = jnp.broadcast_to(counts[8:9, 128:256], (8, LANES))
    left = (lane // 8) % 2 == 0
    sigma = jnp.where(left, 1.0, -1.0).astype(f32)

    def swap(value):
        return jnp.where(left, pltpu.roll(value, LANES - 8, 1), pltpu.roll(value, 8, 1))

    other = swap(count0)
    x, y, rest = total[304:312], swap(total[312:320]), total[320:328]
    plus = (x - sigma * y) * flat[:, 0:128] * jnp.where(left, count0, other)
    less = (y + sigma * x) * flat[:, 0:128] * jnp.where(left, other, count0)
    rest = rest * flat[:, 128:256] * (count1 + pltpu.roll(count1, 8, 1))
    low = jnp.concatenate([plus + sigma * less, swap(less - sigma * plus), rest], 1)
    gt_scr[128:144, :] = jnp.concatenate([low, jnp.zeros_like(low)], 0).astype(bf16)


def back_kernel(sub, radial, flat, z, *refs):
    basis, payload, out, gt_scr = refs[:PARTS], refs[PARTS:-2], refs[-2], refs[-1]
    width = out.shape[2]
    filter_rows(payload, radial, flat, gt_scr)
    for j, piece in enumerate(basis):
        size = piece.shape[1]
        product = jnp.dot(gt_scr[:, 0:ROWS], piece[...], preferred_element_type=f32)
        for start in range(0, size, sub):
            place = j * size + start
            message = product[128:136, start : start + sub]
            for m in range(16):
                part = product[8 * m : 8 * m + 8, start : start + sub]
                message = message + z[m : m + 1, place : place + sub] * part
            offset = place % width
            out[place // width, :, offset : offset + sub] = message.astype(bf16)


def update_kernel(sub, message, feat, gain, up, down, out):
    width = feat.shape[1]
    eye = iota((64, 64), 0) == iota((64, 64), 1)
    column = jnp.sum(jnp.where(eye, jnp.broadcast_to(gain[...], (64, 64)), 0.0), axis=1, keepdims=True)
    for start in range(0, width, sub):
        part = pl.ds(start, sub)
        value = message[:, :, part].astype(f32).reshape(64, sub)
        mean_sq = jnp.mean(value * value, axis=0, keepdims=True)
        normed = (value * lax.rsqrt(mean_sq + 1e-06) * column).astype(bf16)
        pre = lax.dot_general(up[...], normed, (((0,), (0,)), ((), ())), preferred_element_type=f32)
        half = 0.5 * pre
        hidden = (half + half * jnp.tanh(half)).astype(bf16)
        update = jnp.dot(down[...], hidden, preferred_element_type=f32)
        out[:, part] = (feat[:, part].astype(f32) + update).astype(bf16)


def body(
    positions,
    features,
    species,
    miller,
    species_table,
    filter_weight,
    norm_gain,
    up_weight,
    down_weight,
):
    atoms_here = features.shape[1]
    channels = features.shape[0]
    n_atom = lax.axis_size("atom")
    n_ka = lax.axis_size("ka")
    ka_split = n_ka // (channels // GROUP)
    local_count = atoms_here // n_ka
    scaling = 1.0 / math.sqrt(atoms_here * n_atom * K)
    params = pltpu.CompilerParams(vmem_limit_bytes=24 * 1024 * 1024)

    def exchange(value, flips):
        pairs = []
        for a in range(n_atom):
            for b in range(n_ka):
                if flips[a]:
                    pairs.append((a * n_ka + (b ^ flips[a]), a * n_ka + b))
        return lax.ppermute(value, ("atom", "ka"), pairs)

    chained = (n_atom, n_ka) == (4, 8)
    if chained:
        millers = [exchange(miller, FAR)]
    else:
        blocks = n_ka // n_atom
        near = blocks // 2
        flips = [
            [near * a + j for j in range(near)] + [n_ka - 1 - near * a - j for j in range(blocks - near)]
            for a in range(n_atom)
        ]
        millers = [exchange(miller, [row[j] for row in flips]) for j in range(blocks)]

    whole = pl.BlockSpec(memory_space=pltpu.VMEM)
    hbm = pl.BlockSpec(memory_space=pltpu.HBM)
    hbm = pl.BlockSpec(memory_space=pltpu.HBM)
    z, acc, local_features, *basis = pl.pallas_call(
        functools.partial(factor_kernel, ka_split),
        in_specs=[hbm] * 4,
        out_specs=[whole] * (3 + PARTS),
        out_shape=[
            jax.ShapeDtypeStruct((16, atoms_here), f32),
            jax.ShapeDtypeStruct((ROWS, 144), f32),
            jax.ShapeDtypeStruct((channels, local_count), bf16),
        ]
        + [jax.ShapeDtypeStruct((ROWS, atoms_here // PARTS), bf16)] * PARTS,
        scratch_shapes=[
            pltpu.VMEM((3, atoms_here), f32),
            pltpu.VMEM((16, atoms_here), bf16),
            pltpu.VMEM((1, atoms_here), jnp.int32),
            pltpu.VMEM((NSPEC, channels), f32),
            pltpu.VMEM((144, atoms_here), bf16),
            pltpu.VMEM((LANES + 8, LANES), f32),
            pltpu.VMEM((LANES + 8, LANES), f32),
            pltpu.VMEM((LANES + 8, LANES), f32),
            pltpu.SemaphoreType.DMA((2 + 3 * PARTS,)),
        ],
        compiler_params=params,
        cost_estimate=pl.CostEstimate(flops=5 * 10**9, bytes_accessed=14 * 10**6, transcendentals=0),
        name="factors",
    )(
        pltpu.with_memory_space_constraint(positions, pltpu.HBM),
        pltpu.with_memory_space_constraint(features, pltpu.HBM),
        pltpu.with_memory_space_constraint(species.reshape(1, atoms_here), pltpu.HBM),
        pltpu.with_memory_space_constraint(species_table.T, pltpu.HBM),
    )

    packed = [jax.ShapeDtypeStruct((PAYLOAD, LANES), bf16)]
    if chained:
        packed.append(jax.ShapeDtypeStruct((6, miller.shape[1]), jnp.int32))
    payload, *pair = pl.pallas_call(
        functools.partial(pack_kernel, chained),
        in_specs=[whole] * (2 + len(millers)),
        out_specs=[whole] * len(packed),
        out_shape=packed,
        compiler_params=params,
        name="pack",
    )(acc, miller, *millers[::-1])
    radial, flat, own_counts = pl.pallas_call(
        functools.partial(tables_kernel, ka_split, scaling),
        in_specs=[whole, whole, pl.BlockSpec(memory_space=pl.ANY)],
        out_specs=[whole] * 3,
        out_shape=[
            jax.ShapeDtypeStruct((152, LANES), f32),
            jax.ShapeDtypeStruct((GROUP, 2 * LANES), f32),
            jax.ShapeDtypeStruct((64, LANES), f32),
        ],
        compiler_params=params,
        cost_estimate=pl.CostEstimate(flops=10**9, bytes_accessed=10**6, transcendentals=10**6),
        name="tables",
    )(filter_weight.T, miller, payload)
    if chained:
        across = lax.ppermute(payload, "atom", [(a, a ^ 2) for a in range(4)])
        payload = pl.pallas_call(
            fold_kernel,
            in_specs=[whole] * 4,
            out_specs=whole,
            out_shape=jax.ShapeDtypeStruct((PAYLOAD, LANES), bf16),
            compiler_params=params,
            name="fold",
        )(payload, across, exchange(pair[0], NEAR), own_counts)
        gathered = [payload, lax.ppermute(payload, "atom", [(a, a ^ 1) for a in range(4)])]
    else:
        gathered = list(lax.all_gather(payload, "atom"))

    message = pl.pallas_call(
        functools.partial(back_kernel, min(512, local_count)),
        in_specs=[whole] * (3 + PARTS + len(gathered)),
        out_specs=whole,
        out_shape=jax.ShapeDtypeStruct((n_ka, GROUP, local_count), bf16),
        scratch_shapes=[pltpu.VMEM((144, 384), bf16)],
        compiler_params=params,
        cost_estimate=pl.CostEstimate(flops=5 * 10**9, bytes_accessed=11 * 10**6, transcendentals=0),
        name="back",
    )(radial, flat, z, *basis, *gathered)

    groups = None
    if ka_split > 1:
        message = message.reshape(n_ka // ka_split, ka_split, GROUP, local_count)
        message = lax.dynamic_index_in_dim(message, lax.axis_index("ka") % ka_split, 1, False)
        groups = [[g * ka_split + s for g in range(n_ka // ka_split)] for s in range(ka_split)]
    message = lax.all_to_all(message, "ka", 0, 0, axis_index_groups=groups, tiled=True)

    return pl.pallas_call(
        functools.partial(update_kernel, local_count),
        in_specs=[whole] * 5,
        out_specs=whole,
        out_shape=jax.ShapeDtypeStruct((channels, local_count), bf16),
        compiler_params=params,
        name="update",
    )(message, local_features, norm_gain.reshape(1, channels), up_weight.T, down_weight)


def solution(mesh):
    in_specs = (P(None, "atom"), P(None, "atom"), P("atom"), P(None, "ka"), P(), P(), P(), P(), P())
    out_specs = P(None, ("atom", "ka"))
    return jax.shard_map(body, mesh=mesh, in_specs=in_specs, out_specs=out_specs, check_vma=False)
```

```python
import functools
import math

import jax
import jax.numpy as jnp
import numpy as np
from jax import lax
from jax.experimental import pallas as pl
from jax.experimental.pallas import tpu as pltpu
from jax.sharding import PartitionSpec as P

K = 4096
NRBF = 16
NSPEC = 8
MAXM = 8
GROUP = 8
ROWS = 304
CHUNK = 1024
SPAN = 4
PARTS = 4
LANES = 128
PAYLOAD = 400
k_cutoff = 14.0
FAR = (6, 3, 4, 5)
NEAR = (1, 2, 1, 2)
f32 = jnp.float32
bf16 = jnp.bfloat16


def fit(function, terms, odd):
    nodes = np.cos((np.arange(64) + 0.5) * np.pi / 64) * 0.5
    nodes = np.abs(nodes)
    target = function(2.0 * np.pi * nodes)
    if odd:
        target = target / nodes
    series = np.polynomial.chebyshev.Chebyshev.fit(nodes * nodes, target, terms - 1, domain=[0, 0.25])
    return [float(v) for v in series.convert(kind=np.polynomial.Polynomial).coef]


SIN = fit(np.sin, 6, True)
COS = fit(np.cos, 7, False)


def horner(coefs, x):
    total = coefs[-1] * x + coefs[-2]
    for value in coefs[-3::-1]:
        total = total * x + value
    return total


def first_harmonic(x):
    turns = x - jnp.floor(x + 0.5)
    square = turns * turns
    return horner(COS, square), turns * horner(SIN, square)


def iota(shape, axis):
    return lax.broadcasted_iota(jnp.int32, shape, axis)


def waves_to(scr, x):
    cosine, sine = first_harmonic(x)
    twice = cosine + cosine
    lower_c, lower_s = jnp.ones_like(cosine), jnp.zeros_like(sine)
    upper_c, upper_s = cosine, sine
    for m in range(MAXM):
        scr[8 * m : 8 * m + 8, :] = upper_c
        scr[64 + 8 * m : 72 + 8 * m, :] = upper_s
        lower_c, upper_c = upper_c, twice * upper_c - lower_c
        lower_s, upper_s = upper_s, twice * upper_s - lower_s


def spread(scr, row):
    pieces = [scr[pl.ds(row + k, 8, stride=0), :] for k in range(SPAN)]
    return jnp.concatenate(pieces, 1)


def comb(scr, row):
    return jnp.concatenate([scr[pl.ds(row + k, 8, stride=8), :] for k in range(SPAN)], 1)


def harmonics_chunk(pos, start, w0, w1, w2):
    for axis, scr in enumerate((w0, w1, w2)):
        rows = [pos[axis : axis + 1, pl.ds(start + LANES * k, LANES)] for k in range(8)]
        waves_to(scr, jnp.concatenate(rows, 0))


def factor_chunk(feat, species, table, odd, start, here, k, full, terms, z_out, w0, w1, w2):
    part = pl.ds(start, LANES * SPAN)
    local = pl.ds(here, LANES * SPAN)
    c1 = comb(w1, k)
    s1 = comb(w1, 64 + k)
    for m in range(16):
        left = spread(w0, 8 * m + k)
        full[16 * m : 16 * m + 16, local] = jnp.concatenate([left * c1, left * s1], 0).astype(bf16)
    full[256:272, local] = jnp.concatenate([comb(w0, k), comb(w0, 64 + k)], 0).astype(bf16)
    full[272:288, local] = jnp.concatenate([c1, s1], 0).astype(bf16)
    z_out[0:8, part] = comb(w2, k)
    z_out[8:16, part] = comb(w2, 64 + k)
    kinds = jnp.broadcast_to(species[0:1, part], (8, LANES * SPAN))
    embedded = table[0]
    for s in range(1, NSPEC):
        embedded = jnp.where(kinds == s, table[s], embedded)
    wide = feat[:, part].astype(f32)
    own = jnp.where(odd, wide[8:16], wide[0:8])
    source = (own + embedded).astype(bf16).astype(f32)
    for m in range(0, 16, 2):
        pair = [source * spread(w2, 8 * m + k), source * spread(w2, 8 * m + 8 + k)]
        terms[8 * m : 8 * m + 16, part] = jnp.concatenate(pair, 0).astype(bf16)
    terms[128:144, part] = jnp.concatenate([source, jnp.zeros_like(source)], 0).astype(bf16)


def choose(group, count):
    return (iota((count, 64), 1) == group * GROUP + iota((count, 64), 0) % GROUP).astype(f32)


def exact_dot(left, right, left_dim, right_dim):
    return lax.dot_general(
        left, right, (((left_dim,), (right_dim,)), ((), ())),
        precision=lax.Precision.HIGHEST, preferred_element_type=f32,
    )


def factor_kernel(ka_split, pos_hbm, feat_hbm, species_hbm, table_hbm, z_out, acc, local_out, *refs):
    basis = refs[:PARTS]
    pos, feat, species, table, terms, w0, w1, w2, sems = refs[PARTS:]
    me = lax.axis_index("ka")
    group = me // ka_split
    atoms, width = feat.shape[1], local_out.shape[1]
    first = pl.multiple_of((group // 2) * 16, 16)
    size = atoms // PARTS
    copies = [pltpu.make_async_copy(table_hbm, table, sems.at[0])]
    waits = []
    for p in range(PARTS):
        cut = pl.ds(p * size, size)
        waits.append(
            [
                pltpu.make_async_copy(pos_hbm.at[:, cut], pos.at[:, cut], sems.at[3 * p + 2]),
                pltpu.make_async_copy(species_hbm.at[:, cut], species.at[:, cut], sems.at[3 * p + 3]),
                pltpu.make_async_copy(
                    feat_hbm.at[pl.ds(first, 16), cut], feat.at[:, cut], sems.at[3 * p + 4]
                ),
            ]
        )
        copies += waits[p]
    keep = pltpu.make_async_copy(
        feat_hbm.at[:, pl.ds(pl.multiple_of(me * width, width), width)], local_out, sems.at[1]
    )
    for copy in copies + [keep]:
        copy.start()
    for full in basis:
        full[288:304, :] = (iota((16, size), 0) == 0).astype(f32).astype(bf16)
    odd = (group % 2) == 1
    copies[0].wait()
    mask = iota((8, 64), 1) == group * GROUP + iota((8, 64), 0)
    columns = []
    for s in range(NSPEC):
        own = jnp.sum(jnp.where(mask, table[s : s + 1, :], 0.0), axis=1, keepdims=True)
        columns.append(jnp.broadcast_to(own, (8, LANES * SPAN)))

    def step(p, j):
        here = pl.multiple_of(j * CHUNK, CHUNK)
        harmonics_chunk(pos, p * size + here, w0, w1, w2)
        for k in range(0, 8, SPAN):
            factor_chunk(
                feat, species, columns, odd, p * size + here + k * LANES, here + k * LANES, k,
                basis[p], terms, z_out, w0, w1, w2,
            )

    for p in range(PARTS):
        for copy in waits[p]:
            copy.wait()
        lax.fori_loop(0, size // CHUNK, lambda j, carry: step(p, j), None, unroll=4)
    total = None
    for p, full in enumerate(basis):
        piece = lax.dot_general(
            full[...], terms[:, p * size : (p + 1) * size],
            (((1,), (1,)), ((), ())), preferred_element_type=f32,
        )
        total = piece if total is None else total + piece
    acc[...] = total
    keep.wait()


def histogram(value):
    m0, m1, m2 = value[0:1, :], value[1:2, :], value[2:3, :]
    sign = jnp.where(17 * m0 + m1 < 0, -1, 1)
    m0, m1, m2 = m0 * sign, m1 * sign, m2 * sign
    inner = jnp.where(
        m1 > 0, 16 * m0 + m1 - 17, jnp.where(m1 < 0, 16 * m0 - m1 - 9, 127 + m0)
    )
    row = jnp.where(m0 > 0, inner, jnp.where(m1 > 0, 143 + m1, 160))
    column = jnp.where(row == 160, jnp.abs(m2), m2) + MAXM
    size = row.shape[1]
    row_hot = (iota((256, size), 0) == row).astype(f32).astype(bf16)
    column_hot = (iota((32, size), 0) == column).astype(f32).astype(bf16)
    return lax.dot_general(
        column_hot, row_hot, (((1,), (1,)), ((), ())), preferred_element_type=f32
    )


def pack_kernel(chained, acc, own, *refs):
    if chained:
        (first,), (out, pair_out) = refs[:1], refs[1:]
        pair_out[0:3, :] = own[...]
        pair_out[3:6, :] = first[...]
        counts = histogram(first[...])
    else:
        millers, out = refs[:-1], refs[-1]
        at_start = lax.axis_index("atom") == 0
        counts = jnp.zeros((32, 256), f32)
        for j, ref in enumerate(millers[::-1]):
            value = jnp.where(at_start, own[...], ref[...]) if j == 0 else ref[...]
            counts = counts + histogram(value)
    out[0:ROWS, :] = acc[:, 0:LANES].astype(bf16)
    tail = jnp.concatenate([acc[:, 128:144], jnp.zeros((ROWS, 112), f32)], 1)
    tail = jnp.concatenate([tail, jnp.zeros((384 - ROWS, LANES), f32)], 0)
    flat = tail.T
    zero = jnp.zeros((GROUP, LANES), f32)
    pieces = [flat[0:8, 0:128], flat[0:8, 128:256], flat[0:8, 256:384], zero]
    out[304:336, :] = jnp.concatenate(pieces, 0).astype(bf16)
    out[336:368, :] = counts[:, 0:128].astype(bf16)
    out[368:400, :] = counts[:, 128:256].astype(bf16)


def fold_kernel(left, right, pair, own_counts, out):
    out[0:336, :] = (left[0:336, :].astype(f32) + right[0:336, :].astype(f32)).astype(bf16)
    atom = lax.axis_index("atom")
    last = jnp.where(atom // 2 == atom % 2, 1.0, 0.0)
    extra = histogram(pair[0:3, :]) + last * histogram(pair[3:6, :])
    counts = left[336:400, :].astype(f32) + right[336:400, :].astype(f32)
    counts = counts + jnp.where(atom % 2 == 0, 1.0, 0.0) * own_counts[...]
    out[336:400, :] = (counts + jnp.concatenate([extra[:, 0:128], extra[:, 128:256]], 0)).astype(bf16)


def radial_sum(square, weight_of):
    magnitude = jnp.sqrt(square)
    total = None
    for b in range(NRBF):
        offset = (magnitude - b * (k_cutoff / (NRBF - 1))) * (NRBF / k_cutoff)
        term = weight_of(b) * jnp.exp(-(offset * offset))
        total = term if total is None else total + term
    return total


def tables_kernel(ka_split, scaling, weights, own, token, radial_out, flat_out, counts_out):
    del token
    counts = histogram(own[...])
    counts_out[...] = jnp.concatenate([counts[:, 0:128], counts[:, 128:256]], 0)
    group = lax.axis_index("ka") // ka_split
    across = exact_dot(weights[...], choose(group, LANES), 1, 1)
    lane = iota((88, LANES), 1)
    row = iota((88, LANES), 0)
    third = (lane % 64) // 8 + 1
    first = row // 8 + 1
    second = row % 8 + 1
    planar = jnp.where(
        row < 64,
        first * first + second * second,
        jnp.where(row < 80, second * second, 0),
    )
    radial = radial_sum((planar + third * third).astype(f32), lambda b: across[b : b + 1, :]) * scaling
    radial = jnp.concatenate([radial[0:64], radial], 0)

    radial_out[...] = radial

    lane = iota((8, LANES), 1)
    cell = (lane // 16 + 1) * (lane // 16 + 1) + (lane % 8 + 1) * (lane % 8 + 1)
    edge = jnp.where(lane < 32, (lane % 8 + 1) * (lane % 8 + 1), 0)
    own = exact_dot(choose(group, GROUP), weights[...], 1, 1)
    flat_out[...] = radial_sum(
        jnp.concatenate([cell, edge], 1).astype(f32), lambda b: own[:, b : b + 1]
    ) * scaling


def filter_rows(payload, radial, flat, gt_scr):
    total = payload[0][...].astype(f32)
    for part in payload[1:]:
        total = total + part[...].astype(f32)
    counts = jnp.concatenate([total[336:368], total[368:400]], 1)
    lane = iota((32, LANES), 1)
    index = iota((32, LANES), 0) - MAXM
    height = (lane % 64) // 8 + 1
    plus = jnp.where(jnp.abs(index) == height, 1.0, 0.0)
    minus = jnp.where(index == height, 1.0, jnp.where(index == -height, -1.0, 0.0))
    minus = jnp.where(lane < 64, -minus, minus)
    spread = jnp.concatenate([plus, minus], 1).astype(f32)
    high = jnp.floor(counts * (1.0 / 64.0))
    split = jnp.concatenate([high, counts - 64.0 * high], 0).astype(bf16)
    scale = jnp.concatenate([64.0 * spread, spread], 0).astype(bf16)
    wide = lax.dot_general(split, scale, (((0,), (0,)), ((), ())), preferred_element_type=f32)
    def by_rows(value):
        both = value[0:128].reshape(8, 2, 8, LANES)
        edges = [value[128:136], value[144:152], value[160:168]]
        return jnp.concatenate([both[:, 0].reshape(64, LANES), both[:, 1].reshape(64, LANES)] + edges, 0)

    w_sum = by_rows(wide[:, 0:128]) * radial[...]
    w_dif = by_rows(wide[:, 128:256]) * radial[...]
    upper = total[0:128].reshape(8, 2, 8, LANES)
    lower = total[128:256].reshape(8, 2, 8, LANES)
    cc, cs = upper[:, 0].reshape(64, LANES), upper[:, 1].reshape(64, LANES)
    sc, ss = lower[:, 0].reshape(64, LANES), lower[:, 1].reshape(64, LANES)
    zero = jnp.zeros((8, LANES), f32)
    v_cos = jnp.concatenate([cc - ss, cc + ss, total[256:264], total[272:280], total[288:296]], 0)
    v_sin = jnp.concatenate([sc + cs, sc - cs, total[264:272], total[280:288], zero], 0)
    g_cos = w_sum * v_cos + w_dif * pltpu.roll(v_sin, 64, 1)
    g_sin = w_sum * v_sin - w_dif * pltpu.roll(v_cos, 64, 1)
    cp, cm, sp, sm = g_cos[0:64], g_cos[64:128], g_sin[0:64], g_sin[64:128]

    def pair_up(left, right):
        both = [left.reshape(8, 1, 8, LANES), right.reshape(8, 1, 8, LANES)]
        return jnp.concatenate(both, 1).reshape(128, LANES)

    rows = [pair_up(cp + cm, sp - sm), pair_up(sp + sm, cm - cp), g_cos[128:136], g_sin[128:136]]
    rows += [g_cos[136:144], g_sin[136:144], g_cos[144:152], jnp.zeros((88, LANES), f32)]
    full = jnp.concatenate(rows, 0)
    gt_scr[0:128, :] = full.T.astype(bf16)

    lane = iota((8, LANES), 1)
    count0 = jnp.broadcast_to(counts[8:9, 0:128], (8, LANES))
    count1 = jnp.broadcast_to(counts[8:9, 128:256], (8, LANES))
    left = (lane // 8) % 2 == 0
    sigma = jnp.where(left, 1.0, -1.0).astype(f32)

    def swap(value):
        return jnp.where(left, pltpu.roll(value, LANES - 8, 1), pltpu.roll(value, 8, 1))

    other = swap(count0)
    x, y, rest = total[304:312], swap(total[312:320]), total[320:328]
    plus = (x - sigma * y) * flat[:, 0:128] * jnp.where(left, count0, other)
    less = (y + sigma * x) * flat[:, 0:128] * jnp.where(left, other, count0)
    rest = rest * flat[:, 128:256] * (count1 + pltpu.roll(count1, 8, 1))
    low = jnp.concatenate([plus + sigma * less, swap(less - sigma * plus), rest], 1)
    gt_scr[128:144, :] = jnp.concatenate([low, jnp.zeros_like(low)], 0).astype(bf16)


def back_kernel(sub, radial, flat, z, *refs):
    basis, payload, out, gt_scr = refs[:PARTS], refs[PARTS:-2], refs[-2], refs[-1]
    width = out.shape[2]
    filter_rows(payload, radial, flat, gt_scr)
    for j, piece in enumerate(basis):
        size = piece.shape[1]
        product = jnp.dot(gt_scr[:, 0:ROWS], piece[...], preferred_element_type=f32)
        for start in range(0, size, sub):
            place = j * size + start
            message = product[128:136, start : start + sub]
            for m in range(16):
                part = product[8 * m : 8 * m + 8, start : start + sub]
                message = message + z[m : m + 1, place : place + sub] * part
            offset = place % width
            out[place // width, :, offset : offset + sub] = message.astype(bf16)


def update_kernel(sub, message, feat, gain, up, down, out):
    width = feat.shape[1]
    eye = iota((64, 64), 0) == iota((64, 64), 1)
    column = jnp.sum(jnp.where(eye, jnp.broadcast_to(gain[...], (64, 64)), 0.0), axis=1, keepdims=True)
    for start in range(0, width, sub):
        part = pl.ds(start, sub)
        value = message[:, :, part].astype(f32).reshape(64, sub)
        mean_sq = jnp.mean(value * value, axis=0, keepdims=True)
        normed = (value * lax.rsqrt(mean_sq + 1e-06) * column).astype(bf16)
        pre = lax.dot_general(up[...], normed, (((0,), (0,)), ((), ())), preferred_element_type=f32)
        half = 0.5 * pre
        hidden = (half + half * jnp.tanh(half)).astype(bf16)
        update = jnp.dot(down[...], hidden, preferred_element_type=f32)
        out[:, part] = (feat[:, part].astype(f32) + update).astype(bf16)


def body(
    positions,
    features,
    species,
    miller,
    species_table,
    filter_weight,
    norm_gain,
    up_weight,
    down_weight,
):
    atoms_here = features.shape[1]
    channels = features.shape[0]
    n_atom = lax.axis_size("atom")
    n_ka = lax.axis_size("ka")
    ka_split = n_ka // (channels // GROUP)
    local_count = atoms_here // n_ka
    scaling = 1.0 / math.sqrt(atoms_here * n_atom * K)
    params = pltpu.CompilerParams(vmem_limit_bytes=24 * 1024 * 1024)

    def exchange(value, flips):
        pairs = []
        for a in range(n_atom):
            for b in range(n_ka):
                if flips[a]:
                    pairs.append((a * n_ka + (b ^ flips[a]), a * n_ka + b))
        return lax.ppermute(value, ("atom", "ka"), pairs)

    chained = (n_atom, n_ka) == (4, 8)
    if chained:
        millers = [exchange(miller, FAR)]
    else:
        blocks = n_ka // n_atom
        near = blocks // 2
        flips = [
            [near * a + j for j in range(near)] + [n_ka - 1 - near * a - j for j in range(blocks - near)]
            for a in range(n_atom)
        ]
        millers = [exchange(miller, [row[j] for row in flips]) for j in range(blocks)]

    whole = pl.BlockSpec(memory_space=pltpu.VMEM)
    hbm = pl.BlockSpec(memory_space=pltpu.HBM)
    hbm = pl.BlockSpec(memory_space=pltpu.HBM)
    z, acc, local_features, *basis = pl.pallas_call(
        functools.partial(factor_kernel, ka_split),
        in_specs=[hbm] * 4,
        out_specs=[whole] * (3 + PARTS),
        out_shape=[
            jax.ShapeDtypeStruct((16, atoms_here), f32),
            jax.ShapeDtypeStruct((ROWS, 144), f32),
            jax.ShapeDtypeStruct((channels, local_count), bf16),
        ]
        + [jax.ShapeDtypeStruct((ROWS, atoms_here // PARTS), bf16)] * PARTS,
        scratch_shapes=[
            pltpu.VMEM((3, atoms_here), f32),
            pltpu.VMEM((16, atoms_here), bf16),
            pltpu.VMEM((1, atoms_here), jnp.int32),
            pltpu.VMEM((NSPEC, channels), f32),
            pltpu.VMEM((144, atoms_here), bf16),
            pltpu.VMEM((LANES + 8, LANES), f32),
            pltpu.VMEM((LANES + 8, LANES), f32),
            pltpu.VMEM((LANES + 8, LANES), f32),
            pltpu.SemaphoreType.DMA((2 + 3 * PARTS,)),
        ],
        compiler_params=params,
        cost_estimate=pl.CostEstimate(flops=5 * 10**9, bytes_accessed=14 * 10**6, transcendentals=0),
        name="factors",
    )(
        pltpu.with_memory_space_constraint(positions, pltpu.HBM),
        pltpu.with_memory_space_constraint(features, pltpu.HBM),
        pltpu.with_memory_space_constraint(species.reshape(1, atoms_here), pltpu.HBM),
        pltpu.with_memory_space_constraint(species_table.T, pltpu.HBM),
    )

    packed = [jax.ShapeDtypeStruct((PAYLOAD, LANES), bf16)]
    if chained:
        packed.append(jax.ShapeDtypeStruct((6, miller.shape[1]), jnp.int32))
    payload, *pair = pl.pallas_call(
        functools.partial(pack_kernel, chained),
        in_specs=[whole] * (2 + len(millers)),
        out_specs=[whole] * len(packed),
        out_shape=packed,
        compiler_params=params,
        name="pack",
    )(acc, miller, *millers[::-1])
    radial, flat, own_counts = pl.pallas_call(
        functools.partial(tables_kernel, ka_split, scaling),
        in_specs=[whole, whole, pl.BlockSpec(memory_space=pl.ANY)],
        out_specs=[whole] * 3,
        out_shape=[
            jax.ShapeDtypeStruct((152, LANES), f32),
            jax.ShapeDtypeStruct((GROUP, 2 * LANES), f32),
            jax.ShapeDtypeStruct((64, LANES), f32),
        ],
        compiler_params=params,
        cost_estimate=pl.CostEstimate(flops=10**9, bytes_accessed=10**6, transcendentals=10**6),
        name="tables",
    )(filter_weight.T, miller, payload)
    if chained:
        across = lax.ppermute(payload, "atom", [(a, a ^ 2) for a in range(4)])
        payload = pl.pallas_call(
            fold_kernel,
            in_specs=[whole] * 4,
            out_specs=whole,
            out_shape=jax.ShapeDtypeStruct((PAYLOAD, LANES), bf16),
            compiler_params=params,
            name="fold",
        )(payload, across, exchange(pair[0], NEAR), own_counts)
        gathered = [payload, lax.ppermute(payload, "atom", [(a, a ^ 1) for a in range(4)])]
    else:
        gathered = list(lax.all_gather(payload, "atom"))

    message = pl.pallas_call(
        functools.partial(back_kernel, min(512, local_count)),
        in_specs=[whole] * (3 + PARTS + len(gathered)),
        out_specs=whole,
        out_shape=jax.ShapeDtypeStruct((n_ka, GROUP, local_count), bf16),
        scratch_shapes=[pltpu.VMEM((144, 384), bf16)],
        compiler_params=params,
        cost_estimate=pl.CostEstimate(flops=5 * 10**9, bytes_accessed=11 * 10**6, transcendentals=0),
        name="back",
    )(radial, flat, z, *basis, *gathered)

    groups = None
    if ka_split > 1:
        message = message.reshape(n_ka // ka_split, ka_split, GROUP, local_count)
        message = lax.dynamic_index_in_dim(message, lax.axis_index("ka") % ka_split, 1, False)
        groups = [[g * ka_split + s for g in range(n_ka // ka_split)] for s in range(ka_split)]
    message = lax.all_to_all(message, "ka", 0, 0, axis_index_groups=groups, tiled=True)

    return pl.pallas_call(
        functools.partial(update_kernel, local_count),
        in_specs=[whole] * 5,
        out_specs=whole,
        out_shape=jax.ShapeDtypeStruct((channels, local_count), bf16),
        compiler_params=params,
        name="update",
    )(message, local_features, norm_gain.reshape(1, channels), up_weight.T, down_weight)


def solution(mesh):
    in_specs = (P(None, "atom"), P(None, "atom"), P("atom"), P(None, "ka"), P(), P(), P(), P(), P())
    out_specs = P(None, ("atom", "ka"))
    return jax.shard_map(body, mesh=mesh, in_specs=in_specs, out_specs=out_specs, check_vma=False)
```
